256 devices in a mesh: seq: 64 (over z, y, core), dp: 4 (over x).
Axes of the slice: x: 4, y: 4, z: 8, core: 2. Of those that a mesh axis runs over, the one named last changes fastest.
Arguments:
- patches: bfloat16 [4, 16384, 1280], P('dp', 'seq')
- lengths: int32 [4, 64, 4], P('dp', 'seq'), may hold values from 1 to 32, 64 in all within a row
- token_dest: int32 [4, 4096], P('dp', 'seq'), may hold values from 0 to 4095, as said below
- gain: float32 [1280], replicated, may hold values from 0.1 to 1.9
- w_qkv: bfloat16 [1280, 3840], replicated
- w_out: bfloat16 [1280, 1280], P('seq'), may hold values from -0.15625 to 0.15625
- cotangent: bfloat16 [4, 4096, 5120], P('dp', 'seq'), may hold values from -6 to 6
Outputs:
- merged: bfloat16 [4, 4096, 5120], P('dp', 'seq')
- grad_patches: bfloat16 [4, 16384, 1280], P('dp', 'seq')
- grad_out_weight: float32 [1280, 1280], P('seq')
- grad_gain: float32 [1280], P('seq')
The draws below stay inside these ranges and needn't reach their ends.
Inputs may be any that keep to these rules, and one draw needn't show every extreme that they name: The lengths of a shard add up to 64. `token_dest`: A token of shard s that goes to shard d lands at a position from d*64 + s*1 to d*64 + (s+1) - 1, and each of these positions receives exactly one token of shard s.
All inputs are finite; a program needn't handle non-finite values.
Results may differ from the reference program's by a relative error of at most 0.01.
Values may be sent and summed in bfloat16 or wider, within the bound.
A program may use at most 128 MiB of HBM per device.

```python
import math
import jax
import jax.numpy as jnp
import numpy as np
from jax import lax

D = 1280
HEADS = 16
GROUP = 4
IMGS = 4
ROWS = 256
M_TOK = 64
PEER_TOK = 1
MOST = 32
TOTAL_ROWS = 65536
N_SEQ = 64
N_DP = 4


def draw_patches(key, part):
    key = jax.random.fold_in(key, 11)
    key_base, key_rows, key_cols = jax.random.split(key, 3)
    shape = (N_DP, N_SEQ * ROWS, D)
    row_scale = jnp.exp(jax.random.uniform(key_rows, (N_DP, N_SEQ * ROWS, 1), minval=jnp.log(0.5), maxval=jnp.log(5.0)))
    col_scale = jnp.exp(jax.random.uniform(key_cols, (1, 1, D), minval=jnp.log(0.3), maxval=jnp.log(3.0)))
    base = jnp.clip(jax.random.normal(key_base, shape), -6.0, 6.0)
    scaled = base * row_scale * col_scale
    return scaled.astype(jnp.bfloat16)


def draw_w_qkv(key, part):
    key = jax.random.fold_in(key, 23)
    key_base = jax.random.fold_in(key, 0)
    shape = (D, 3, HEADS, D // HEADS)
    base = jnp.clip(jax.random.normal(key_base, shape), -6.0, 6.0) * D ** (-0.5)
    return base.reshape(D, 3 * D).astype(jnp.bfloat16)


def draw_token_dest(key, part):
    key = jax.random.fold_in(key, 37)
    shard_keys = jax.random.split(key, N_DP * N_SEQ)
    slot_ids = jax.vmap(lambda one_key: jax.random.permutation(one_key, M_TOK))(shard_keys).astype(jnp.int32)
    shard_ids = (jnp.arange(N_DP * N_SEQ, dtype=jnp.int32) % N_SEQ)[:, None]
    targets = slot_ids // PEER_TOK * M_TOK + shard_ids * PEER_TOK + slot_ids % PEER_TOK
    return targets.reshape(N_DP, N_SEQ * M_TOK).astype(jnp.int32)


def level_of(own_key, extent, pieces, smallest, high):
    def one(position, parts):
        heights = jax.random.uniform(jax.random.fold_in(jax.random.fold_in(own_key, 6), position), (parts,), jnp.float32, smallest / len(pieces), high / len(pieces))
        return jnp.repeat(jnp.exp(heights), extent[position] // parts).reshape((-1,) + (1,) * (len(extent) - position - 1))

    level = one(*pieces[0])
    for cut in pieces[1:]:
        level = level * one(*cut)
    return level


def length_profile(count, total, limit, slope):
    portions = [(1 << 20) // math.isqrt(rank ** slope) + 1 for rank in range(2, count + 1)]
    spare, given = total - limit - (count - 1), [1] * (count - 1)
    while spare > 0:
        free = [i for i in range(count - 1) if given[i] < limit]
        pool, remaining = sum([portions[i] for i in free]), spare
        for i in free:
            addition = min(limit - given[i], max(1, remaining * portions[i] // pool), spare)
            given[i] = given[i] + addition
            spare = spare - addition
    return np.array([limit] + given)


def ragged(key, number_of, total, reach, skew):
    if number_of == 2:
        one = jax.random.randint(key, (), max(1, total - reach), min(reach, total - 1) + 1)
        return jnp.stack([one, total - one])
    sizes = jnp.asarray(length_profile(number_of, total, reach, skew), jnp.int32)
    twos = (number_of - 1) // 2
    donor, receiver = sizes[1:1 + 2 * twos:2], sizes[2:2 + 2 * twos:2]
    margin = jnp.minimum(donor - 1, reach - receiver)
    shifted = jax.random.randint(jax.random.fold_in(key, 1), (twos,), 0, 1 << 20) % (margin + 1)
    sizes = sizes.at[1:1 + 2 * twos:2].set(donor - shifted).at[2:2 + 2 * twos:2].set(receiver + shifted)
    return sizes[jax.random.permutation(jax.random.fold_in(key, 2), number_of)]


def gaussian(stream_key, shape, deviation, bound, cuts=(), kind=jnp.bfloat16):
    values = jax.random.normal(stream_key, shape, jnp.float32) * deviation
    if len(cuts) > 0:
        values = level_of(stream_key, shape, cuts, -0.22, 0.18) * values
    return jnp.clip(values, min=-bound, max=bound).astype(kind)


def setup_inputs(seed: int = 0) -> dict:
    splits = jax.random.split(jax.random.key(seed), 8)
    return {
        "patches": draw_patches(jax.random.fold_in(splits[7], 71), 0),
        "lengths": jax.vmap(lambda own: ragged(own, IMGS, M_TOK, MOST, 2))(jax.random.split(splits[1], N_DP * N_SEQ)).reshape((N_DP, N_SEQ, IMGS)).astype(jnp.int32),
        "token_dest": draw_token_dest(jax.random.fold_in(splits[7], 71), 0),
        "gain": jnp.clip(1.0 + 0.18 * jax.random.normal(splits[3], (D,), jnp.float32), 0.1, 1.9),
        "w_qkv": draw_w_qkv(jax.random.fold_in(splits[7], 71), 0),
        "w_out": gaussian(splits[5], (D, D), D ** -0.5, 0.15625, ((0, 64),)),
        "cotangent": gaussian(splits[6], (N_DP, N_SEQ * M_TOK, GROUP * D), 1.0, 6.0, ((0, 4), (1, 64))),
    }


eps = 1e-06

def image_mask(shard_lengths, row_count):
    image_ends = jnp.cumsum(shard_lengths.astype(jnp.int32) * GROUP).astype(jnp.int32)
    row_index = jnp.arange(row_count, dtype=jnp.int32)
    image_ids = lax.optimization_barrier(jnp.sum((row_index[:, None] >= image_ends[None, :]).astype(jnp.int32), axis=1))
    return image_ids[:, None] == image_ids[None, :]

def forward(patch_rows, shard_lengths, gain, w_qkv, w_out):
    row_count, model_width = patch_rows.shape
    head_size = model_width // HEADS
    score_scale = 1.0 / math.sqrt(head_size)
    wide_rows = patch_rows.astype(jnp.float32)
    centred = wide_rows - lax.optimization_barrier(jnp.mean(wide_rows, axis=-1, keepdims=True))
    inv_spread = lax.rsqrt(lax.optimization_barrier(jnp.mean(centred * centred, axis=-1, keepdims=True)) + eps)
    standard = centred * inv_spread
    normed = (standard * gain).astype(jnp.bfloat16)
    projected = jnp.dot(normed, w_qkv, preferred_element_type=jnp.float32).astype(jnp.bfloat16)
    queries = projected[:, :model_width].reshape(row_count, HEADS, head_size)
    key_rows = projected[:, model_width:2 * model_width].reshape(row_count, HEADS, head_size)
    value_rows = projected[:, 2 * model_width:].reshape(row_count, HEADS, head_size)
    scores = jnp.einsum('qhe,khe->hqk', queries.astype(jnp.float32), key_rows.astype(jnp.float32)) * score_scale
    same_image = image_mask(shard_lengths, row_count)
    scores = jnp.where(same_image[None], scores, -jnp.inf)
    row_max = lax.optimization_barrier(jnp.max(scores, axis=-1, keepdims=True))
    weights_exp = jnp.exp(scores - row_max)
    probs = weights_exp / lax.optimization_barrier(jnp.sum(weights_exp, axis=-1, keepdims=True))
    probs_low = probs.astype(jnp.bfloat16)
    attended = jnp.einsum('hqk,khe->qhe', probs_low.astype(jnp.float32), value_rows.astype(jnp.float32))
    attended = attended.astype(jnp.bfloat16).reshape(row_count, model_width)
    branch = jnp.dot(attended, w_out, preferred_element_type=jnp.float32)
    block = (wide_rows + branch).astype(jnp.bfloat16)
    return (block, (standard, inv_spread, queries, key_rows, value_rows, probs, probs_low, attended))

def backward(saved, block_grad, gain, w_qkv, w_out):
    standard, inv_spread, queries, key_rows, value_rows, probs, probs_low, attended = saved
    row_count, model_width = block_grad.shape
    head_size = model_width // HEADS
    score_scale = 1.0 / math.sqrt(head_size)
    incoming = block_grad.astype(jnp.float32)
    weight_grad = lax.dot_general(attended, block_grad, (((0,), (0,)), ((), ())), preferred_element_type=jnp.float32)
    grad_attended = lax.dot_general(block_grad, w_out, (((1,), (1,)), ((), ())), preferred_element_type=jnp.float32)
    grad_attended = grad_attended.astype(jnp.bfloat16).reshape(row_count, HEADS, head_size)
    grad_probs = jnp.einsum('qhe,khe->hqk', grad_attended.astype(jnp.float32), value_rows.astype(jnp.float32))
    grad_values = jnp.einsum('hqk,qhe->khe', probs_low.astype(jnp.float32), grad_attended.astype(jnp.float32)).astype(jnp.bfloat16)
    grad_scores = probs * (grad_probs - lax.optimization_barrier(jnp.sum(grad_probs * probs, axis=-1, keepdims=True))) * score_scale
    grad_scores = grad_scores.astype(jnp.bfloat16)
    grad_queries = jnp.einsum('hqk,khe->qhe', grad_scores.astype(jnp.float32), key_rows.astype(jnp.float32)).astype(jnp.bfloat16)
    grad_keys = jnp.einsum('hqk,qhe->khe', grad_scores.astype(jnp.float32), queries.astype(jnp.float32)).astype(jnp.bfloat16)
    grad_projected = jnp.concatenate([grad_queries.reshape(row_count, model_width), grad_keys.reshape(row_count, model_width), grad_values.reshape(row_count, model_width)], axis=1)
    grad_normed = lax.dot_general(grad_projected, w_qkv, (((1,), (1,)), ((), ())), preferred_element_type=jnp.float32)
    gain_grad = lax.optimization_barrier(jnp.sum(grad_normed * standard, axis=0))
    grad_standard = grad_normed * gain
    grad_branch = inv_spread * (grad_standard - lax.optimization_barrier(jnp.mean(grad_standard, axis=-1, keepdims=True)) - standard * lax.optimization_barrier(jnp.mean(grad_standard * standard, axis=-1, keepdims=True)))
    patch_grad = (incoming + grad_branch).astype(jnp.bfloat16)
    return (patch_grad, weight_grad, gain_grad)

def reference(patches, lengths, token_dest, gain, w_qkv, w_out, cotangent):
    shard_count = N_DP * N_SEQ
    patch_blocks = patches.reshape(shard_count, ROWS, D)
    length_blocks = lengths.reshape(shard_count, IMGS)
    routed = jax.vmap(lambda grads, where: jnp.take(grads, where, axis=0))(cotangent, token_dest)
    grad_blocks = routed.reshape(shard_count, ROWS, D)

    def step(carry, inputs):
        weight_sum, gain_sum = carry
        patch_rows, shard_lengths, block_grad = inputs
        block, saved = forward(patch_rows, shard_lengths, gain, w_qkv, w_out)
        patch_grad, weight_grad, gain_grad = backward(saved, block_grad, gain, w_qkv, w_out)
        return ((weight_sum + weight_grad, gain_sum + gain_grad), (block, patch_grad))
    start = (jnp.zeros((D, D), jnp.float32), jnp.zeros((D,), jnp.float32))
    (weight_sum, gain_sum), (blocks, patch_grads) = lax.scan(step, start, (patch_blocks, length_blocks, grad_blocks))
    tokens = blocks.reshape(N_DP, N_SEQ * M_TOK, GROUP * D)
    merged = jax.vmap(lambda rows_in, where: jnp.zeros_like(rows_in).at[where].set(rows_in))(tokens, token_dest)
    grad_patches = patch_grads.reshape(N_DP, N_SEQ * ROWS, D)
    norm_scale = 1.0 / math.sqrt(TOTAL_ROWS)
    return (merged, grad_patches, weight_sum * norm_scale, gain_sum * norm_scale)
```

```python
import math

import jax
import jax.numpy as jnp
from jax import lax
from jax.experimental import pallas as pl
from jax.experimental.pallas import tpu as pltpu
from jax.sharding import PartitionSpec as P

HEADS = 16
GROUP = 4
D = 1280
HALF = 640
NZ, NY, NX = 8, 4, 4
SEQ = 64
LIMIT = 56 * 2**20

eps = 1e-06
F32 = jnp.float32
BF16 = jnp.bfloat16


def place():
    seq = lax.axis_index("seq")
    x = lax.axis_index("dp")
    return seq, x, lax.div(seq, 8), lax.rem(lax.div(seq, 2), 4), lax.rem(seq, 2)


def seq_of(z, y, core):
    return z * 8 + y * 2 + core


def dev(seq, x):
    return {"seq": seq, "dp": x}


def remote(src, dst, send, recv, seq, x):
    return pltpu.make_async_remote_copy(
        src_ref=src,
        dst_ref=dst,
        send_sem=send,
        recv_sem=recv,
        device_id=dev(seq, x),
        device_id_type=pl.DeviceIdType.MESH,
    )


def greet(with_xy):
    seq, x, z, y, core = place()
    barrier = pltpu.get_barrier_semaphore()

    @pl.loop(1, SEQ)
    def _(k):
        pl.semaphore_signal(
            barrier, inc=1, device_id=dev(lax.rem(seq + k, SEQ), x), device_id_type=pl.DeviceIdType.MESH
        )

    count = SEQ - 1
    if with_xy:
        for kx in range(1, NX):
            for ky in range(NY):
                pl.semaphore_signal(
                    barrier,
                    inc=1,
                    device_id=dev(seq_of(z, lax.rem(y + ky, NY), core), lax.rem(x + kx, NX)),
                    device_id_type=pl.DeviceIdType.MESH,
                )
                count += 1
    pl.semaphore_wait(barrier, count)


def exchange_start(src, dst, send, recv):
    seq, x, z, y, core = place()

    @pl.loop(1, SEQ)
    def _(k):
        to = lax.rem(seq + k, SEQ)
        remote(src.at[to], dst.at[seq], send, recv, to, x).start()

    pltpu.make_async_copy(src.at[seq], dst.at[seq], recv).start()


def exchange_wait(src, dst, send, recv):
    pltpu.make_async_copy(dst, dst, recv).wait()
    part = src.at[pl.ds(0, SEQ - 1)]
    pltpu.make_async_copy(part, part, send).wait()


def pick(rows, columns, first):
    r = lax.broadcasted_iota(jnp.int32, (rows, columns), 0)
    c = lax.broadcasted_iota(jnp.int32, (rows, columns), 1)
    return r, c


def gather_out_weight(w_ref, slots, wg, sems):
    seq, x, z, y, core = place()
    own = jnp.concatenate([w_ref[...].astype(F32), jnp.zeros((12, D), F32)], axis=0).astype(BF16)
    slots[core] = own
    pair = remote(slots.at[core], slots.at[core], sems.at[0], sems.at[1], seq_of(z, y, 1 - core), x)
    pair.start()
    pair.wait()
    r, c = pick(48, 64, 0)
    want = jnp.where(r < 20, r, r + 12)
    chosen = jnp.where((c == want) & (r < 40), 1.0, 0.0).astype(BF16)
    first = pl.multiple_of(core * HALF, 128)
    rows = jnp.concatenate([slots[0, :, pl.ds(first, HALF)], slots[1, :, pl.ds(first, HALF)]], axis=0)
    wg[core, z, y] = jnp.dot(chosen, rows, preferred_element_type=F32).astype(BF16)
    copies = []
    for k in range(1, NZ):
        copies.append(
            remote(
                wg.at[core, z, y], wg.at[core, z, y], sems.at[2 * k], sems.at[2 * k + 1],
                seq_of(lax.rem(z + k, NZ), y, core), x,
            )
        )
    for one in copies:
        one.start()
    for one in copies:
        one.wait()
    copies = []
    for k in range(1, NY):
        copies.append(
            remote(
                wg.at[core, :, y], wg.at[core, :, y], sems.at[14 + 2 * k], sems.at[15 + 2 * k],
                seq_of(z, lax.rem(y + k, NY), core), x,
            )
        )
    for one in copies:
        one.start()
    for one in copies:
        one.wait()
    last = remote(wg.at[core], wg.at[core], sems.at[22], sems.at[23], seq_of(z, y, 1 - core), x)
    last.start()
    last.wait()


def incoming_kernel(cot_ref, w_ref, got_ref, wg_ref, slots, send, recv, sems):
    greet(False)
    exchange_start(cot_ref, got_ref, send, recv)
    gather_out_weight(w_ref, slots, wg_ref, sems)
    exchange_wait(cot_ref, got_ref, send, recv)


def incoming(cot, w_out):
    vmem = pl.BlockSpec(memory_space=pltpu.VMEM)
    return pl.pallas_call(
        incoming_kernel,
        out_shape=(
            jax.ShapeDtypeStruct((SEQ, GROUP, D), BF16),
            jax.ShapeDtypeStruct((2, NZ, NY, 48, HALF), BF16),
        ),
        in_specs=[vmem, vmem],
        out_specs=(vmem, vmem),
        scratch_shapes=[
            pltpu.VMEM((2, 32, D), BF16),
            pltpu.SemaphoreType.DMA,
            pltpu.SemaphoreType.DMA,
            pltpu.SemaphoreType.DMA((24,)),
        ],
        compiler_params=pltpu.CompilerParams(
            collective_id=0, has_side_effects=True, vmem_limit_bytes=LIMIT
        ),
    )(cot, w_out)


def scatter_weight(at_ref, bg_ref, out, bufs, sems, norm_scale):
    at2, bg2, wsum, wb, xr, s1, wb2, yr, zs, zr, s3 = bufs
    seq, x, z, y, core = place()
    other = 1 - core
    partner = seq_of(z, y, other)
    mine = pl.multiple_of(core * HALF, 128)
    theirs = pl.multiple_of(other * HALF, 128)
    c0 = remote(at_ref, at2, sems.at[0], sems.at[1], partner, x)
    c1 = remote(bg_ref.at[:, pl.ds(theirs, HALF)], bg2, sems.at[2], sems.at[3], partner, x)
    c0.start()
    c1.start()
    c0.wait()
    c1.wait()

    @pl.loop(0, NX)
    def _(i):
        for j in range(NY):
            rows = pl.ds(pl.multiple_of((i * NY + j) * 80, 16), 80)
            part = jnp.dot(at_ref[rows, :], bg_ref[:, pl.ds(mine, HALF)], preferred_element_type=F32)
            part += jnp.dot(at2[rows, :], bg2[...], preferred_element_type=F32)
            wsum[i, j] = part
            wb[i, j] = part.astype(BF16)

    copies = []
    for k in range(1, NX):
        to = lax.rem(x + k, NX)
        copies.append(remote(wb.at[to], xr.at[k - 1], sems.at[2 + 2 * k], sems.at[3 + 2 * k], seq, to))
    for one in copies:
        one.start()
    for one in copies:
        one.wait()

    for j in range(NY):
        total = wsum[x, j]
        for k in range(3):
            total += xr[k, j].astype(F32)
        s1[j] = total
        wb2[j] = total.astype(BF16)
    copies = []
    for k in range(1, NY):
        to = lax.rem(y + k, NY)
        copies.append(
            remote(wb2.at[to], yr.at[k - 1], sems.at[8 + 2 * k], sems.at[9 + 2 * k], seq_of(z, to, core), x)
        )
    for one in copies:
        one.start()
    for one in copies:
        one.wait()
    total = s1[y]
    for k in range(3):
        total += yr[k].astype(F32)
    r, c = pick(128, 80, 0)
    low = lax.rem(r, 16)
    chosen = jnp.where((c == lax.div(r, 16) * 10 + low) & (low < 10), 1.0, 0.0).astype(BF16)
    zs[...] = jnp.dot(chosen, total.astype(BF16), preferred_element_type=F32).astype(BF16)
    copies = []
    for k in range(1, NZ):
        to = lax.rem(z + k, NZ)
        src = zs.at[pl.ds(pl.multiple_of(to * 16, 16), 16)]
        copies.append(remote(src, zr.at[k - 1], sems.at[14 + 2 * k], sems.at[15 + 2 * k], seq_of(to, y, core), x))
    for one in copies:
        one.start()
    for one in copies:
        one.wait()
    total = zs[pl.ds(pl.multiple_of(z * 16, 16), 16), :].astype(F32)
    for k in range(7):
        total += zr[k].astype(F32)
    s3[...] = total * norm_scale
    owner = 16 * x + 4 * y + lax.div(z, 2)
    slot = out.at[lax.rem(z, 2), core]

    @pl.when(owner != seq)
    def _():
        one = remote(s3, slot, sems.at[30], sems.at[31], owner, x)
        one.start()
        one.wait_send()

    @pl.when(owner == seq)
    def _():
        pltpu.make_async_copy(s3, slot, sems.at[31]).start()

    holds = x == lax.div(seq, 16)

    @pl.when(holds)
    def _():
        pltpu.make_async_copy(out, out, sems.at[31]).wait()
        copies = []
        for k in range(1, NX):
            copies.append(remote(out, out, sems.at[31 + k], sems.at[35], seq, lax.rem(x + k, NX)))
        for one in copies:
            one.start()
        for one in copies:
            one.wait_send()

    @pl.when(jnp.logical_not(holds))
    def _():
        pltpu.make_async_copy(out, out, sems.at[35]).wait()


def sum_gain(gain_ref, out_ref, g1, g2, ghold, sems, norm_scale):
    seq, x, z, y, core = place()
    copies = []
    for k in range(1, 16):
        kx, ky = k // 4, k % 4
        to = seq_of(z, lax.rem(y + ky, NY), core)
        copies.append(
            remote(gain_ref, g1.at[k - 1], sems.at[2 * k - 2], sems.at[2 * k - 1], to, lax.rem(x + kx, NX))
        )
    for one in copies:
        one.start()
    for one in copies:
        one.wait()
    total = gain_ref[...]
    for k in range(15):
        total += g1[k]
    ghold[...] = total
    copies = []
    for k in range(1, 16):
        kz, kc = k // 2, k % 2
        to = seq_of(lax.rem(z + kz, NZ), y, lax.rem(core + kc, 2))
        copies.append(remote(ghold, g2.at[k - 1], sems.at[28 + 2 * k], sems.at[29 + 2 * k], to, x))
    for one in copies:
        one.start()
    for one in copies:
        one.wait()
    for k in range(15):
        total += g2[k]
    out_ref[...] = total * norm_scale


def outgoing_kernel(
    norm_scale, tok_ref, at_ref, bg_ref, gain_ref, got_ref, dw_ref, dg_ref,
    at2, bg2, wsum, wb, xr, s1, wb2, yr, zs, zr, s3, g1, g2, ghold, send, recv, sems, gsems,
):
    greet(True)
    exchange_start(tok_ref, got_ref, send, recv)
    scatter_weight(
        at_ref, bg_ref, dw_ref, (at2, bg2, wsum, wb, xr, s1, wb2, yr, zs, zr, s3), sems, norm_scale
    )
    sum_gain(gain_ref, dg_ref, g1, g2, ghold, gsems, norm_scale)
    exchange_wait(tok_ref, got_ref, send, recv)


def outgoing(tok, at, bg, gain_terms, norm_scale):
    vmem = pl.BlockSpec(memory_space=pltpu.VMEM)

    def kernel(*refs):
        return outgoing_kernel(norm_scale, *refs)

    return pl.pallas_call(
        kernel,
        out_shape=(
            jax.ShapeDtypeStruct((SEQ, GROUP, D), BF16),
            jax.ShapeDtypeStruct((2, 2, 16, HALF), F32),
            jax.ShapeDtypeStruct((10, 128), F32),
        ),
        in_specs=[vmem] * 4,
        out_specs=(vmem,) * 3,
        scratch_shapes=[
            pltpu.VMEM((D, 256), BF16),
            pltpu.VMEM((256, HALF), BF16),
            pltpu.VMEM((NX, NY, 80, HALF), F32),
            pltpu.VMEM((NX, NY, 80, HALF), BF16),
            pltpu.VMEM((3, NY, 80, HALF), BF16),
            pltpu.VMEM((NY, 80, HALF), F32),
            pltpu.VMEM((NY, 80, HALF), BF16),
            pltpu.VMEM((3, 80, HALF), BF16),
            pltpu.VMEM((128, HALF), BF16),
            pltpu.VMEM((7, 16, HALF), BF16),
            pltpu.VMEM((16, HALF), F32),
            pltpu.VMEM((15, 10, 128), F32),
            pltpu.VMEM((15, 10, 128), F32),
            pltpu.VMEM((10, 128), F32),
            pltpu.SemaphoreType.DMA,
            pltpu.SemaphoreType.DMA,
            pltpu.SemaphoreType.DMA((36,)),
            pltpu.SemaphoreType.DMA((60,)),
        ],
        compiler_params=pltpu.CompilerParams(
            collective_id=1, has_side_effects=True, vmem_limit_bytes=LIMIT
        ),
    )(tok, at, bg, gain_terms)


def image_mask(shard_lengths, row_count):
    image_ends = jnp.cumsum(shard_lengths * GROUP)
    row_index = jnp.arange(row_count, dtype=jnp.int32)
    image_ids = jnp.sum((row_index[:, None] >= image_ends[None, :]).astype(jnp.int32), axis=1)
    return image_ids[:, None] == image_ids[None, :]


def forward(patch_rows, shard_lengths, gain, w_qkv, w_out):
    row_count, model_width = patch_rows.shape
    head_size = model_width // HEADS
    score_scale = 1.0 / math.sqrt(head_size)
    wide_rows = patch_rows.astype(jnp.float32)
    centred = wide_rows - jnp.mean(wide_rows, axis=-1, keepdims=True)
    inv_spread = lax.rsqrt(jnp.mean(centred * centred, axis=-1, keepdims=True) + eps)
    standard = centred * inv_spread
    normed = (standard * gain).astype(jnp.bfloat16)
    projected = jnp.dot(normed, w_qkv, preferred_element_type=jnp.float32).astype(jnp.bfloat16)
    queries = projected[:, :model_width].reshape(row_count, HEADS, head_size)
    key_rows = projected[:, model_width : 2 * model_width].reshape(row_count, HEADS, head_size)
    value_rows = projected[:, 2 * model_width :].reshape(row_count, HEADS, head_size)
    scores = (
        jnp.einsum("qhe,khe->hqk", queries, key_rows, preferred_element_type=jnp.float32)
        * score_scale
    )
    same_image = image_mask(shard_lengths, row_count)
    scores = jnp.where(same_image[None], scores, -jnp.inf)
    row_max = jnp.max(scores, axis=-1, keepdims=True)
    weights_exp = jnp.exp(scores - row_max)
    probs = weights_exp / jnp.sum(weights_exp, axis=-1, keepdims=True)
    probs_low = probs.astype(jnp.bfloat16)
    attended = jnp.einsum("hqk,khe->qhe", probs_low, value_rows, preferred_element_type=jnp.float32)
    attended = attended.astype(jnp.bfloat16).reshape(row_count, model_width)
    branch = jnp.dot(attended, w_out, preferred_element_type=jnp.float32)
    block = (wide_rows + branch).astype(jnp.bfloat16)
    return (
        block,
        (standard, inv_spread, queries, key_rows, value_rows, probs, probs_low, attended),
    )


def backward(saved, block_grad, gain, w_qkv, w_out):
    standard, inv_spread, queries, key_rows, value_rows, probs, probs_low, attended = saved
    row_count, model_width = block_grad.shape
    head_size = model_width // HEADS
    score_scale = 1.0 / math.sqrt(head_size)
    incoming = block_grad.astype(jnp.float32)
    grad_attended = lax.dot_general(
        block_grad, w_out, (((1,), (1,)), ((), ())), preferred_element_type=jnp.float32
    )
    grad_attended = grad_attended.astype(jnp.bfloat16).reshape(row_count, HEADS, head_size)
    grad_probs = jnp.einsum(
        "qhe,khe->hqk", grad_attended, value_rows, preferred_element_type=jnp.float32
    )
    grad_values = jnp.einsum(
        "hqk,qhe->khe", probs_low, grad_attended, preferred_element_type=jnp.float32
    ).astype(jnp.bfloat16)
    grad_scores = (
        probs * (grad_probs - jnp.sum(grad_probs * probs, axis=-1, keepdims=True)) * score_scale
    )
    grad_scores = grad_scores.astype(jnp.bfloat16)
    grad_queries = jnp.einsum(
        "hqk,khe->qhe", grad_scores, key_rows, preferred_element_type=jnp.float32
    ).astype(jnp.bfloat16)
    grad_keys = jnp.einsum(
        "hqk,qhe->khe", grad_scores, queries, preferred_element_type=jnp.float32
    ).astype(jnp.bfloat16)
    grad_projected = jnp.concatenate(
        [
            grad_queries.reshape(row_count, model_width),
            grad_keys.reshape(row_count, model_width),
            grad_values.reshape(row_count, model_width),
        ],
        axis=1,
    )
    grad_normed = lax.dot_general(
        grad_projected, w_qkv, (((1,), (1,)), ((), ())), preferred_element_type=jnp.float32
    )
    gain_grad = jnp.sum(grad_normed * standard, axis=0)
    grad_standard = grad_normed * gain
    grad_branch = inv_spread * (
        grad_standard
        - jnp.mean(grad_standard, axis=-1, keepdims=True)
        - standard * jnp.mean(grad_standard * standard, axis=-1, keepdims=True)
    )
    patch_grad = (incoming + grad_branch).astype(jnp.bfloat16)
    return (patch_grad, gain_grad)


def per_device(patches, lengths, token_dest, gain, w_qkv, w_out, cotangent):
    returned, wg = incoming(cotangent[0].reshape(SEQ, GROUP, D), w_out)
    full_out = jnp.transpose(wg[:, :, :, :40], (1, 2, 3, 0, 4)).reshape(D, D)
    patch_rows = patches[0]
    row_count, model_width = patch_rows.shape
    block, saved = forward(patch_rows, lengths[0, 0], gain, w_qkv, full_out)
    token_count = row_count // GROUP
    tokens = block.reshape(token_count, GROUP * model_width)
    slot_ids = token_dest[0] // token_count
    placing = (slot_ids[:, None] == jnp.arange(token_count, dtype=jnp.int32)[None, :]).astype(BF16)
    sent = lax.dot_general(
        placing, tokens, (((0,), (0,)), ((), ())), preferred_element_type=jnp.float32
    ).astype(BF16)
    token_grad = jnp.dot(
        placing, returned.reshape(SEQ, GROUP * D), preferred_element_type=jnp.float32
    ).astype(BF16)
    block_grad = token_grad.reshape(row_count, model_width)
    patch_grad, gain_grad = backward(saved, block_grad, gain, w_qkv, full_out)
    norm_scale = 1.0 / math.sqrt(row_count * SEQ * NX)
    merged, dw, dg = outgoing(
        sent.reshape(SEQ, GROUP, D), saved[7].T, block_grad, gain_grad.reshape(10, 128), norm_scale
    )
    own_weight = jnp.transpose(dw[:, :, :10], (0, 2, 1, 3)).reshape(20, D)
    own_gain = lax.dynamic_slice_in_dim(dg.reshape(D), lax.axis_index("seq") * 20, 20, 0)
    return (merged.reshape(1, SEQ, GROUP * D), patch_grad[None], own_weight, own_gain)


def solution(mesh):
    placed = (
        P("dp", "seq", None),
        P("dp", "seq", None),
        P("dp", "seq"),
        P(),
        P(),
        P("seq", None),
        P("dp", "seq", None),
    )
    return jax.shard_map(
        per_device,
        mesh=mesh,
        in_specs=placed,
        out_specs=(P("dp", "seq", None), P("dp", "seq", None), P("seq", None), P("seq")),
        check_vma=False,
    )
```

```python
import math

import jax
import jax.numpy as jnp
from jax import lax
from jax.experimental import pallas as pl
from jax.experimental.pallas import tpu as pltpu
from jax.sharding import PartitionSpec as P

HEADS = 16
GROUP = 4
D = 1280
HALF = 640
NZ, NY, NX = 8, 4, 4
SEQ = 64
LIMIT = 56 * 2**20

eps = 1e-06
F32 = jnp.float32
BF16 = jnp.bfloat16


def place():
    seq = lax.axis_index("seq")
    x = lax.axis_index("dp")
    return seq, x, lax.div(seq, 8), lax.rem(lax.div(seq, 2), 4), lax.rem(seq, 2)


def seq_of(z, y, core):
    return z * 8 + y * 2 + core


def dev(seq, x):
    return {"seq": seq, "dp": x}


def remote(src, dst, send, recv, seq, x):
    return pltpu.make_async_remote_copy(
        src_ref=src,
        dst_ref=dst,
        send_sem=send,
        recv_sem=recv,
        device_id=dev(seq, x),
        device_id_type=pl.DeviceIdType.MESH,
    )


def greet(with_xy):
    seq, x, z, y, core = place()
    barrier = pltpu.get_barrier_semaphore()

    @pl.loop(1, SEQ)
    def _(k):
        pl.semaphore_signal(
            barrier, inc=1, device_id=dev(lax.rem(seq + k, SEQ), x), device_id_type=pl.DeviceIdType.MESH
        )

    count = SEQ - 1
    if with_xy:
        for kx in range(1, NX):
            for ky in range(NY):
                pl.semaphore_signal(
                    barrier,
                    inc=1,
                    device_id=dev(seq_of(z, lax.rem(y + ky, NY), core), lax.rem(x + kx, NX)),
                    device_id_type=pl.DeviceIdType.MESH,
                )
                count += 1
    pl.semaphore_wait(barrier, count)


def exchange_start(src, dst, send, recv):
    seq, x, z, y, core = place()

    @pl.loop(1, SEQ)
    def _(k):
        to = lax.rem(seq + k, SEQ)
        remote(src.at[to], dst.at[seq], send, recv, to, x).start()

    pltpu.make_async_copy(src.at[seq], dst.at[seq], recv).start()


def exchange_wait(src, dst, send, recv):
    pltpu.make_async_copy(dst, dst, recv).wait()
    part = src.at[pl.ds(0, SEQ - 1)]
    pltpu.make_async_copy(part, part, send).wait()


def matmul(a, b):
    return jnp.dot(a, b, preferred_element_type=F32)


def matmul_t(a, b):
    return lax.dot_general(a, b, (((1,), (1,)), ((), ())), preferred_element_type=F32)


def one_hot(rows, columns, want):
    r = lax.broadcasted_iota(jnp.int32, (rows, columns), 0)
    c = lax.broadcasted_iota(jnp.int32, (rows, columns), 1)
    return jnp.where(want(r, c), 1.0, 0.0).astype(BF16)


WINDOWS = []
for _h in range(8):
    _first = 80 * _h // 128 * 128
    _off = 80 * _h - _first
    WINDOWS.append((_first, 128 if _off + 80 <= 128 else 256, _off))


def lanes_of(width, offset):
    lane = lax.broadcasted_iota(jnp.int32, (1, width), 1)
    return jnp.where((lane >= offset) & (lane < offset + 80), 1.0, 0.0).astype(BF16)


class Gather:
    def __init__(self, w_ref, slots, wg, sems):
        self.w_ref, self.slots, self.wg, self.sems = w_ref, slots, wg, sems

    def step0(self):
        seq, x, z, y, core = place()
        slots, sems = self.slots, self.sems
        own = jnp.concatenate([self.w_ref[...].astype(F32), jnp.zeros((12, D), F32)], axis=0)
        slots[core] = own.astype(BF16)
        self.now = [remote(slots.at[core], slots.at[core], sems.at[0], sems.at[1], seq_of(z, y, 1 - core), x)]
        self.start()

    def start(self):
        for one in self.now:
            one.start()

    def wait(self):
        for one in self.now:
            one.wait()

    def step1(self):
        seq, x, z, y, core = place()
        slots, sems, wg = self.slots, self.sems, self.wg
        self.wait()

        def want(r, c):
            return (c == jnp.where(r < 20, r, r + 12)) & (r < 40)

        first = pl.multiple_of(core * HALF, 128)
        rows = jnp.concatenate([slots[0, :, pl.ds(first, HALF)], slots[1, :, pl.ds(first, HALF)]], axis=0)
        wg[core, z, y] = matmul(one_hot(48, 64, want), rows).astype(BF16)
        self.now = []
        for k in range(1, NZ):
            self.now.append(
                remote(
                    wg.at[core, z, y], wg.at[core, z, y], sems.at[2 * k], sems.at[2 * k + 1],
                    seq_of(lax.rem(z + k, NZ), y, core), x,
                )
            )
        self.start()

    def step2(self):
        seq, x, z, y, core = place()
        sems, wg = self.sems, self.wg
        self.wait()
        self.now = []
        for k in range(1, NY):
            self.now.append(
                remote(
                    wg.at[core, :, y], wg.at[core, :, y], sems.at[14 + 2 * k], sems.at[15 + 2 * k],
                    seq_of(z, lax.rem(y + k, NY), core), x,
                )
            )
        self.start()

    def step3(self):
        seq, x, z, y, core = place()
        sems, wg = self.sems, self.wg
        self.wait()
        self.now = [remote(wg.at[core], wg.at[core], sems.at[22], sems.at[23], seq_of(z, y, 1 - core), x)]
        self.start()


class Scatter:
    def __init__(self, at_ref, bg_ref, out, bufs, sems, norm_scale):
        self.at_ref, self.bg_ref, self.out, self.bufs, self.sems = at_ref, bg_ref, out, bufs, sems
        self.norm_scale = norm_scale

    def start(self):
        for one in self.now:
            one.start()

    def wait(self):
        for one in self.now:
            one.wait()

    def send_attended(self):
        seq, x, z, y, core = place()
        partner = seq_of(z, y, 1 - core)
        self.now = [remote(self.at_ref, self.bufs[0], self.sems.at[0], self.sems.at[1], partner, x)]
        self.now[0].start()

    def send_grad(self):
        seq, x, z, y, core = place()
        partner = seq_of(z, y, 1 - core)
        theirs = pl.multiple_of((1 - core) * HALF, 128)
        one = remote(
            self.bg_ref.at[:, pl.ds(theirs, HALF)], self.bufs[1], self.sems.at[2], self.sems.at[3], partner, x
        )
        one.start()
        self.now.append(one)

    def product(self):
        at2, bg2, wsum, wb, xr, s1, wb2, yr, zs, zr, s3 = self.bufs
        seq, x, z, y, core = place()
        at_ref, bg_ref, sems = self.at_ref, self.bg_ref, self.sems
        mine = pl.multiple_of(core * HALF, 128)
        self.wait()

        @pl.loop(0, NX)
        def _(i):
            rows = pl.ds(pl.multiple_of(i * 320, 64), 320)
            part = matmul(at_ref[rows, :], bg_ref[:, pl.ds(mine, HALF)])
            part += matmul(at2[rows, :], bg2[...])
            part = part.reshape(NY, 80, HALF)
            wsum[i] = part
            wb[i] = part.astype(BF16)

        self.now = []
        for k in range(1, NX):
            to = lax.rem(x + k, NX)
            self.now.append(remote(wb.at[to], xr.at[k - 1], sems.at[2 + 2 * k], sems.at[3 + 2 * k], seq, to))
        self.start()

    def after_x(self):
        at2, bg2, wsum, wb, xr, s1, wb2, yr, zs, zr, s3 = self.bufs
        seq, x, z, y, core = place()
        sems = self.sems
        self.wait()

        @pl.loop(0, NY)
        def _(j):
            total = wsum[x, j]
            for k in range(3):
                total += xr[k, j].astype(F32)
            s1[j] = total
            wb2[j] = total.astype(BF16)

        self.now = []
        for k in range(1, NY):
            to = lax.rem(y + k, NY)
            self.now.append(
                remote(wb2.at[to], yr.at[k - 1], sems.at[8 + 2 * k], sems.at[9 + 2 * k], seq_of(z, to, core), x)
            )
        self.start()

    def after_y(self):
        at2, bg2, wsum, wb, xr, s1, wb2, yr, zs, zr, s3 = self.bufs
        seq, x, z, y, core = place()
        sems = self.sems
        self.wait()
        total = s1[y]
        for k in range(3):
            total += yr[k].astype(F32)

        def want(r, c):
            low = lax.rem(r, 16)
            return (c == lax.div(r, 16) * 10 + low) & (low < 10)

        zs[...] = matmul(one_hot(128, 80, want), total.astype(BF16)).astype(BF16)
        self.now = []
        for k in range(1, NZ):
            to = lax.rem(z + k, NZ)
            src = zs.at[pl.ds(pl.multiple_of(to * 16, 16), 16)]
            self.now.append(
                remote(src, zr.at[k - 1], sems.at[14 + 2 * k], sems.at[15 + 2 * k], seq_of(to, y, core), x)
            )
        self.start()

    def after_z(self):
        at2, bg2, wsum, wb, xr, s1, wb2, yr, zs, zr, s3 = self.bufs
        seq, x, z, y, core = place()
        sems, out = self.sems, self.out
        self.wait()
        total = zs[pl.ds(pl.multiple_of(z * 16, 16), 16), :].astype(F32)
        for k in range(7):
            total += zr[k].astype(F32)
        s3[...] = total * self.norm_scale
        owner = 16 * x + 4 * y + lax.div(z, 2)
        slot = out.at[lax.rem(z, 2), core]

        @pl.when(owner != seq)
        def _():
            remote(s3, slot, sems.at[30], sems.at[31], owner, x).start()

        @pl.when(owner == seq)
        def _():
            pltpu.make_async_copy(s3, slot, sems.at[31]).start()

    def share(self):
        seq, x, z, y, core = place()
        sems, out, s3 = self.sems, self.out, self.bufs[-1]
        owner = 16 * x + 4 * y + lax.div(z, 2)

        @pl.when(owner != seq)
        def _():
            pltpu.make_async_copy(s3, s3, sems.at[30]).wait()

        @pl.when(x == lax.div(seq, 16))
        def _():
            pltpu.make_async_copy(out, out, sems.at[31]).wait()
            for k in range(1, NX):
                remote(out, out, sems.at[31 + k], sems.at[35], seq, lax.rem(x + k, NX)).start()

    def finish(self):
        seq, x, z, y, core = place()
        sems, out = self.sems, self.out

        @pl.when(x == lax.div(seq, 16))
        def _():
            for k in range(1, NX):
                pltpu.make_async_copy(out, out, sems.at[31 + k]).wait()

        @pl.when(x != lax.div(seq, 16))
        def _():
            pltpu.make_async_copy(out, out, sems.at[35]).wait()


class GainSum:
    def __init__(self, ghold, g1, g2, sems):
        self.ghold, self.g1, self.g2, self.sems = ghold, g1, g2, sems

    def first(self, total):
        seq, x, z, y, core = place()
        self.ghold[0] = total
        self.now = []
        for k in range(1, 16):
            kx, ky = k // 4, k % 4
            to = seq_of(z, lax.rem(y + ky, NY), core)
            self.now.append(
                remote(
                    self.ghold.at[0], self.g1.at[k - 1], self.sems.at[2 * k - 2], self.sems.at[2 * k - 1],
                    to, lax.rem(x + kx, NX),
                )
            )
        for one in self.now:
            one.start()

    def second(self):
        seq, x, z, y, core = place()
        for one in self.now:
            one.wait()
        total = self.ghold[0]
        for k in range(15):
            total += self.g1[k]
        self.ghold[1] = total
        self.now = []
        for k in range(1, 16):
            kz, kc = k // 2, k % 2
            to = seq_of(lax.rem(z + kz, NZ), y, lax.rem(core + kc, 2))
            self.now.append(
                remote(
                    self.ghold.at[1], self.g2.at[k - 1], self.sems.at[28 + 2 * k], self.sems.at[29 + 2 * k], to, x
                )
            )
        for one in self.now:
            one.start()

    def finish(self):
        for one in self.now:
            one.wait()
        total = self.ghold[1]
        for k in range(15):
            total += self.g2[k]
        return total


def kernel_body(norm_scale, refs):
    (x_ref, rowi_ref, coli_ref, gain_ref, gaincol_ref, wqkv_hbm, wout_ref, cot_ref,
     merged_ref, gx_ref, dw_ref, dg_ref,
     wqkv, slots, wg, cslab, crecv, tok, got, xp, normed, kv, projt, eye, perm, permt, probs, at, atp, apad, bg, dat, gt, gn,
     at2, bg2, wsum, wb, xr, s1, wb2, yr, zs, zr, s3, ghold, g1, g2,
     wsem, asem, csend, crecvs, tsend, trecvs, ssem, gsem) = refs
    score_scale = 1.0 / math.sqrt(80)

    loads = []
    for j in range(3):
        cols = pl.ds(j * D, D)
        loads.append(pltpu.make_async_copy(wqkv_hbm.at[:, cols], wqkv.at[:, cols], wsem.at[j]))
    for one in loads:
        one.start()

    def shuffle(r, c):
        return c == lax.rem(r, 4) * 64 + lax.div(r, 4)

    stacked = jnp.concatenate([cot_ref[:, pl.ds(c * D, D)] for c in range(4)], axis=0)
    cslab[...] = matmul(one_hot(256, 256, shuffle), stacked).astype(BF16).reshape(SEQ, GROUP, D)
    greet(True)
    gather = Gather(wout_ref, slots, wg, asem)
    gather.step0()
    exchange_start(cslab, crecv, csend, crecvs)

    key_row, key_col = rowi_ref[0:1, :], coli_ref[:, 0:1]
    id_row, id_col = rowi_ref[1:2, :], coli_ref[:, 1:2]
    ir = lax.broadcasted_iota(jnp.int32, (256, 256), 0)
    ic = lax.broadcasted_iota(jnp.int32, (256, 256), 1)
    eye[...] = jnp.where(ir == ic, 1.0, 0.0).astype(BF16)
    perm[...] = jnp.where(ir == key_row, 1.0, 0.0).astype(BF16)
    permt[...] = jnp.where(ic == key_col, 1.0, 0.0).astype(BF16)
    ids_k = jnp.sum(jnp.where(ir == key_row, id_row.astype(F32), 0.0), axis=1, keepdims=True)
    ids_q = jnp.sum(jnp.where(ic == key_col, id_col.astype(F32), 0.0), axis=0, keepdims=True)

    wide = matmul(perm[...], x_ref[...])
    xp[...] = wide.astype(BF16)
    centred = wide - jnp.mean(wide, axis=-1, keepdims=True)
    spread = lax.rsqrt(jnp.mean(centred * centred, axis=-1, keepdims=True) + eps)
    normed[...] = (centred * spread * gain_ref[...]).astype(BF16)
    gather.step1()

    for j in range(3):
        loads[j].wait()

        @pl.loop(0, 5)
        def _(i):
            cols = pl.ds(pl.multiple_of(j * D + i * 256, 256), 256)
            part = matmul(normed[...], wqkv[:, cols]).astype(BF16)
            if j > 0:
                kv[:, pl.ds(pl.multiple_of((j - 1) * D + i * 256, 256), 256)] = part
            projt[cols, :] = matmul_t(eye[...], part).astype(BF16)

    gather.step2()
    same = ids_k == ids_q

    @pl.loop(0, 2)
    def _(g):
        for h in range(8):
            first, width, off = WINDOWS[h]
            lanes = pl.ds(pl.multiple_of(g * HALF + first, 128), width)
            rows = pl.multiple_of(g * HALF + h * 80, 16)
            keys = kv[:, lanes] * lanes_of(width, off)
            scores = matmul(keys, projt[lanes, :]) * score_scale
            scores = jnp.where(same, scores, -jnp.inf)
            scores = jnp.exp(scores - jnp.max(scores, axis=0, keepdims=True))
            share = scores * (1.0 / jnp.sum(scores, axis=0, keepdims=True))
            probs[g * 8 + h] = share
            part = matmul(projt[pl.ds(2 * D + rows, 80), :], share.astype(BF16))
            at[pl.ds(rows, 80), :] = part.astype(BF16)
            gap = jnp.zeros((8, 256), F32)
            padded = jnp.concatenate([part[0:40], gap, part[40:80], gap], axis=0).astype(BF16)
            atp[pl.ds(pl.multiple_of(g * 768 + h * 96, 16), 96), :] = padded

    gather.step3()
    scatter = Scatter(
        at, bg, dw_ref, (at2, bg2, wsum, wb, xr, s1, wb2, yr, zs, zr, s3), ssem, norm_scale
    )
    scatter.send_attended()
    exchange_wait(cslab, crecv, csend, crecvs)
    bg[...] = crecv[...].reshape(256, D)
    scatter.send_grad()
    for j in range(6):
        apad[:, pl.ds(j * 256, 256)] = matmul_t(eye[...], atp[pl.ds(j * 256, 256), :]).astype(BF16)
    scatter.product()

    gather.wait()
    for half in range(2):
        cols = pl.ds(half * HALF, HALF)
        branch = matmul(apad[...], wg[half].reshape(1536, HALF))
        block = (xp[:, cols].astype(F32) + branch).astype(BF16)
        tok[:, :, cols] = block.reshape(SEQ, GROUP, HALF)
    exchange_start(tok, got, tsend, trecvs)

    @pl.loop(0, 4)
    def _(i):
        part = matmul_t(wg[0, pl.ds(2 * i, 2)].reshape(384, HALF), bg[:, pl.ds(0, HALF)])
        part += matmul_t(wg[1, pl.ds(2 * i, 2)].reshape(384, HALF), bg[:, pl.ds(HALF, HALF)])
        for h in range(4):
            own = part[96 * h : 96 * h + 96]
            own = jnp.concatenate([own[0:40], own[48:88]], axis=0).astype(BF16)
            dat[pl.ds(pl.multiple_of(i * 320 + 80 * h, 16), 80), :] = own

    def back(g):
        for h in range(8):
            first, width, off = WINDOWS[h]
            lanes = pl.ds(pl.multiple_of(g * HALF + first, 128), width)
            rows = pl.multiple_of(g * HALF + h * 80, 16)
            values = kv[:, pl.ds(pl.multiple_of(D + g * HALF + first, 128), width)] * lanes_of(width, off)
            share = probs[g * 8 + h]
            gp = matmul(values, dat[lanes, :])
            delta = jnp.sum(gp * share, axis=0, keepdims=True)
            gs = (share * (gp - delta) * score_scale).astype(BF16)
            low = share.astype(BF16)
            gt[pl.ds(rows, 80), :] = matmul(projt[pl.ds(D + rows, 80), :], gs).astype(BF16)
            gt[pl.ds(D + rows, 80), :] = matmul_t(projt[pl.ds(rows, 80), :], gs).astype(BF16)
            gt[pl.ds(2 * D + rows, 80), :] = matmul_t(dat[pl.ds(rows, 80), :], low).astype(BF16)

    @pl.loop(0, 2)
    def _(g):
        back(g)

    scatter.after_x()

    def standard_of(i):
        return matmul_t(eye[...], xp[:, pl.ds(pl.multiple_of(i * 256, 256), 256)])

    def sums(i, carry):
        return carry + jnp.sum(standard_of(i), axis=0, keepdims=True)

    mean = lax.fori_loop(0, 5, sums, jnp.zeros((1, 256), F32)) * (1.0 / D)

    def squares(i, carry):
        part = standard_of(i) - mean
        return carry + jnp.sum(part * part, axis=0, keepdims=True)

    inv = lax.rsqrt(lax.fori_loop(0, 5, squares, jnp.zeros((1, 256), F32)) * (1.0 / D) + eps)

    def grads(i, carry):
        rows = pl.ds(pl.multiple_of(i * 256, 256), 256)
        part = matmul(wqkv[rows, :], gt[...])
        std = (standard_of(i) - mean) * inv
        both = part * std
        hi = both.astype(BF16)
        rest = both - hi.astype(F32)
        mid = rest.astype(BF16)
        lo = (rest - mid.astype(F32)).astype(BF16)
        ones = jnp.ones((8, 256), BF16)
        row = matmul_t(ones, hi) + matmul_t(ones, mid) + matmul_t(ones, lo)
        ghold[2, :, rows] = row[0:1]
        scaled = part * gaincol_ref[rows, :]
        gn[rows, :] = scaled
        a, b = carry
        return (a + jnp.sum(scaled, axis=0, keepdims=True), b + jnp.sum(scaled * std, axis=0, keepdims=True))

    zero = jnp.zeros((1, 256), F32)
    mean_g, mean_gs = lax.fori_loop(0, 5, grads, (zero, zero))
    gains = GainSum(ghold, g1, g2, gsem)
    gains.first(ghold[2])
    scatter.after_y()
    mean_g = mean_g * (1.0 / D)
    mean_gs = mean_gs * (1.0 / D)

    @pl.loop(0, 5)
    def _(i):
        rows = pl.ds(pl.multiple_of(i * 256, 256), 256)
        std = (standard_of(i) - mean) * inv
        branch = inv * (gn[rows, :] - mean_g - std * mean_gs)
        total = (matmul_t(eye[...], bg[:, rows]) + branch).astype(BF16)
        gx_ref[:, rows] = matmul_t(permt[...], total).astype(BF16)

    gains.second()
    scatter.after_z()
    exchange_wait(tok, got, tsend, trecvs)

    def unshuffle(r, c):
        return r == lax.rem(c, 4) * 64 + lax.div(c, 4)

    unmix = one_hot(256, 256, unshuffle)
    ordered = matmul(unmix, got[...].reshape(256, D)).astype(BF16)
    for c in range(4):
        merged_ref[:, pl.ds(c * D, D)] = ordered[64 * c : 64 * c + 64]
    scatter.share()
    dg_ref[...] = gains.finish() * norm_scale
    scatter.finish()


def per_device(patches, lengths, token_dest, gain, w_qkv, w_out, cotangent):
    norm_scale = 1.0 / math.sqrt(256 * SEQ * NX)
    row = jnp.arange(256, dtype=jnp.int32)
    slot = jnp.repeat(token_dest[0] // 64, GROUP)
    key = slot * GROUP + row % GROUP
    ends = jnp.cumsum(lengths[0, 0] * GROUP)
    ids = jnp.sum((row[:, None] >= ends[None, :]).astype(jnp.int32), axis=1)
    rows = jnp.stack([key, ids])
    columns = jnp.stack([key, ids], axis=1)
    vmem = pl.BlockSpec(memory_space=pltpu.VMEM)
    hbm = pl.BlockSpec(memory_space=pl.ANY)

    def kernel(*refs):
        kernel_body(norm_scale, refs)

    merged, gx, dw, dg = pl.pallas_call(
        kernel,
        out_shape=(
            jax.ShapeDtypeStruct((SEQ, GROUP * D), BF16),
            jax.ShapeDtypeStruct((256, D), BF16),
            jax.ShapeDtypeStruct((2, 2, 16, HALF), F32),
            jax.ShapeDtypeStruct((1, D), F32),
        ),
        in_specs=[vmem] * 5 + [hbm] + [vmem] * 2,
        out_specs=(vmem,) * 4,
        scratch_shapes=[
            pltpu.VMEM((D, 3 * D), BF16),
            pltpu.VMEM((2, 32, D), BF16),
            pltpu.VMEM((2, NZ, NY, 48, HALF), BF16),
            pltpu.VMEM((SEQ, GROUP, D), BF16),
            pltpu.VMEM((SEQ, GROUP, D), BF16),
            pltpu.VMEM((SEQ, GROUP, D), BF16),
            pltpu.VMEM((SEQ, GROUP, D), BF16),
            pltpu.VMEM((256, D), BF16),
            pltpu.VMEM((256, D), BF16),
            pltpu.VMEM((256, 2 * D), BF16),
            pltpu.VMEM((3 * D, 256), BF16),
            pltpu.VMEM((256, 256), BF16),
            pltpu.VMEM((256, 256), BF16),
            pltpu.VMEM((256, 256), BF16),
            pltpu.VMEM((HEADS, 256, 256), F32),
            pltpu.VMEM((D, 256), BF16),
            pltpu.VMEM((1536, 256), BF16),
            pltpu.VMEM((256, 1536), BF16),
            pltpu.VMEM((256, D), BF16),
            pltpu.VMEM((D, 256), BF16),
            pltpu.VMEM((3 * D, 256), BF16),
            pltpu.VMEM((D, 256), F32),
            pltpu.VMEM((D, 256), BF16),
            pltpu.VMEM((256, HALF), BF16),
            pltpu.VMEM((NX, NY, 80, HALF), F32),
            pltpu.VMEM((NX, NY, 80, HALF), BF16),
            pltpu.VMEM((3, NY, 80, HALF), BF16),
            pltpu.VMEM((NY, 80, HALF), F32),
            pltpu.VMEM((NY, 80, HALF), BF16),
            pltpu.VMEM((3, 80, HALF), BF16),
            pltpu.VMEM((128, HALF), BF16),
            pltpu.VMEM((7, 16, HALF), BF16),
            pltpu.VMEM((16, HALF), F32),
            pltpu.VMEM((3, 1, D), F32),
            pltpu.VMEM((15, 1, D), F32),
            pltpu.VMEM((15, 1, D), F32),
            pltpu.SemaphoreType.DMA((3,)),
            pltpu.SemaphoreType.DMA((24,)),
            pltpu.SemaphoreType.DMA,
            pltpu.SemaphoreType.DMA,
            pltpu.SemaphoreType.DMA,
            pltpu.SemaphoreType.DMA,
            pltpu.SemaphoreType.DMA((36,)),
            pltpu.SemaphoreType.DMA((60,)),
        ],
        compiler_params=pltpu.CompilerParams(
            collective_id=0, has_side_effects=True, vmem_limit_bytes=LIMIT
        ),
    )(
        patches[0], rows, columns, gain.reshape(1, D), gain.reshape(D, 1), w_qkv, w_out,
        cotangent[0],
    )
    own_weight = jnp.transpose(dw[:, :, :10], (0, 2, 1, 3)).reshape(20, D)
    own_gain = lax.dynamic_slice_in_dim(dg.reshape(D), lax.axis_index("seq") * 20, 20, 0)
    return (merged[None], gx[None], own_weight, own_gain)


def solution(mesh):
    placed = (
        P("dp", "seq", None),
        P("dp", "seq", None),
        P("dp", "seq"),
        P(),
        P(),
        P("seq", None),
        P("dp", "seq", None),
    )
    return jax.shard_map(
        per_device,
        mesh=mesh,
        in_specs=placed,
        out_specs=(P("dp", "seq", None), P("dp", "seq", None), P("seq", None), P("seq")),
        check_vma=False,
    )
```

```python
import math

import jax
import jax.numpy as jnp
from jax import lax
from jax.experimental import pallas as pl
from jax.experimental.pallas import tpu as pltpu
from jax.sharding import PartitionSpec as P

HEADS = 16
GROUP = 4
D = 1280
HALF = 640
NZ, NY, NX = 8, 4, 4
SEQ = 64
LIMIT = 56 * 2**20

eps = 1e-06
F32 = jnp.float32
BF16 = jnp.bfloat16


def place():
    seq = lax.axis_index("seq")
    x = lax.axis_index("dp")
    return seq, x, lax.div(seq, 8), lax.rem(lax.div(seq, 2), 4), lax.rem(seq, 2)


def seq_of(z, y, core):
    return z * 8 + y * 2 + core


def dev(seq, x):
    return {"seq": seq, "dp": x}


def remote(src, dst, send, recv, seq, x):
    return pltpu.make_async_remote_copy(
        src_ref=src,
        dst_ref=dst,
        send_sem=send,
        recv_sem=recv,
        device_id=dev(seq, x),
        device_id_type=pl.DeviceIdType.MESH,
    )


def owner_of(x, y, z):
    return 16 * x + 4 * y + lax.div(z, 2)


def greet():
    seq, x, z, y, core = place()
    barrier = pltpu.get_barrier_semaphore()

    def signal(to, where):
        pl.semaphore_signal(barrier, inc=1, device_id=dev(to, where), device_id_type=pl.DeviceIdType.MESH)

    @pl.loop(1, SEQ)
    def _(k):
        signal(lax.rem(seq + k, SEQ), x)

    for kx in range(1, NX):
        for ky in range(NY):
            signal(seq_of(z, lax.rem(y + ky, NY), core), lax.rem(x + kx, NX))
        signal(owner_of(x, y, z), lax.rem(x + kx, NX))

    @pl.when(x != lax.div(seq, 16))
    def _():
        for part in range(2):
            for other in range(2):
                to = seq_of(2 * lax.rem(seq, 4) + part, lax.rem(lax.div(seq, 4), 4), other)
                signal(to, lax.div(seq, 16))


def all_here():
    seq, x, z, y, core = place()
    count = SEQ - 1 + 12 + 3 + jnp.where(x != lax.div(seq, 16), 4, 0)
    pl.semaphore_wait(pltpu.get_barrier_semaphore(), count)


def exchange_start(src, dst, send, recv):
    seq, x, z, y, core = place()

    @pl.loop(1, SEQ)
    def _(k):
        to = lax.rem(seq + k, SEQ)
        remote(src.at[to], dst.at[seq], send, recv, to, x).start()

    pltpu.make_async_copy(src.at[seq], dst.at[seq], recv).start()


def exchange_wait(src, dst, send, recv):
    pltpu.make_async_copy(dst, dst, recv).wait()
    part = src.at[pl.ds(0, SEQ - 1)]
    pltpu.make_async_copy(part, part, send).wait()


def matmul(a, b):
    return jnp.dot(a, b, preferred_element_type=F32)


def matmul_t(a, b):
    return lax.dot_general(a, b, (((1,), (1,)), ((), ())), preferred_element_type=F32)


def one_hot(rows, columns, want):
    r = lax.broadcasted_iota(jnp.int32, (rows, columns), 0)
    c = lax.broadcasted_iota(jnp.int32, (rows, columns), 1)
    return jnp.where(want(r, c), 1.0, 0.0).astype(BF16)


WINDOWS = []
for _h in range(8):
    _first = 80 * _h // 128 * 128
    _off = 80 * _h - _first
    WINDOWS.append((_first, 128 if _off + 80 <= 128 else 256, _off))


def lanes_of(width, offset):
    lane = lax.broadcasted_iota(jnp.int32, (1, width), 1)
    return jnp.where((lane >= offset) & (lane < offset + 80), 1.0, 0.0).astype(BF16)


class Gather:
    def __init__(self, w_ref, slots, wg, sems):
        self.w_ref, self.slots, self.wg, self.sems = w_ref, slots, wg, sems
        self.p, self.q = pl.ds(0, 256), pl.ds(256, 384)

    def pair(self):
        seq, x, z, y, core = place()
        slots, sems = self.slots, self.sems
        own = jnp.concatenate([self.w_ref[...].astype(F32), jnp.zeros((12, D), F32)], axis=0)
        slots[core] = own.astype(BF16)
        self.first = remote(slots.at[core], slots.at[core], sems.at[0], sems.at[1], seq_of(z, y, 1 - core), x)
        self.first.start()

    def along_z(self):
        seq, x, z, y, core = place()
        slots, sems, wg = self.slots, self.sems, self.wg
        zh, zl = lax.div(z, 4), lax.rem(z, 4)
        self.first.wait()

        def want(r, c):
            return (c == jnp.where(r < 20, r, r + 12)) & (r < 40)

        first = pl.multiple_of(core * HALF, 128)
        rows = jnp.concatenate([slots[0, :, pl.ds(first, HALF)], slots[1, :, pl.ds(first, HALF)]], axis=0)
        own = matmul(one_hot(48, 64, want), rows).astype(BF16)
        wg[core, zh, zl, y, :, self.p] = own[:, 0:256]

        @pl.when(zl == x)
        def _():
            wg[core, zh, zl, y, :, self.q] = own[:, 256:640]
            part = wg.at[core, zh, zl, y, :, self.q]
            for k in range(1, NZ):
                to = seq_of(lax.rem(z + k, NZ), y, core)
                remote(part, part, sems.at[1 + k], sems.at[9 + zh], to, x).start()

        self.pz = []
        part = wg.at[core, zh, zl, y, :, self.p]
        for k in range(1, NZ):
            to = seq_of(lax.rem(z + k, NZ), y, core)
            self.pz.append(remote(part, part, sems.at[10 + 2 * k], sems.at[11 + 2 * k], to, x))
        for one in self.pz:
            one.start()

    def q_along_y(self):
        seq, x, z, y, core = place()
        sems, wg = self.sems, self.wg
        for j in range(2):

            @pl.when(z != x + 4 * j)
            def _():
                part = wg.at[core, j, x, y, :, self.q]
                pltpu.make_async_copy(part, part, sems.at[9 + j]).wait()

        part = wg.at[core, :, x, y, :, self.q]
        self.qy = []
        for k in range(1, NY):
            to = seq_of(z, lax.rem(y + k, NY), core)
            self.qy.append(remote(part, part, sems.at[26 + 2 * k], sems.at[27 + 2 * k], to, x))
        for one in self.qy:
            one.start()

    def p_along_y(self):
        seq, x, z, y, core = place()
        sems, wg = self.sems, self.wg
        for one in self.pz:
            one.wait()
        part = wg.at[core, :, :, y, :, self.p]
        self.py = []
        for k in range(1, NY):
            to = seq_of(z, lax.rem(y + k, NY), core)
            self.py.append(remote(part, part, sems.at[32 + 2 * k], sems.at[33 + 2 * k], to, x))
        for one in self.py:
            one.start()

    def q_along_x(self):
        seq, x, z, y, core = place()
        sems, wg = self.sems, self.wg
        for one in self.qy:
            one.wait()
        part = wg.at[core, :, x, :, :, self.q]
        self.qx = []
        for k in range(1, NX):
            self.qx.append(
                remote(part, part, sems.at[38 + 2 * k], sems.at[39 + 2 * k], seq, lax.rem(x + k, NX))
            )
        for one in self.qx:
            one.start()

    def p_pair(self):
        seq, x, z, y, core = place()
        for one in self.py:
            one.wait()
        part = self.wg.at[core, :, :, :, :, self.p]
        self.pc = remote(part, part, self.sems.at[46], self.sems.at[47], seq_of(z, y, 1 - core), x)
        self.pc.start()

    def q_pair(self):
        seq, x, z, y, core = place()
        for one in self.qx:
            one.wait()
        part = self.wg.at[core, :, :, :, :, self.q]
        self.qc = remote(part, part, self.sems.at[48], self.sems.at[49], seq_of(z, y, 1 - core), x)
        self.qc.start()

    def finish(self):
        seq, x, z, y, core = place()
        self.pc.wait()
        self.qc.wait()

        @pl.when(lax.rem(z, 4) == x)
        def _():
            part = self.wg.at[core, 0, 0, 0, :, self.q]
            for k in range(1, NZ):
                pltpu.make_async_copy(part, part, self.sems.at[1 + k]).wait()


class Scatter:
    def __init__(self, at_ref, bg_ref, out, bufs, sems, norm_scale):
        self.at_ref, self.bg_ref, self.out, self.bufs, self.sems = at_ref, bg_ref, out, bufs, sems
        self.norm_scale = norm_scale
        self.a, self.b = pl.ds(0, 384), pl.ds(384, 256)

    def start(self):
        for one in self.now:
            one.start()

    def wait(self):
        for one in self.now:
            one.wait()

    def send_attended(self):
        seq, x, z, y, core = place()
        partner = seq_of(z, y, 1 - core)
        self.now = [remote(self.at_ref, self.bufs[0], self.sems.at[0], self.sems.at[1], partner, x)]
        self.now[0].start()

    def send_grad(self):
        seq, x, z, y, core = place()
        partner = seq_of(z, y, 1 - core)
        theirs = pl.multiple_of((1 - core) * HALF, 128)
        one = remote(
            self.bg_ref.at[:, pl.ds(theirs, HALF)], self.bufs[1], self.sems.at[2], self.sems.at[3], partner, x
        )
        one.start()
        self.now.append(one)

    def product(self):
        at2, bg2, wsum, wb, xa, yb, sa, sb, wa2, wb2, ya, xb, zs, zr, s3 = self.bufs
        seq, x, z, y, core = place()
        at_ref, bg_ref, sems = self.at_ref, self.bg_ref, self.sems
        mine = pl.multiple_of(core * HALF, 128)
        self.wait()

        @pl.loop(0, NX)
        def _(i):
            rows = pl.ds(pl.multiple_of(i * 320, 64), 320)
            part = matmul(at_ref[rows, :], bg_ref[:, pl.ds(mine, HALF)])
            part += matmul(at2[rows, :], bg2[...])
            part = part.reshape(NY, 80, HALF)
            wsum[i] = part
            wb[i] = part.astype(BF16)

        self.now = []
        for k in range(1, NX):
            to = lax.rem(x + k, NX)
            self.now.append(
                remote(wb.at[to, :, :, self.a], xa.at[k - 1], sems.at[2 + 2 * k], sems.at[3 + 2 * k], seq, to)
            )
            to = lax.rem(y + k, NY)
            self.now.append(
                remote(
                    wb.at[:, to, :, self.b], yb.at[k - 1], sems.at[8 + 2 * k], sems.at[9 + 2 * k],
                    seq_of(z, to, core), x,
                )
            )
        self.start()

    def after_one(self):
        at2, bg2, wsum, wb, xa, yb, sa, sb, wa2, wb2, ya, xb, zs, zr, s3 = self.bufs
        seq, x, z, y, core = place()
        sems = self.sems
        self.wait()

        @pl.loop(0, 4)
        def _(j):
            total = wsum[x, j, :, self.a]
            for k in range(3):
                total += xa[k, j].astype(F32)
            sa[j] = total
            wa2[j] = total.astype(BF16)
            total = wsum[j, y, :, self.b]
            for k in range(3):
                total += yb[k, j].astype(F32)
            sb[j] = total
            wb2[j] = total.astype(BF16)

        self.now = []
        for k in range(1, NY):
            to = lax.rem(y + k, NY)
            self.now.append(
                remote(wa2.at[to], ya.at[k - 1], sems.at[14 + 2 * k], sems.at[15 + 2 * k], seq_of(z, to, core), x)
            )
            to = lax.rem(x + k, NX)
            self.now.append(remote(wb2.at[to], xb.at[k - 1], sems.at[20 + 2 * k], sems.at[21 + 2 * k], seq, to))
        self.start()

    def after_two(self):
        at2, bg2, wsum, wb, xa, yb, sa, sb, wa2, wb2, ya, xb, zs, zr, s3 = self.bufs
        seq, x, z, y, core = place()
        sems = self.sems
        self.wait()
        total = sa[y]
        for k in range(3):
            total += ya[k].astype(F32)
        second = sb[x]
        for k in range(3):
            second += xb[k].astype(F32)

        def want(r, c):
            low = lax.rem(r, 16)
            return (c == lax.div(r, 16) * 10 + low) & (low < 10)

        chosen = one_hot(128, 80, want)
        zs[:, self.a] = matmul(chosen, total.astype(BF16)).astype(BF16)
        zs[:, self.b] = matmul(chosen, second.astype(BF16)).astype(BF16)
        self.now = []
        for k in range(1, NZ):
            to = lax.rem(z + k, NZ)
            src = zs.at[pl.ds(pl.multiple_of(to * 16, 16), 16)]
            self.now.append(
                remote(src, zr.at[k - 1], sems.at[26 + 2 * k], sems.at[27 + 2 * k], seq_of(to, y, core), x)
            )
        self.start()

    def after_z(self):
        zs, zr, s3 = self.bufs[-3:]
        seq, x, z, y, core = place()
        sems, out = self.sems, self.out
        self.wait()
        total = zs[pl.ds(pl.multiple_of(z * 16, 16), 16), :].astype(F32)
        for k in range(7):
            total += zr[k].astype(F32)
        s3[...] = total * self.norm_scale
        owner = owner_of(x, y, z)
        slot = out.at[lax.rem(z, 2), core]
        self.now = []
        for k in range(1, NX):
            self.now.append(remote(s3, slot, sems.at[41 + k], sems.at[46], owner, lax.rem(x + k, NX)))
        self.start()

        @pl.when(owner != seq)
        def _():
            remote(s3, slot, sems.at[45], sems.at[46], owner, x).start()

        @pl.when(owner == seq)
        def _():
            pltpu.make_async_copy(s3, slot, sems.at[46]).start()

    def finish(self):
        seq, x, z, y, core = place()
        sems, out, s3 = self.sems, self.out, self.bufs[-1]
        for one in self.now:
            one.wait_send()

        @pl.when(owner_of(x, y, z) != seq)
        def _():
            pltpu.make_async_copy(s3, s3, sems.at[45]).wait()

        pltpu.make_async_copy(out, out, sems.at[46]).wait()


class GainSum:
    def __init__(self, ghold, g1, g2, sems):
        self.ghold, self.g1, self.g2, self.sems = ghold, g1, g2, sems

    def first(self, total):
        seq, x, z, y, core = place()
        self.ghold[0] = total
        self.now = []
        for k in range(1, 16):
            kx, ky = k // 4, k % 4
            to = seq_of(z, lax.rem(y + ky, NY), core)
            self.now.append(
                remote(
                    self.ghold.at[0], self.g1.at[k - 1], self.sems.at[2 * k - 2], self.sems.at[2 * k - 1],
                    to, lax.rem(x + kx, NX),
                )
            )
        for one in self.now:
            one.start()

    def second(self):
        seq, x, z, y, core = place()
        for one in self.now:
            one.wait()
        total = self.ghold[0]
        for k in range(15):
            total += self.g1[k]
        self.ghold[1] = total
        self.now = []
        for k in range(1, 16):
            kz, kc = k // 2, k % 2
            to = seq_of(lax.rem(z + kz, NZ), y, lax.rem(core + kc, 2))
            self.now.append(
                remote(
                    self.ghold.at[1], self.g2.at[k - 1], self.sems.at[28 + 2 * k], self.sems.at[29 + 2 * k], to, x
                )
            )
        for one in self.now:
            one.start()

    def finish(self):
        for one in self.now:
            one.wait()
        total = self.ghold[1]
        for k in range(15):
            total += self.g2[k]
        return total


def kernel_body(norm_scale, refs):
    (x_ref, rowi_ref, coli_ref, gain_ref, gaincol_ref, wqkv_hbm, wout_ref, cot_ref,
     merged_ref, gx_ref, dw_ref, dg_ref,
     wqkv, slots, wg, cslab, crecv, tok, got, xp, normed, kv, projt, eye, perm, permt, probs, at, atp, apad, bg, dat, gt, gn,
     at2, bg2, wsum, wb, xa, yb, sa, sb, wa2, wb2, ya, xb, zs, zr, s3, ghold, g1, g2,
     wsem, asem, csend, crecvs, tsend, trecvs, ssem, gsem) = refs
    score_scale = 1.0 / math.sqrt(80)

    loads = []
    for j in range(3):
        cols = pl.ds(j * D, D)
        loads.append(pltpu.make_async_copy(wqkv_hbm.at[:, cols], wqkv.at[:, cols], wsem.at[j]))
    for one in loads:
        one.start()

    greet()

    def shuffle(r, c):
        return c == lax.rem(r, 4) * 64 + lax.div(r, 4)

    stacked = jnp.concatenate([cot_ref[:, pl.ds(c * D, D)] for c in range(4)], axis=0)
    cslab[...] = matmul(one_hot(256, 256, shuffle), stacked).astype(BF16).reshape(SEQ, GROUP, D)
    all_here()
    gather = Gather(wout_ref, slots, wg, asem)
    gather.pair()

    key_row, key_col = rowi_ref[0:1, :], coli_ref[:, 0:1]
    id_row, id_col = rowi_ref[1:2, :], coli_ref[:, 1:2]
    ir = lax.broadcasted_iota(jnp.int32, (256, 256), 0)
    ic = lax.broadcasted_iota(jnp.int32, (256, 256), 1)
    eye[...] = jnp.where(ir == ic, 1.0, 0.0).astype(BF16)
    perm[...] = jnp.where(ir == key_row, 1.0, 0.0).astype(BF16)
    permt[...] = jnp.where(ic == key_col, 1.0, 0.0).astype(BF16)
    ids_k = jnp.sum(jnp.where(ir == key_row, id_row.astype(F32), 0.0), axis=1, keepdims=True)
    ids_q = jnp.sum(jnp.where(ic == key_col, id_col.astype(F32), 0.0), axis=0, keepdims=True)

    wide = matmul(perm[...], x_ref[...])
    xp[...] = wide.astype(BF16)
    centred = wide - jnp.mean(wide, axis=-1, keepdims=True)
    spread = lax.rsqrt(jnp.mean(centred * centred, axis=-1, keepdims=True) + eps)
    normed[...] = (centred * spread * gain_ref[...]).astype(BF16)
    gather.along_z()
    exchange_start(cslab, crecv, csend, crecvs)

    for j in range(3):
        loads[j].wait()
        if j == 2:
            gather.q_along_y()

        @pl.loop(0, 5)
        def _(i):
            cols = pl.ds(pl.multiple_of(j * D + i * 256, 256), 256)
            part = matmul(normed[...], wqkv[:, cols]).astype(BF16)
            if j > 0:
                kv[:, pl.ds(pl.multiple_of((j - 1) * D + i * 256, 256), 256)] = part
            projt[cols, :] = matmul_t(eye[...], part).astype(BF16)

    gather.p_along_y()
    same = ids_k == ids_q

    def attend(g):
        for h in range(8):
            first, width, off = WINDOWS[h]
            lanes = pl.ds(pl.multiple_of(g * HALF + first, 128), width)
            rows = pl.multiple_of(g * HALF + h * 80, 16)
            keys = kv[:, lanes] * lanes_of(width, off)
            scores = matmul(keys, projt[lanes, :]) * score_scale
            scores = jnp.where(same, scores, -jnp.inf)
            scores = jnp.exp(scores - jnp.max(scores, axis=0, keepdims=True))
            share = scores * (1.0 / jnp.sum(scores, axis=0, keepdims=True))
            probs[g * 8 + h] = share
            part = matmul(projt[pl.ds(2 * D + rows, 80), :], share.astype(BF16))
            at[pl.ds(rows, 80), :] = part.astype(BF16)
            gap = jnp.zeros((8, 256), F32)
            padded = jnp.concatenate([part[0:40], gap, part[40:80], gap], axis=0).astype(BF16)
            atp[pl.ds(pl.multiple_of(g * 768 + h * 96, 16), 96), :] = padded

    attend(0)
    gather.q_along_x()
    attend(1)
    scatter = Scatter(
        at, bg, dw_ref, (at2, bg2, wsum, wb, xa, yb, sa, sb, wa2, wb2, ya, xb, zs, zr, s3), ssem, norm_scale
    )
    scatter.send_attended()
    exchange_wait(cslab, crecv, csend, crecvs)
    bg[...] = crecv[...].reshape(256, D)
    scatter.send_grad()
    gather.p_pair()
    for j in range(6):
        apad[:, pl.ds(j * 256, 256)] = matmul_t(eye[...], atp[pl.ds(j * 256, 256), :]).astype(BF16)
    scatter.product()

    gather.q_pair()
    gather.finish()
    for half in range(2):
        cols = pl.ds(half * HALF, HALF)
        branch = matmul(apad[...], wg[half].reshape(1536, HALF))
        block = (xp[:, cols].astype(F32) + branch).astype(BF16)
        tok[:, :, cols] = block.reshape(SEQ, GROUP, HALF)
    exchange_start(tok, got, tsend, trecvs)

    for i in range(4):
        part = matmul_t(wg[0, i // 2, pl.ds(2 * (i % 2), 2)].reshape(384, HALF), bg[:, pl.ds(0, HALF)])
        part += matmul_t(wg[1, i // 2, pl.ds(2 * (i % 2), 2)].reshape(384, HALF), bg[:, pl.ds(HALF, HALF)])
        for h in range(4):
            own = part[96 * h : 96 * h + 96]
            own = jnp.concatenate([own[0:40], own[48:88]], axis=0).astype(BF16)
            dat[pl.ds(i * 320 + 80 * h, 80), :] = own

    def back(g):
        for h in range(8):
            first, width, off = WINDOWS[h]
            lanes = pl.ds(pl.multiple_of(g * HALF + first, 128), width)
            rows = pl.multiple_of(g * HALF + h * 80, 16)
            values = kv[:, pl.ds(pl.multiple_of(D + g * HALF + first, 128), width)] * lanes_of(width, off)
            share = probs[g * 8 + h]
            gp = matmul(values, dat[lanes, :])
            delta = jnp.sum(gp * share, axis=0, keepdims=True)
            gs = (share * (gp - delta) * score_scale).astype(BF16)
            low = share.astype(BF16)
            gt[pl.ds(rows, 80), :] = matmul(projt[pl.ds(D + rows, 80), :], gs).astype(BF16)
            gt[pl.ds(D + rows, 80), :] = matmul_t(projt[pl.ds(rows, 80), :], gs).astype(BF16)
            gt[pl.ds(2 * D + rows, 80), :] = matmul_t(dat[pl.ds(rows, 80), :], low).astype(BF16)

    back(0)
    scatter.after_one()
    back(1)
    scatter.after_two()

    def standard_of(i):
        return matmul_t(eye[...], xp[:, pl.ds(pl.multiple_of(i * 256, 256), 256)])

    def sums(i, carry):
        return carry + jnp.sum(standard_of(i), axis=0, keepdims=True)

    mean = lax.fori_loop(0, 5, sums, jnp.zeros((1, 256), F32)) * (1.0 / D)

    def squares(i, carry):
        part = standard_of(i) - mean
        return carry + jnp.sum(part * part, axis=0, keepdims=True)

    inv = lax.rsqrt(lax.fori_loop(0, 5, squares, jnp.zeros((1, 256), F32)) * (1.0 / D) + eps)

    def grads(i, carry):
        rows = pl.ds(pl.multiple_of(i * 256, 256), 256)
        part = matmul(wqkv[rows, :], gt[...])
        std = (standard_of(i) - mean) * inv
        both = part * std
        hi = both.astype(BF16)
        rest = both - hi.astype(F32)
        mid = rest.astype(BF16)
        lo = (rest - mid.astype(F32)).astype(BF16)
        ones = jnp.ones((8, 256), BF16)
        row = matmul_t(ones, hi) + matmul_t(ones, mid) + matmul_t(ones, lo)
        ghold[2, :, rows] = row[0:1]
        scaled = part * gaincol_ref[rows, :]
        gn[rows, :] = scaled
        a, b = carry
        return (a + jnp.sum(scaled, axis=0, keepdims=True), b + jnp.sum(scaled * std, axis=0, keepdims=True))

    zero = jnp.zeros((1, 256), F32)
    mean_g, mean_gs = lax.fori_loop(0, 5, grads, (zero, zero))
    gains = GainSum(ghold, g1, g2, gsem)
    gains.first(ghold[2])
    scatter.after_z()
    mean_g = mean_g * (1.0 / D)
    mean_gs = mean_gs * (1.0 / D)

    @pl.loop(0, 5)
    def _(i):
        rows = pl.ds(pl.multiple_of(i * 256, 256), 256)
        std = (standard_of(i) - mean) * inv
        branch = inv * (gn[rows, :] - mean_g - std * mean_gs)
        total = (matmul_t(eye[...], bg[:, rows]) + branch).astype(BF16)
        gx_ref[:, rows] = matmul_t(permt[...], total).astype(BF16)

    gains.second()
    exchange_wait(tok, got, tsend, trecvs)

    def unshuffle(r, c):
        return r == lax.rem(c, 4) * 64 + lax.div(c, 4)

    unmix = one_hot(256, 256, unshuffle)
    ordered = matmul(unmix, got[...].reshape(256, D)).astype(BF16)
    for c in range(4):
        merged_ref[:, pl.ds(c * D, D)] = ordered[64 * c : 64 * c + 64]
    dg_ref[...] = gains.finish() * norm_scale
    scatter.finish()


def per_device(patches, lengths, token_dest, gain, w_qkv, w_out, cotangent):
    norm_scale = 1.0 / math.sqrt(256 * SEQ * NX)
    row = jnp.arange(256, dtype=jnp.int32)
    slot = jnp.repeat(token_dest[0] // 64, GROUP)
    key = slot * GROUP + row % GROUP
    ends = jnp.cumsum(lengths[0, 0] * GROUP)
    ids = jnp.sum((row[:, None] >= ends[None, :]).astype(jnp.int32), axis=1)
    rows = jnp.stack([key, ids])
    columns = jnp.stack([key, ids], axis=1)
    vmem = pl.BlockSpec(memory_space=pltpu.VMEM)
    hbm = pl.BlockSpec(memory_space=pl.ANY)

    def kernel(*refs):
        kernel_body(norm_scale, refs)

    merged, gx, dw, dg = pl.pallas_call(
        kernel,
        out_shape=(
            jax.ShapeDtypeStruct((SEQ, GROUP * D), BF16),
            jax.ShapeDtypeStruct((256, D), BF16),
            jax.ShapeDtypeStruct((2, 2, 16, HALF), F32),
            jax.ShapeDtypeStruct((1, D), F32),
        ),
        in_specs=[vmem] * 5 + [hbm] + [vmem] * 2,
        out_specs=(vmem,) * 4,
        scratch_shapes=[
            pltpu.VMEM((D, 3 * D), BF16),
            pltpu.VMEM((2, 32, D), BF16),
            pltpu.VMEM((2, 2, 4, NY, 48, HALF), BF16),
            pltpu.VMEM((SEQ, GROUP, D), BF16),
            pltpu.VMEM((SEQ, GROUP, D), BF16),
            pltpu.VMEM((SEQ, GROUP, D), BF16),
            pltpu.VMEM((SEQ, GROUP, D), BF16),
            pltpu.VMEM((256, D), BF16),
            pltpu.VMEM((256, D), BF16),
            pltpu.VMEM((256, 2 * D), BF16),
            pltpu.VMEM((3 * D, 256), BF16),
            pltpu.VMEM((256, 256), BF16),
            pltpu.VMEM((256, 256), BF16),
            pltpu.VMEM((256, 256), BF16),
            pltpu.VMEM((HEADS, 256, 256), F32),
            pltpu.VMEM((D, 256), BF16),
            pltpu.VMEM((1536, 256), BF16),
            pltpu.VMEM((256, 1536), BF16),
            pltpu.VMEM((256, D), BF16),
            pltpu.VMEM((D, 256), BF16),
            pltpu.VMEM((3 * D, 256), BF16),
            pltpu.VMEM((D, 256), F32),
            pltpu.VMEM((D, 256), BF16),
            pltpu.VMEM((256, HALF), BF16),
            pltpu.VMEM((NX, NY, 80, HALF), F32),
            pltpu.VMEM((NX, NY, 80, HALF), BF16),
            pltpu.VMEM((3, NY, 80, 384), BF16),
            pltpu.VMEM((3, NX, 80, 256), BF16),
            pltpu.VMEM((NY, 80, 384), F32),
            pltpu.VMEM((NX, 80, 256), F32),
            pltpu.VMEM((NY, 80, 384), BF16),
            pltpu.VMEM((NX, 80, 256), BF16),
            pltpu.VMEM((3, 80, 384), BF16),
            pltpu.VMEM((3, 80, 256), BF16),
            pltpu.VMEM((128, HALF), BF16),
            pltpu.VMEM((7, 16, HALF), BF16),
            pltpu.VMEM((16, HALF), F32),
            pltpu.VMEM((3, 1, D), F32),
            pltpu.VMEM((15, 1, D), F32),
            pltpu.VMEM((15, 1, D), F32),
            pltpu.SemaphoreType.DMA((3,)),
            pltpu.SemaphoreType.DMA((50,)),
            pltpu.SemaphoreType.DMA,
            pltpu.SemaphoreType.DMA,
            pltpu.SemaphoreType.DMA,
            pltpu.SemaphoreType.DMA,
            pltpu.SemaphoreType.DMA((47,)),
            pltpu.SemaphoreType.DMA((60,)),
        ],
        compiler_params=pltpu.CompilerParams(
            collective_id=0, has_side_effects=True, vmem_limit_bytes=LIMIT
        ),
    )(
        patches[0], rows, columns, gain.reshape(1, D), gain.reshape(D, 1), w_qkv, w_out,
        cotangent[0],
    )
    own_weight = jnp.transpose(dw[:, :, :10], (0, 2, 1, 3)).reshape(20, D)
    own_gain = lax.dynamic_slice_in_dim(dg.reshape(D), lax.axis_index("seq") * 20, 20, 0)
    return (merged[None], gx[None], own_weight, own_gain)


def solution(mesh):
    placed = (
        P("dp", "seq", None),
        P("dp", "seq", None),
        P("dp", "seq"),
        P(),
        P(),
        P("seq", None),
        P("dp", "seq", None),
    )
    return jax.shard_map(
        per_device,
        mesh=mesh,
        in_specs=placed,
        out_specs=(P("dp", "seq", None), P("dp", "seq", None), P("seq", None), P("seq")),
        check_vma=False,
    )
```

```python
import math

import jax
import jax.numpy as jnp
from jax import lax
from jax.experimental import pallas as pl
from jax.experimental.pallas import tpu as pltpu
from jax.sharding import PartitionSpec as P

HEADS = 16
GROUP = 4
D = 1280
HALF = 640
NZ, NY, NX = 8, 4, 4
SEQ = 64
LIMIT = 56 * 2**20

eps = 1e-06
F32 = jnp.float32
BF16 = jnp.bfloat16


def place():
    seq = lax.axis_index("seq")
    x = lax.axis_index("dp")
    return seq, x, lax.div(seq, 8), lax.rem(lax.div(seq, 2), 4), lax.rem(seq, 2)


def seq_of(z, y, core):
    return z * 8 + y * 2 + core


def dev(seq, x):
    return {"seq": seq, "dp": x}


def remote(src, dst, send, recv, seq, x):
    return pltpu.make_async_remote_copy(
        src_ref=src,
        dst_ref=dst,
        send_sem=send,
        recv_sem=recv,
        device_id=dev(seq, x),
        device_id_type=pl.DeviceIdType.MESH,
    )


def owner_of(x, y, z):
    return 16 * x + 4 * y + lax.div(z, 2)


def greet():
    seq, x, z, y, core = place()
    barrier = pltpu.get_barrier_semaphore()

    def signal(to, where):
        pl.semaphore_signal(barrier, inc=1, device_id=dev(to, where), device_id_type=pl.DeviceIdType.MESH)

    @pl.loop(1, SEQ)
    def _(k):
        signal(lax.rem(seq + k, SEQ), x)

    for kx in range(1, NX):
        for ky in range(NY):
            signal(seq_of(z, lax.rem(y + ky, NY), core), lax.rem(x + kx, NX))
        signal(owner_of(x, y, z), lax.rem(x + kx, NX))

    @pl.when(x != lax.div(seq, 16))
    def _():
        for part in range(2):
            for other in range(2):
                to = seq_of(2 * lax.rem(seq, 4) + part, lax.rem(lax.div(seq, 4), 4), other)
                signal(to, lax.div(seq, 16))


def all_here():
    seq, x, z, y, core = place()
    count = SEQ - 1 + 12 + 3 + jnp.where(x != lax.div(seq, 16), 4, 0)
    pl.semaphore_wait(pltpu.get_barrier_semaphore(), count)


def exchange_start(src, dst, send, recv):
    seq, x, z, y, core = place()

    @pl.loop(1, SEQ)
    def _(k):
        to = lax.rem(seq + k, SEQ)
        remote(src.at[to], dst.at[seq], send, recv, to, x).start()

    pltpu.make_async_copy(src.at[seq], dst.at[seq], recv).start()


def exchange_wait(src, dst, send, recv):
    pltpu.make_async_copy(dst, dst, recv).wait()
    part = src.at[pl.ds(0, SEQ - 1)]
    pltpu.make_async_copy(part, part, send).wait()


def matmul(a, b):
    return jnp.dot(a, b, preferred_element_type=F32)


def matmul_t(a, b):
    return lax.dot_general(a, b, (((1,), (1,)), ((), ())), preferred_element_type=F32)


def three_parts(a):
    hi = a.astype(BF16)
    rest = a - hi.astype(F32)
    mid = rest.astype(BF16)
    return hi, mid, (rest - mid.astype(F32)).astype(BF16)


def one_hot(rows, columns, want):
    r = lax.broadcasted_iota(jnp.int32, (rows, columns), 0)
    c = lax.broadcasted_iota(jnp.int32, (rows, columns), 1)
    return jnp.where(want(r, c), 1.0, 0.0).astype(BF16)


WINDOWS = []
for _h in range(8):
    _first = 80 * _h // 128 * 128
    _off = 80 * _h - _first
    WINDOWS.append((_first, 128 if _off + 80 <= 128 else 256, _off))


def lanes_of(width, offset):
    lane = lax.broadcasted_iota(jnp.int32, (1, width), 1)
    return jnp.where((lane >= offset) & (lane < offset + 80), 1.0, 0.0).astype(BF16)


class Gather:
    def __init__(self, w_ref, slots, wg, sems):
        self.w_ref, self.slots, self.wg, self.sems = w_ref, slots, wg, sems
        self.p, self.q = pl.ds(0, 256), pl.ds(256, 384)

    def pair(self):
        seq, x, z, y, core = place()
        slots, sems = self.slots, self.sems
        own = jnp.concatenate([self.w_ref[...].astype(F32), jnp.zeros((12, D), F32)], axis=0)
        slots[core] = own.astype(BF16)
        self.first = remote(slots.at[core], slots.at[core], sems.at[0], sems.at[1], seq_of(z, y, 1 - core), x)
        self.first.start()

    def along_z(self):
        seq, x, z, y, core = place()
        slots, sems, wg = self.slots, self.sems, self.wg
        zh, zl = lax.div(z, 4), lax.rem(z, 4)
        self.first.wait()

        def want(r, c):
            return (c == jnp.where(r < 20, r, r + 12)) & (r < 40)

        first = pl.multiple_of(core * HALF, 128)
        rows = jnp.concatenate([slots[0, :, pl.ds(first, HALF)], slots[1, :, pl.ds(first, HALF)]], axis=0)
        own = matmul(one_hot(48, 64, want), rows).astype(BF16)
        wg[core, zh, zl, y, :, self.p] = own[:, 0:256]

        @pl.when(zl == x)
        def _():
            wg[core, zh, zl, y, :, self.q] = own[:, 256:640]
            part = wg.at[core, zh, zl, y, :, self.q]
            for k in range(1, NZ):
                to = seq_of(lax.rem(z + k, NZ), y, core)
                remote(part, part, sems.at[1 + k], sems.at[9 + zh], to, x).start()

        self.pz = []
        part = wg.at[core, zh, zl, y, :, self.p]
        for k in range(1, NZ):
            to = seq_of(lax.rem(z + k, NZ), y, core)
            self.pz.append(remote(part, part, sems.at[10 + 2 * k], sems.at[11 + 2 * k], to, x))
        for one in self.pz:
            one.start()

    def q_along_y(self):
        seq, x, z, y, core = place()
        sems, wg = self.sems, self.wg
        for j in range(2):

            @pl.when(z != x + 4 * j)
            def _():
                part = wg.at[core, j, x, y, :, self.q]
                pltpu.make_async_copy(part, part, sems.at[9 + j]).wait()

        part = wg.at[core, :, x, y, :, self.q]
        self.qy = []
        for k in range(1, NY):
            to = seq_of(z, lax.rem(y + k, NY), core)
            self.qy.append(remote(part, part, sems.at[26 + 2 * k], sems.at[27 + 2 * k], to, x))
        for one in self.qy:
            one.start()

    def p_along_y(self):
        seq, x, z, y, core = place()
        sems, wg = self.sems, self.wg
        for one in self.pz:
            one.wait()
        part = wg.at[core, :, :, y, :, self.p]
        self.py = []
        for k in range(1, NY):
            to = seq_of(z, lax.rem(y + k, NY), core)
            self.py.append(remote(part, part, sems.at[32 + 2 * k], sems.at[33 + 2 * k], to, x))
        for one in self.py:
            one.start()

    def q_along_x(self):
        seq, x, z, y, core = place()
        sems, wg = self.sems, self.wg
        for one in self.qy:
            one.wait()
        part = wg.at[core, :, x, :, :, self.q]
        self.qx = []
        for k in range(1, NX):
            self.qx.append(
                remote(part, part, sems.at[38 + 2 * k], sems.at[39 + 2 * k], seq, lax.rem(x + k, NX))
            )
        for one in self.qx:
            one.start()

    def p_pair(self):
        seq, x, z, y, core = place()
        for one in self.py:
            one.wait()
        part = self.wg.at[core, :, :, :, :, self.p]
        self.pc = remote(part, part, self.sems.at[46], self.sems.at[47], seq_of(z, y, 1 - core), x)
        self.pc.start()

    def q_pair(self):
        seq, x, z, y, core = place()
        for one in self.qx:
            one.wait()
        part = self.wg.at[core, :, :, :, :, self.q]
        self.qc = remote(part, part, self.sems.at[48], self.sems.at[49], seq_of(z, y, 1 - core), x)
        self.qc.start()

    def finish(self):
        seq, x, z, y, core = place()
        self.pc.wait()
        self.qc.wait()

        @pl.when(lax.rem(z, 4) == x)
        def _():
            part = self.wg.at[core, 0, 0, 0, :, self.q]
            for k in range(1, NZ):
                pltpu.make_async_copy(part, part, self.sems.at[1 + k]).wait()


class Scatter:
    def __init__(self, at_ref, bg_ref, out, bufs, sems, norm_scale):
        self.at_ref, self.bg_ref, self.out, self.bufs, self.sems = at_ref, bg_ref, out, bufs, sems
        self.norm_scale = norm_scale
        self.a, self.b = pl.ds(0, 384), pl.ds(384, 256)

    def start(self):
        for one in self.now:
            one.start()

    def wait(self):
        for one in self.now:
            one.wait()

    def send_attended(self):
        seq, x, z, y, core = place()
        partner = seq_of(z, y, 1 - core)
        self.now = [remote(self.at_ref, self.bufs[0], self.sems.at[0], self.sems.at[1], partner, x)]
        self.now[0].start()

    def send_grad(self):
        seq, x, z, y, core = place()
        partner = seq_of(z, y, 1 - core)
        theirs = pl.multiple_of((1 - core) * HALF, 128)
        one = remote(
            self.bg_ref.at[:, pl.ds(theirs, HALF)], self.bufs[1], self.sems.at[2], self.sems.at[3], partner, x
        )
        one.start()
        self.now.append(one)

    def product(self):
        at2, bg2, wsum, wb, xa, yb, sa, sb, wa2, wb2, ya, xb, zs, zr, s3 = self.bufs
        seq, x, z, y, core = place()
        at_ref, bg_ref, sems = self.at_ref, self.bg_ref, self.sems
        mine = pl.multiple_of(core * HALF, 128)
        self.wait()

        @pl.loop(0, NX)
        def _(i):
            rows = pl.ds(pl.multiple_of(i * 320, 64), 320)
            part = matmul(at_ref[rows, :], bg_ref[:, pl.ds(mine, HALF)])
            part += matmul(at2[rows, :], bg2[...])
            part = part.reshape(NY, 80, HALF)
            wsum[i] = part
            wb[i] = part.astype(BF16)

        self.now = []
        for k in range(1, NX):
            to = lax.rem(x + k, NX)
            self.now.append(
                remote(wb.at[to, :, :, self.a], xa.at[k - 1], sems.at[2 + 2 * k], sems.at[3 + 2 * k], seq, to)
            )
            to = lax.rem(y + k, NY)
            self.now.append(
                remote(
                    wb.at[:, to, :, self.b], yb.at[k - 1], sems.at[8 + 2 * k], sems.at[9 + 2 * k],
                    seq_of(z, to, core), x,
                )
            )
        self.start()

    def after_one(self):
        at2, bg2, wsum, wb, xa, yb, sa, sb, wa2, wb2, ya, xb, zs, zr, s3 = self.bufs
        seq, x, z, y, core = place()
        sems = self.sems
        self.wait()

        @pl.loop(0, 4)
        def _(j):
            total = wsum[x, j, :, self.a]
            for k in range(3):
                total += xa[k, j].astype(F32)
            sa[j] = total
            wa2[j] = total.astype(BF16)
            total = wsum[j, y, :, self.b]
            for k in range(3):
                total += yb[k, j].astype(F32)
            sb[j] = total
            wb2[j] = total.astype(BF16)

        self.now = []
        for k in range(1, NY):
            to = lax.rem(y + k, NY)
            self.now.append(
                remote(wa2.at[to], ya.at[k - 1], sems.at[14 + 2 * k], sems.at[15 + 2 * k], seq_of(z, to, core), x)
            )
            to = lax.rem(x + k, NX)
            self.now.append(remote(wb2.at[to], xb.at[k - 1], sems.at[20 + 2 * k], sems.at[21 + 2 * k], seq, to))
        self.start()

    def after_two(self):
        at2, bg2, wsum, wb, xa, yb, sa, sb, wa2, wb2, ya, xb, zs, zr, s3 = self.bufs
        seq, x, z, y, core = place()
        sems = self.sems
        self.wait()
        total = sa[y]
        for k in range(3):
            total += ya[k].astype(F32)
        second = sb[x]
        for k in range(3):
            second += xb[k].astype(F32)

        def want(r, c):
            low = lax.rem(r, 16)
            return (c == lax.div(r, 16) * 10 + low) & (low < 10)

        chosen = one_hot(128, 80, want)
        zs[:, self.a] = matmul(chosen, total.astype(BF16)).astype(BF16)
        zs[:, self.b] = matmul(chosen, second.astype(BF16)).astype(BF16)
        self.now = []
        for k in range(1, NZ):
            to = lax.rem(z + k, NZ)
            src = zs.at[pl.ds(pl.multiple_of(to * 16, 16), 16)]
            self.now.append(
                remote(src, zr.at[k - 1], sems.at[26 + 2 * k], sems.at[27 + 2 * k], seq_of(to, y, core), x)
            )
        self.start()

    def after_z(self):
        zs, zr, s3 = self.bufs[-3:]
        seq, x, z, y, core = place()
        sems, out = self.sems, self.out
        self.wait()
        total = zs[pl.ds(pl.multiple_of(z * 16, 16), 16), :].astype(F32)
        for k in range(7):
            total += zr[k].astype(F32)
        s3[...] = total * self.norm_scale
        owner = owner_of(x, y, z)
        slot = out.at[lax.rem(z, 2), core]
        self.now = []
        for k in range(1, NX):
            self.now.append(remote(s3, slot, sems.at[41 + k], sems.at[46], owner, lax.rem(x + k, NX)))
        self.start()

        @pl.when(owner != seq)
        def _():
            remote(s3, slot, sems.at[45], sems.at[46], owner, x).start()

        @pl.when(owner == seq)
        def _():
            pltpu.make_async_copy(s3, slot, sems.at[46]).start()

    def finish(self):
        seq, x, z, y, core = place()
        sems, out, s3 = self.sems, self.out, self.bufs[-1]
        for one in self.now:
            one.wait_send()

        @pl.when(owner_of(x, y, z) != seq)
        def _():
            pltpu.make_async_copy(s3, s3, sems.at[45]).wait()

        pltpu.make_async_copy(out, out, sems.at[46]).wait()


class GainSum:
    def __init__(self, ghold, g1, g2, sems):
        self.ghold, self.g1, self.g2, self.sems = ghold, g1, g2, sems

    def first(self, total):
        seq, x, z, y, core = place()
        self.ghold[0] = total
        self.now = []
        for k in range(1, 16):
            kx, ky = k // 4, k % 4
            to = seq_of(z, lax.rem(y + ky, NY), core)
            self.now.append(
                remote(
                    self.ghold.at[0], self.g1.at[k - 1], self.sems.at[2 * k - 2], self.sems.at[2 * k - 1],
                    to, lax.rem(x + kx, NX),
                )
            )
        for one in self.now:
            one.start()

    def second(self):
        seq, x, z, y, core = place()
        for one in self.now:
            one.wait()
        total = self.ghold[0]
        for k in range(15):
            total += self.g1[k]
        self.ghold[1] = total
        self.now = []
        for k in range(1, 16):
            kz, kc = k // 2, k % 2
            to = seq_of(lax.rem(z + kz, NZ), y, lax.rem(core + kc, 2))
            self.now.append(
                remote(
                    self.ghold.at[1], self.g2.at[k - 1], self.sems.at[28 + 2 * k], self.sems.at[29 + 2 * k], to, x
                )
            )
        for one in self.now:
            one.start()

    def finish(self):
        for one in self.now:
            one.wait()
        total = self.ghold[1]
        for k in range(15):
            total += self.g2[k]
        return total


def kernel_body(norm_scale, refs):
    (x_ref, dest_ref, len_ref, gain_ref, wqkv_hbm, wout_ref, cot_ref,
     got, gx_ref, dw_ref, dg_ref,
     wqkv, slots, wg, cslab, crecv, tok, xp, normed, kv, projt, eye, perm, permt, probs, at, atp, apad, bg, dat, gt, gn,
     at2, bg2, wsum, wb, xa, yb, sa, sb, wa2, wb2, ya, xb, zs, zr, s3, ghold, g1, g2, gaincol,
     wsem, asem, csend, crecvs, tsend, trecvs, ssem, gsem) = refs
    score_scale = 1.0 / math.sqrt(80)

    loads = []
    for j in range(3):
        cols = pl.ds(j * D, D)
        loads.append(pltpu.make_async_copy(wqkv_hbm.at[:, cols], wqkv.at[:, cols], wsem.at[j]))
    for one in loads:
        one.start()

    greet()

    def shuffle(r, c):
        return c == lax.rem(r, 4) * 64 + lax.div(r, 4)

    stacked = jnp.concatenate([cot_ref[:, pl.ds(c * D, D)] for c in range(4)], axis=0)
    cslab[...] = matmul(one_hot(256, 256, shuffle), stacked).astype(BF16).reshape(SEQ, GROUP, D)
    all_here()
    gather = Gather(wout_ref, slots, wg, asem)
    gather.pair()

    slot = jnp.broadcast_to(lax.shift_right_logical(dest_ref[...], 6), (8, 64)).astype(F32).astype(BF16)
    to_row = matmul(slot, one_hot(64, 256, lambda r, c: r == lax.div(c, 4)))[0:1]
    to_col = matmul_t(one_hot(256, 64, lambda r, c: c == lax.div(r, 4)), slot)[:, 0:1]
    row_number = lax.broadcasted_iota(jnp.int32, (1, 256), 1)
    col_number = lax.broadcasted_iota(jnp.int32, (256, 1), 0)
    key_row = to_row.astype(jnp.int32) * GROUP + lax.rem(row_number, GROUP)
    key_col = to_col.astype(jnp.int32) * GROUP + lax.rem(col_number, GROUP)
    id_row, id_col = jnp.zeros((1, 256), F32), jnp.zeros((256, 1), F32)
    end = 0
    for j in range(3):
        end = end + len_ref[0, j] * GROUP
        id_row += jnp.where(row_number >= end, 1.0, 0.0)
        id_col += jnp.where(col_number >= end, 1.0, 0.0)
    ir = lax.broadcasted_iota(jnp.int32, (256, 256), 0)
    ic = lax.broadcasted_iota(jnp.int32, (256, 256), 1)
    eye[...] = jnp.where(ir == ic, 1.0, 0.0).astype(BF16)
    perm[...] = jnp.where(ir == key_row, 1.0, 0.0).astype(BF16)
    permt[...] = jnp.where(ic == key_col, 1.0, 0.0).astype(BF16)
    ids_k = jnp.sum(jnp.where(ir == key_row, id_row, 0.0), axis=1, keepdims=True)
    ids_q = jnp.sum(jnp.where(ic == key_col, id_col, 0.0), axis=0, keepdims=True)

    wide = matmul(perm[...], x_ref[...])
    xp[...] = wide.astype(BF16)
    centred = wide - jnp.mean(wide, axis=-1, keepdims=True)
    spread = lax.rsqrt(jnp.mean(centred * centred, axis=-1, keepdims=True) + eps)
    normed[...] = (centred * spread * gain_ref[...].reshape(1, D)).astype(BF16)
    gather.along_z()
    exchange_start(cslab, crecv, csend, crecvs)

    for j in range(3):
        loads[j].wait()
        if j == 2:
            gather.q_along_y()

        @pl.loop(0, 5)
        def _(i):
            cols = pl.ds(pl.multiple_of(j * D + i * 256, 256), 256)
            part = matmul(normed[...], wqkv[:, cols]).astype(BF16)
            if j > 0:
                kv[:, pl.ds(pl.multiple_of((j - 1) * D + i * 256, 256), 256)] = part
            projt[cols, :] = matmul_t(eye[...], part).astype(BF16)

    gather.p_along_y()
    same = ids_k == ids_q

    def attend(g):
        for h in range(8):
            first, width, off = WINDOWS[h]
            lanes = pl.ds(pl.multiple_of(g * HALF + first, 128), width)
            rows = pl.multiple_of(g * HALF + h * 80, 16)
            keys = kv[:, lanes] * lanes_of(width, off)
            scores = matmul(keys, projt[lanes, :]) * score_scale
            scores = jnp.where(same, scores, -jnp.inf)
            scores = jnp.exp(scores - jnp.max(scores, axis=0, keepdims=True))
            share = scores * (1.0 / jnp.sum(scores, axis=0, keepdims=True))
            probs[g * 8 + h] = share
            part = matmul(projt[pl.ds(2 * D + rows, 80), :], share.astype(BF16))
            at[pl.ds(rows, 80), :] = part.astype(BF16)
            gap = jnp.zeros((8, 256), F32)
            padded = jnp.concatenate([part[0:40], gap, part[40:80], gap], axis=0).astype(BF16)
            atp[pl.ds(pl.multiple_of(g * 768 + h * 96, 16), 96), :] = padded

    attend(0)
    gather.q_along_x()
    attend(1)
    scatter = Scatter(
        at, bg, dw_ref, (at2, bg2, wsum, wb, xa, yb, sa, sb, wa2, wb2, ya, xb, zs, zr, s3), ssem, norm_scale
    )
    scatter.send_attended()
    exchange_wait(cslab, crecv, csend, crecvs)
    bg[...] = crecv[...].reshape(256, D)
    scatter.send_grad()
    gather.p_pair()
    for j in range(6):
        apad[:, pl.ds(j * 256, 256)] = matmul_t(eye[...], atp[pl.ds(j * 256, 256), :]).astype(BF16)
    scatter.product()


    @pl.loop(0, 5)
    def _(i):
        rows = pl.ds(pl.multiple_of(i * 256, 256), 256)
        total = jnp.zeros((256, 256), F32)
        for part in three_parts(gain_ref[rows].reshape(1, 256)):
            total += matmul_t(eye[...], jnp.broadcast_to(part, (256, 256)))
        gaincol[rows, :] = total

    gather.q_pair()
    gather.finish()
    for half in range(2):
        cols = pl.ds(half * HALF, HALF)
        branch = matmul(apad[...], wg[half].reshape(1536, HALF))
        block = (xp[:, cols].astype(F32) + branch).astype(BF16)
        tok[:, :, cols] = block.reshape(SEQ, GROUP, HALF)
    exchange_start(tok, got, tsend, trecvs)

    for i in range(4):
        part = matmul_t(wg[0, i // 2, pl.ds(2 * (i % 2), 2)].reshape(384, HALF), bg[:, pl.ds(0, HALF)])
        part += matmul_t(wg[1, i // 2, pl.ds(2 * (i % 2), 2)].reshape(384, HALF), bg[:, pl.ds(HALF, HALF)])
        for h in range(4):
            own = part[96 * h : 96 * h + 96]
            own = jnp.concatenate([own[0:40], own[48:88]], axis=0).astype(BF16)
            dat[pl.ds(i * 320 + 80 * h, 80), :] = own

    def back(g):
        for h in range(8):
            first, width, off = WINDOWS[h]
            lanes = pl.ds(pl.multiple_of(g * HALF + first, 128), width)
            rows = pl.multiple_of(g * HALF + h * 80, 16)
            values = kv[:, pl.ds(pl.multiple_of(D + g * HALF + first, 128), width)] * lanes_of(width, off)
            share = probs[g * 8 + h]
            gp = matmul(values, dat[lanes, :])
            delta = jnp.sum(gp * share, axis=0, keepdims=True)
            gs = (share * (gp - delta) * score_scale).astype(BF16)
            low = share.astype(BF16)
            gt[pl.ds(rows, 80), :] = matmul(projt[pl.ds(D + rows, 80), :], gs).astype(BF16)
            gt[pl.ds(D + rows, 80), :] = matmul_t(projt[pl.ds(rows, 80), :], gs).astype(BF16)
            gt[pl.ds(2 * D + rows, 80), :] = matmul_t(dat[pl.ds(rows, 80), :], low).astype(BF16)

    back(0)
    scatter.after_one()
    back(1)
    scatter.after_two()

    def standard_of(i):
        return matmul_t(eye[...], xp[:, pl.ds(pl.multiple_of(i * 256, 256), 256)])

    def sums(i, carry):
        return carry + jnp.sum(standard_of(i), axis=0, keepdims=True)

    mean = lax.fori_loop(0, 5, sums, jnp.zeros((1, 256), F32)) * (1.0 / D)

    def squares(i, carry):
        part = standard_of(i) - mean
        return carry + jnp.sum(part * part, axis=0, keepdims=True)

    inv = lax.rsqrt(lax.fori_loop(0, 5, squares, jnp.zeros((1, 256), F32)) * (1.0 / D) + eps)

    def grads(i, carry):
        rows = pl.ds(pl.multiple_of(i * 256, 256), 256)
        part = matmul(wqkv[rows, :], gt[...])
        std = (standard_of(i) - mean) * inv
        both = part * std
        ones = jnp.ones((8, 256), BF16)
        hi, mid, lo = three_parts(both)
        row = matmul_t(ones, hi) + matmul_t(ones, mid) + matmul_t(ones, lo)
        ghold[2, :, rows] = row[0:1]
        scaled = part * gaincol[rows, :]
        gn[rows, :] = scaled
        a, b = carry
        return (a + jnp.sum(scaled, axis=0, keepdims=True), b + jnp.sum(scaled * std, axis=0, keepdims=True))

    zero = jnp.zeros((1, 256), F32)
    mean_g, mean_gs = lax.fori_loop(0, 5, grads, (zero, zero))
    gains = GainSum(ghold, g1, g2, gsem)
    gains.first(ghold[2])
    scatter.after_z()
    mean_g = mean_g * (1.0 / D)
    mean_gs = mean_gs * (1.0 / D)

    @pl.loop(0, 5)
    def _(i):
        rows = pl.ds(pl.multiple_of(i * 256, 256), 256)
        std = (standard_of(i) - mean) * inv
        branch = inv * (gn[rows, :] - mean_g - std * mean_gs)
        total = (matmul_t(eye[...], bg[:, rows]) + branch).astype(BF16)
        gx_ref[:, rows] = matmul_t(permt[...], total).astype(BF16)

    gains.second()
    exchange_wait(tok, got, tsend, trecvs)

    dg_ref[...] = gains.finish() * norm_scale
    scatter.finish()


def finish_kernel(got_ref, gx_in, dw_ref, dg_ref, merged_ref, gx_ref, own_ref, gain_out):
    ordered = matmul(
        one_hot(256, 256, lambda r, c: r == lax.rem(c, 4) * 64 + lax.div(c, 4)), got_ref[...].reshape(256, D)
    ).astype(BF16)
    for c in range(4):
        merged_ref[:, pl.ds(c * D, D)] = ordered[64 * c : 64 * c + 64]
    gx_ref[...] = gx_in[...]
    for part in range(2):
        for core in range(2):
            own_ref[pl.ds(10 * part, 10), pl.ds(core * HALF, HALF)] = dw_ref[part, core, 0:10, :]
    first = lax.axis_index("seq") * 20
    turned = pltpu.roll(jnp.broadcast_to(dg_ref[...], (8, D)), lax.rem(D - first, D), 1)
    gain_out[...] = turned[0, 0:20]


def per_device(patches, lengths, token_dest, gain, w_qkv, w_out, cotangent):
    norm_scale = 1.0 / math.sqrt(256 * SEQ * NX)
    vmem = pl.BlockSpec(memory_space=pltpu.VMEM)
    hbm = pl.BlockSpec(memory_space=pl.ANY)
    smem = pl.BlockSpec(memory_space=pltpu.SMEM)

    def kernel(*refs):
        kernel_body(norm_scale, refs)

    got, gx, dw, dg = pl.pallas_call(
        kernel,
        out_shape=(
            jax.ShapeDtypeStruct((SEQ, GROUP, D), BF16),
            jax.ShapeDtypeStruct((256, D), BF16),
            jax.ShapeDtypeStruct((2, 2, 16, HALF), F32),
            jax.ShapeDtypeStruct((1, D), F32),
        ),
        in_specs=[vmem, vmem, smem, vmem, hbm, vmem, vmem],
        out_specs=(vmem,) * 4,
        scratch_shapes=[
            pltpu.VMEM((D, 3 * D), BF16),
            pltpu.VMEM((2, 32, D), BF16),
            pltpu.VMEM((2, 2, 4, NY, 48, HALF), BF16),
            pltpu.VMEM((SEQ, GROUP, D), BF16),
            pltpu.VMEM((SEQ, GROUP, D), BF16),
            pltpu.VMEM((SEQ, GROUP, D), BF16),
            pltpu.VMEM((256, D), BF16),
            pltpu.VMEM((256, D), BF16),
            pltpu.VMEM((256, 2 * D), BF16),
            pltpu.VMEM((3 * D, 256), BF16),
            pltpu.VMEM((256, 256), BF16),
            pltpu.VMEM((256, 256), BF16),
            pltpu.VMEM((256, 256), BF16),
            pltpu.VMEM((HEADS, 256, 256), F32),
            pltpu.VMEM((D, 256), BF16),
            pltpu.VMEM((1536, 256), BF16),
            pltpu.VMEM((256, 1536), BF16),
            pltpu.VMEM((256, D), BF16),
            pltpu.VMEM((D, 256), BF16),
            pltpu.VMEM((3 * D, 256), BF16),
            pltpu.VMEM((D, 256), F32),
            pltpu.VMEM((D, 256), BF16),
            pltpu.VMEM((256, HALF), BF16),
            pltpu.VMEM((NX, NY, 80, HALF), F32),
            pltpu.VMEM((NX, NY, 80, HALF), BF16),
            pltpu.VMEM((3, NY, 80, 384), BF16),
            pltpu.VMEM((3, NX, 80, 256), BF16),
            pltpu.VMEM((NY, 80, 384), F32),
            pltpu.VMEM((NX, 80, 256), F32),
            pltpu.VMEM((NY, 80, 384), BF16),
            pltpu.VMEM((NX, 80, 256), BF16),
            pltpu.VMEM((3, 80, 384), BF16),
            pltpu.VMEM((3, 80, 256), BF16),
            pltpu.VMEM((128, HALF), BF16),
            pltpu.VMEM((7, 16, HALF), BF16),
            pltpu.VMEM((16, HALF), F32),
            pltpu.VMEM((3, 1, D), F32),
            pltpu.VMEM((15, 1, D), F32),
            pltpu.VMEM((15, 1, D), F32),
            pltpu.VMEM((D, 256), F32),
            pltpu.SemaphoreType.DMA((3,)),
            pltpu.SemaphoreType.DMA((50,)),
            pltpu.SemaphoreType.DMA,
            pltpu.SemaphoreType.DMA,
            pltpu.SemaphoreType.DMA,
            pltpu.SemaphoreType.DMA,
            pltpu.SemaphoreType.DMA((47,)),
            pltpu.SemaphoreType.DMA((60,)),
        ],
        compiler_params=pltpu.CompilerParams(
            collective_id=0, has_side_effects=True, vmem_limit_bytes=LIMIT
        ),
    )(
        patches[0], token_dest, lengths[0], gain, w_qkv, w_out, cotangent[0],
    )
    merged, gx, own_weight, own_gain = pl.pallas_call(
        finish_kernel,
        out_shape=(
            jax.ShapeDtypeStruct((SEQ, GROUP * D), BF16),
            jax.ShapeDtypeStruct((256, D), BF16),
            jax.ShapeDtypeStruct((20, D), F32),
            jax.ShapeDtypeStruct((20,), F32),
        ),
        in_specs=[vmem] * 4,
        out_specs=(vmem,) * 4,
        compiler_params=pltpu.CompilerParams(vmem_limit_bytes=2**24),
    )(got, gx, dw, dg)
    return (merged[None], gx[None], own_weight, own_gain)


def solution(mesh):
    placed = (
        P("dp", "seq", None),
        P("dp", "seq", None),
        P("dp", "seq"),
        P(),
        P(),
        P("seq", None),
        P("dp", "seq", None),
    )
    return jax.shard_map(
        per_device,
        mesh=mesh,
        in_specs=placed,
        out_specs=(P("dp", "seq", None), P("dp", "seq", None), P("seq", None), P("seq")),
        check_vma=False,
    )
```

```python
import math

import jax
import jax.numpy as jnp
from jax import lax
from jax.experimental import pallas as pl
from jax.experimental.pallas import tpu as pltpu
from jax.sharding import PartitionSpec as P

HEADS = 16
GROUP = 4
D = 1280
HALF = 640
NZ, NY, NX = 8, 4, 4
SEQ = 64
LIMIT = 56 * 2**20

eps = 1e-06
F32 = jnp.float32
BF16 = jnp.bfloat16


def place():
    seq = lax.axis_index("seq")
    x = lax.axis_index("dp")
    return seq, x, lax.div(seq, 8), lax.rem(lax.div(seq, 2), 4), lax.rem(seq, 2)


def seq_of(z, y, core):
    return z * 8 + y * 2 + core


def dev(seq, x):
    return {"seq": seq, "dp": x}


def remote(src, dst, send, recv, seq, x):
    return pltpu.make_async_remote_copy(
        src_ref=src,
        dst_ref=dst,
        send_sem=send,
        recv_sem=recv,
        device_id=dev(seq, x),
        device_id_type=pl.DeviceIdType.MESH,
    )


def owner_of(x, y, z):
    return 16 * x + 4 * y + lax.div(z, 2)


def greet():
    seq, x, z, y, core = place()
    barrier = pltpu.get_barrier_semaphore()

    def signal(to, where):
        pl.semaphore_signal(barrier, inc=1, device_id=dev(to, where), device_id_type=pl.DeviceIdType.MESH)

    @pl.loop(1, SEQ)
    def _(k):
        signal(lax.rem(seq + k, SEQ), x)

    for kx in range(1, NX):
        for ky in range(NY):
            signal(seq_of(z, lax.rem(y + ky, NY), core), lax.rem(x + kx, NX))
        signal(owner_of(x, y, z), lax.rem(x + kx, NX))

    @pl.when(x != lax.div(seq, 16))
    def _():
        for part in range(2):
            for other in range(2):
                to = seq_of(2 * lax.rem(seq, 4) + part, lax.rem(lax.div(seq, 4), 4), other)
                signal(to, lax.div(seq, 16))


def all_here():
    seq, x, z, y, core = place()
    count = SEQ - 1 + 12 + 3 + jnp.where(x != lax.div(seq, 16), 4, 0)
    pl.semaphore_wait(pltpu.get_barrier_semaphore(), count)


def exchange_start(src, dst, send, recv):
    seq, x, z, y, core = place()

    @pl.loop(1, SEQ)
    def _(k):
        to = lax.rem(seq + k, SEQ)
        remote(src.at[to], dst.at[seq], send, recv, to, x).start()

    pltpu.make_async_copy(src.at[seq], dst.at[seq], recv).start()


def exchange_wait(src, dst, send, recv):
    pltpu.make_async_copy(dst, dst, recv).wait()
    part = src.at[pl.ds(0, SEQ - 1)]
    pltpu.make_async_copy(part, part, send).wait()


def matmul(a, b):
    return jnp.dot(a, b, preferred_element_type=F32)


def matmul_t(a, b):
    return lax.dot_general(a, b, (((1,), (1,)), ((), ())), preferred_element_type=F32)


class Pool:
    def __init__(self, sems):
        self.sems, self.used = sems, 0

    def take(self):
        self.used += 1
        return self.sems.at[self.used - 1]


def one_hot(rows, columns, want):
    r = lax.broadcasted_iota(jnp.int32, (rows, columns), 0)
    c = lax.broadcasted_iota(jnp.int32, (rows, columns), 1)
    return jnp.where(want(r, c), 1.0, 0.0).astype(BF16)


WINDOWS = []
for _h in range(8):
    _first = 80 * _h // 128 * 128
    _off = 80 * _h - _first
    WINDOWS.append((_first, 128 if _off + 80 <= 128 else 256, _off))


def lanes_of(width, offset):
    lane = lax.broadcasted_iota(jnp.int32, (1, width), 1)
    return jnp.where((lane >= offset) & (lane < offset + 80), 1.0, 0.0).astype(BF16)


class Gather:
    def __init__(self, w_ref, slots, wg, sems):
        self.w_ref, self.slots, self.wg = w_ref, slots, wg
        self.pool = Pool(sems)
        self.p, self.q = pl.ds(0, 256), pl.ds(256, 384)

    def send(self, part, to, x):
        one = remote(part, part, self.pool.take(), self.pool.take(), to, x)
        one.start()
        return one

    def pair(self):
        seq, x, z, y, core = place()
        slots = self.slots
        own = jnp.concatenate([self.w_ref[...].astype(F32), jnp.zeros((12, D), F32)], axis=0)
        slots[core] = own.astype(BF16)
        self.first = self.send(slots.at[core], seq_of(z, y, 1 - core), x)

    def along_z(self):
        seq, x, z, y, core = place()
        slots, wg = self.slots, self.wg
        zh, zl = lax.div(z, 4), lax.rem(z, 4)
        self.first.wait()

        def want(r, c):
            return (c == jnp.where(r < 20, r, r + 12)) & (r < 40)

        first = pl.multiple_of(core * HALF, 128)
        rows = jnp.concatenate([slots[0, :, pl.ds(first, HALF)], slots[1, :, pl.ds(first, HALF)]], axis=0)
        own = matmul(one_hot(48, 64, want), rows).astype(BF16)
        wg[core, zh, zl, y, :, self.p] = own[:, 0:256]
        self.zsend = [self.pool.take() for _ in range(1, NZ)]
        both = self.pool.used
        self.zrecv = [self.pool.take() for _ in range(2)]

        @pl.when(zl == x)
        def _():
            wg[core, zh, zl, y, :, self.q] = own[:, 256:640]
            part = wg.at[core, zh, zl, y, :, self.q]
            for k in range(1, NZ):
                to = seq_of(lax.rem(z + k, NZ), y, core)
                remote(part, part, self.zsend[k - 1], self.pool.sems.at[both + zh], to, x).start()

        part = wg.at[core, zh, zl, y, :, self.p]
        self.pz = [self.send(part, seq_of(lax.rem(z + k, NZ), y, core), x) for k in range(1, NZ)]

    def q_forward(self, k):
        seq, x, z, y, core = place()
        part = self.wg.at[core, :, x, lax.rem(y + NY - k, NY), :, self.q]
        self.qx.append([self.send(part, seq, lax.rem(x + j, NX)) for j in range(1, NX)])

    def q_along_y(self):
        seq, x, z, y, core = place()
        wg = self.wg
        for j in range(2):

            @pl.when(z != x + 4 * j)
            def _():
                part = wg.at[core, j, x, y, :, self.q]
                pltpu.make_async_copy(part, part, self.zrecv[j]).wait()

        part = wg.at[core, :, x, y, :, self.q]
        self.qy = [self.send(part, seq_of(z, lax.rem(y + k, NY), core), x) for k in range(1, NY)]
        self.qx = []
        self.q_forward(0)

    def p_to_pair(self, k):
        seq, x, z, y, core = place()
        part = self.wg.at[core, :, :, lax.rem(y + NY - k, NY), :, self.p]
        self.last.append(self.send(part, seq_of(z, y, 1 - core), x))

    def p_along_y(self):
        seq, x, z, y, core = place()
        for one in self.pz:
            one.wait()
        part = self.wg.at[core, :, :, y, :, self.p]
        self.py = [self.send(part, seq_of(z, lax.rem(y + k, NY), core), x) for k in range(1, NY)]
        self.last = []
        self.p_to_pair(0)

    def q_along_x(self):
        for k in range(1, NY):
            self.qy[k - 1].wait()
            self.q_forward(k)

    def p_pair(self):
        for k in range(1, NY):
            self.py[k - 1].wait()
            self.p_to_pair(k)

    def q_pair(self):
        seq, x, z, y, core = place()
        for k in range(NY):
            for one in self.qx[k]:
                one.wait()
            part = self.wg.at[core, :, :, lax.rem(y + NY - k, NY), :, self.q]
            self.last.append(self.send(part, seq_of(z, y, 1 - core), x))

    def finish(self):
        seq, x, z, y, core = place()
        for one in self.last:
            one.wait()

        @pl.when(lax.rem(z, 4) == x)
        def _():
            part = self.wg.at[core, 0, 0, 0, :, self.q]
            for k in range(1, NZ):
                pltpu.make_async_copy(part, part, self.zsend[k - 1]).wait()


class Scatter:
    def __init__(self, at_ref, bg_ref, out, bufs, sems, norm_scale):
        self.at_ref, self.bg_ref, self.out, self.bufs, self.sems = at_ref, bg_ref, out, bufs, sems
        self.pool = Pool(sems)
        self.norm_scale = norm_scale
        self.a, self.b = pl.ds(0, 384), pl.ds(384, 256)

    def wait(self):
        for one in self.now:
            one.wait()

    def send(self, src, dst, to, x):
        one = remote(src, dst, self.pool.take(), self.pool.take(), to, x)
        one.start()
        return one

    def send_attended(self):
        seq, x, z, y, core = place()
        at = self.at_ref
        self.now = [self.send(at.at[:, pl.ds(0, 256)], at.at[:, pl.ds(256, 256)], seq_of(z, y, 1 - core), x)]

    def send_grad(self):
        seq, x, z, y, core = place()
        pair = self.bufs[0]
        theirs = pl.multiple_of((1 - core) * HALF, 128)
        src = self.bg_ref.at[:, pl.ds(theirs, HALF)]
        self.now.append(self.send(src, pair.at[pl.ds(256, 256)], seq_of(z, y, 1 - core), x))
        pair[pl.ds(0, 256), :] = self.bg_ref[:, pl.ds(pl.multiple_of(core * HALF, 128), HALF)]

    def product(self):
        pair, wsum, wb, xa, yb, sa, sb, wa2, wb2, ya, xb, zs, zr, s3 = self.bufs
        seq, x, z, y, core = place()
        self.wait()
        self.now = []
        for k in (1, 2, 3, 0):
            i = lax.rem(x + k, NX)
            rows = pl.ds(pl.multiple_of(i * 320, 64), 320)
            part = matmul(self.at_ref[rows, :], pair[...]).reshape(NY, 80, HALF)
            wsum[i] = part
            wb[i] = part.astype(BF16)
            if k > 0:
                self.now.append(self.send(wb.at[i, :, :, self.a], xa.at[k - 1], seq, i))
            for j in range(1, NY):
                to = lax.rem(y + j, NY)
                self.now.append(self.send(wb.at[i, to, :, self.b], yb.at[j - 1, i], seq_of(z, to, core), x))

    def after_one(self):
        pair, wsum, wb, xa, yb, sa, sb, wa2, wb2, ya, xb, zs, zr, s3 = self.bufs
        seq, x, z, y, core = place()
        self.wait()

        @pl.loop(0, 4)
        def _(j):
            total = wsum[x, j, :, self.a]
            for k in range(3):
                total += xa[k, j].astype(F32)
            sa[j] = total
            wa2[j] = total.astype(BF16)
            total = wsum[j, y, :, self.b]
            for k in range(3):
                total += yb[k, j].astype(F32)
            sb[j] = total
            wb2[j] = total.astype(BF16)

        self.now = []
        for k in range(1, NY):
            to = lax.rem(y + k, NY)
            self.now.append(self.send(wa2.at[to], ya.at[k - 1], seq_of(z, to, core), x))
            to = lax.rem(x + k, NX)
            self.now.append(self.send(wb2.at[to], xb.at[k - 1], seq, to))

    def after_two(self):
        pair, wsum, wb, xa, yb, sa, sb, wa2, wb2, ya, xb, zs, zr, s3 = self.bufs
        seq, x, z, y, core = place()
        self.wait()
        total = sa[y]
        for k in range(3):
            total += ya[k].astype(F32)
        second = sb[x]
        for k in range(3):
            second += xb[k].astype(F32)

        def want(r, c):
            low = lax.rem(r, 16)
            return (c == lax.div(r, 16) * 10 + low) & (low < 10)

        chosen = one_hot(128, 80, want)
        zs[:, self.a] = matmul(chosen, total.astype(BF16)).astype(BF16)
        zs[:, self.b] = matmul(chosen, second.astype(BF16)).astype(BF16)
        self.now = []
        for k in range(1, NZ):
            to = lax.rem(z + k, NZ)
            src = zs.at[pl.ds(pl.multiple_of(to * 16, 16), 16)]
            self.now.append(self.send(src, zr.at[k - 1], seq_of(to, y, core), x))

    def after_z(self):
        zs, zr, s3 = self.bufs[-3:]
        seq, x, z, y, core = place()
        out = self.out
        self.wait()
        total = zs[pl.ds(pl.multiple_of(z * 16, 16), 16), :].astype(F32)
        for k in range(7):
            total += zr[k].astype(F32)
        s3[...] = total * self.norm_scale
        owner = owner_of(x, y, z)
        slot = out.at[lax.rem(z, 2), core]
        self.sent, self.got = self.pool.take(), self.pool.take()
        self.now = [
            remote(s3, slot, self.pool.take(), self.got, owner, lax.rem(x + k, NX)) for k in range(1, NX)
        ]
        for one in self.now:
            one.start()

        @pl.when(owner != seq)
        def _():
            remote(s3, slot, self.sent, self.got, owner, x).start()

        @pl.when(owner == seq)
        def _():
            pltpu.make_async_copy(s3, slot, self.got).start()

    def finish(self):
        seq, x, z, y, core = place()
        out, s3 = self.out, self.bufs[-1]
        for one in self.now:
            one.wait_send()

        @pl.when(owner_of(x, y, z) != seq)
        def _():
            pltpu.make_async_copy(s3, s3, self.sent).wait()

        pltpu.make_async_copy(out, out, self.got).wait()


class GainSum:
    def __init__(self, ghold, g1, g2, sems):
        self.ghold, self.g1, self.g2, self.sems = ghold, g1, g2, sems

    def first(self, total):
        seq, x, z, y, core = place()
        self.ghold[0] = total
        self.now = []
        for k in range(1, 16):
            kx, ky = k // 4, k % 4
            to = seq_of(z, lax.rem(y + ky, NY), core)
            self.now.append(
                remote(
                    self.ghold.at[0], self.g1.at[k - 1], self.sems.at[2 * k - 2], self.sems.at[2 * k - 1],
                    to, lax.rem(x + kx, NX),
                )
            )
        for one in self.now:
            one.start()

    def second(self):
        seq, x, z, y, core = place()
        for one in self.now:
            one.wait()
        total = self.ghold[0]
        for k in range(15):
            total += self.g1[k]
        self.ghold[1] = total
        self.now = []
        for k in range(1, 16):
            kz, kc = k // 2, k % 2
            to = seq_of(lax.rem(z + kz, NZ), y, lax.rem(core + kc, 2))
            self.now.append(
                remote(
                    self.ghold.at[1], self.g2.at[k - 1], self.sems.at[28 + 2 * k], self.sems.at[29 + 2 * k], to, x
                )
            )
        for one in self.now:
            one.start()

    def finish(self):
        for one in self.now:
            one.wait()
        total = self.ghold[1]
        for k in range(15):
            total += self.g2[k]
        return total


def kernel_body(norm_scale, refs):
    (x_ref, dest_ref, len_ref, gain_ref, wqkv_hbm, wout_ref, cot_ref,
     got, gx_ref, dw_ref, dg_ref,
     wqkv, slots, wg, cslab, crecv, tok, xp, normed, kv, projt, permt, probs, at, atp, apad, bg, bgt, dat, gt, gn, std, pair,
     wsum, wb, xa, yb, sa, sb, wa2, wb2, ya, xb, zs, zr, s3, ghold, g1, g2, gaincol,
     wsem, asem, csend, crecvs, tsend, trecvs, ssem, gsem) = refs
    score_scale = 1.0 / math.sqrt(80)

    loads = []
    for j in range(3):
        cols = pl.ds(j * D, D)
        loads.append(pltpu.make_async_copy(wqkv_hbm.at[:, cols], wqkv.at[:, cols], wsem.at[j]))
    for one in loads:
        one.start()

    greet()

    def shuffle(r, c):
        return c == lax.rem(r, 4) * 64 + lax.div(r, 4)

    stacked = jnp.concatenate([cot_ref[:, pl.ds(c * D, D)] for c in range(4)], axis=0)
    cslab[...] = matmul(one_hot(256, 256, shuffle), stacked).astype(BF16).reshape(SEQ, GROUP, D)
    slot = jnp.broadcast_to(lax.shift_right_logical(dest_ref[...], 6), (8, 64)).astype(F32).astype(BF16)
    to_row = matmul(slot, one_hot(64, 256, lambda r, c: r == lax.div(c, 4)))[0:1]
    to_col = matmul_t(one_hot(256, 64, lambda r, c: c == lax.div(r, 4)), slot)[:, 0:1]
    row_number = lax.broadcasted_iota(jnp.int32, (1, 256), 1)
    col_number = lax.broadcasted_iota(jnp.int32, (256, 1), 0)
    key_row = to_row.astype(jnp.int32) * GROUP + lax.rem(row_number, GROUP)
    key_col = to_col.astype(jnp.int32) * GROUP + lax.rem(col_number, GROUP)
    id_row, id_col = jnp.zeros((1, 256), F32), jnp.zeros((256, 1), F32)
    end = 0
    for j in range(3):
        end = end + len_ref[0, j] * GROUP
        id_row += jnp.where(row_number >= end, 1.0, 0.0)
        id_col += jnp.where(col_number >= end, 1.0, 0.0)
    ir = lax.broadcasted_iota(jnp.int32, (256, 256), 0)
    ic = lax.broadcasted_iota(jnp.int32, (256, 256), 1)
    perm = jnp.where(ir == key_row, 1.0, 0.0).astype(BF16)
    permt[...] = jnp.where(ic == key_col, 1.0, 0.0).astype(BF16)
    ids_k = jnp.sum(jnp.where(ir == key_row, id_row, 0.0), axis=1, keepdims=True)
    ids_q = jnp.sum(jnp.where(ic == key_col, id_col, 0.0), axis=0, keepdims=True)

    wide = matmul(perm, x_ref[...])
    xp[...] = wide.astype(BF16)
    centred = wide - jnp.mean(wide, axis=-1, keepdims=True)
    spread = lax.rsqrt(jnp.mean(centred * centred, axis=-1, keepdims=True) + eps)
    normed[...] = (centred * spread * gain_ref[...].reshape(1, D)).astype(BF16)

    all_here()
    gather = Gather(wout_ref, slots, wg, asem)
    gather.pair()

    def project(j):
        loads[j].wait()
        cols = pl.ds(j * D, D)
        part = matmul(normed[...], wqkv[:, cols]).astype(BF16)
        if j > 0:
            kv[:, pl.ds((j - 1) * D, D)] = part
        projt[cols, :] = part.T

    project(0)
    gather.along_z()
    exchange_start(cslab, crecv, csend, crecvs)
    project(1)
    project(2)
    gather.q_along_y()
    gather.p_along_y()
    same = ids_k == ids_q

    def attend(g):
        for h in range(8):
            first, width, off = WINDOWS[h]
            lanes = pl.ds(pl.multiple_of(g * HALF + first, 128), width)
            rows = pl.multiple_of(g * HALF + h * 80, 16)
            keys = kv[:, lanes] * lanes_of(width, off)
            scores = matmul(keys, projt[lanes, :]) * score_scale
            scores = jnp.where(same, scores, -jnp.inf)
            scores = jnp.exp(scores - jnp.max(scores, axis=0, keepdims=True))
            share = scores * (1.0 / jnp.sum(scores, axis=0, keepdims=True))
            probs[g * 8 + h] = share
            part = matmul(projt[pl.ds(2 * D + rows, 80), :], share.astype(BF16))
            at[pl.ds(rows, 80), pl.ds(0, 256)] = part.astype(BF16)
            gap = jnp.zeros((8, 256), F32)
            padded = jnp.concatenate([part[0:40], gap, part[40:80], gap], axis=0).astype(BF16)
            atp[pl.ds(pl.multiple_of(g * 768 + h * 96, 16), 96), :] = padded

    attend(0)
    gather.q_along_x()
    attend(1)
    scatter = Scatter(
        at, bg, dw_ref, (pair, wsum, wb, xa, yb, sa, sb, wa2, wb2, ya, xb, zs, zr, s3), ssem, norm_scale
    )
    scatter.send_attended()

    across = xp[...].T.astype(F32)
    across = across - jnp.mean(across, axis=0, keepdims=True)
    inv = lax.rsqrt(jnp.mean(across * across, axis=0, keepdims=True) + eps)
    std[...] = across * inv
    column = jnp.broadcast_to(gain_ref[...].reshape(1, D), (128, D)).T
    gaincol[:, 0:128] = column
    gaincol[:, 128:256] = column
    apad[...] = atp[...].T
    gather.p_pair()
    exchange_wait(cslab, crecv, csend, crecvs)
    bg[...] = crecv[...].reshape(256, D)
    scatter.send_grad()
    bgt[...] = bg[...].T
    scatter.product()
    gather.q_pair()
    gather.finish()
    for half in range(2):
        cols = pl.ds(half * HALF, HALF)
        branch = matmul(apad[...], wg[half].reshape(1536, HALF))
        block = (xp[:, cols].astype(F32) + branch).astype(BF16)
        tok[:, :, cols] = block.reshape(SEQ, GROUP, HALF)
    exchange_start(tok, got, tsend, trecvs)

    for i in range(4):
        part = matmul_t(wg[0, i // 2, pl.ds(2 * (i % 2), 2)].reshape(384, HALF), bg[:, pl.ds(0, HALF)])
        part += matmul_t(wg[1, i // 2, pl.ds(2 * (i % 2), 2)].reshape(384, HALF), bg[:, pl.ds(HALF, HALF)])
        for h in range(4):
            own = part[96 * h : 96 * h + 96]
            own = jnp.concatenate([own[0:40], own[48:88]], axis=0).astype(BF16)
            dat[pl.ds(i * 320 + 80 * h, 80), :] = own

    def back(g):
        for h in range(8):
            first, width, off = WINDOWS[h]
            lanes = pl.ds(pl.multiple_of(g * HALF + first, 128), width)
            rows = pl.multiple_of(g * HALF + h * 80, 16)
            values = kv[:, pl.ds(pl.multiple_of(D + g * HALF + first, 128), width)] * lanes_of(width, off)
            share = probs[g * 8 + h]
            gp = matmul(values, dat[lanes, :])
            delta = jnp.sum(gp * share, axis=0, keepdims=True)
            gs = (share * (gp - delta) * score_scale).astype(BF16)
            low = share.astype(BF16)
            gt[pl.ds(rows, 80), :] = matmul(projt[pl.ds(D + rows, 80), :], gs).astype(BF16)
            gt[pl.ds(D + rows, 80), :] = matmul_t(projt[pl.ds(rows, 80), :], gs).astype(BF16)
            gt[pl.ds(2 * D + rows, 80), :] = matmul_t(dat[pl.ds(rows, 80), :], low).astype(BF16)

    back(0)
    scatter.after_one()
    back(1)

    def grads(i):
        rows = pl.ds(i * HALF, HALF)
        part = matmul(wqkv[rows, :], gt[...])
        both = part * std[rows, :]
        both = both[:, 0:128] + both[:, 128:256]
        ghold[2, :, rows] = jnp.sum(both.T, axis=0, keepdims=True)
        scaled = part * gaincol[rows, :]
        gn[rows, :] = scaled
        return jnp.sum(scaled, axis=0, keepdims=True), jnp.sum(scaled * std[rows, :], axis=0, keepdims=True)

    low = grads(0)
    scatter.after_two()
    high = grads(1)
    gains = GainSum(ghold, g1, g2, gsem)
    gains.first(ghold[2])
    mean_g = (low[0] + high[0]) * (1.0 / D)
    mean_gs = (low[1] + high[1]) * (1.0 / D)
    branch = inv * (gn[...] - mean_g - std[...] * mean_gs)
    total = (bgt[...].astype(F32) + branch).astype(BF16)
    gx_ref[...] = matmul_t(permt[...], total).astype(BF16)
    scatter.after_z()
    gains.second()
    exchange_wait(tok, got, tsend, trecvs)
    dg_ref[...] = gains.finish() * norm_scale
    scatter.finish()


def finish_kernel(got_ref, gx_in, dw_ref, dg_ref, merged_ref, gx_ref, own_ref, gain_out):
    ordered = matmul(
        one_hot(256, 256, lambda r, c: r == lax.rem(c, 4) * 64 + lax.div(c, 4)), got_ref[...].reshape(256, D)
    ).astype(BF16)
    for c in range(4):
        merged_ref[:, pl.ds(c * D, D)] = ordered[64 * c : 64 * c + 64]
    gx_ref[...] = gx_in[...]
    for part in range(2):
        for core in range(2):
            own_ref[pl.ds(10 * part, 10), pl.ds(core * HALF, HALF)] = dw_ref[part, core, 0:10, :]
    first = lax.axis_index("seq") * 20
    turned = pltpu.roll(jnp.broadcast_to(dg_ref[...], (8, D)), lax.rem(D - first, D), 1)
    gain_out[...] = turned[0, 0:20]


def per_device(patches, lengths, token_dest, gain, w_qkv, w_out, cotangent):
    norm_scale = 1.0 / math.sqrt(256 * SEQ * NX)
    vmem = pl.BlockSpec(memory_space=pltpu.VMEM)
    hbm = pl.BlockSpec(memory_space=pl.ANY)
    smem = pl.BlockSpec(memory_space=pltpu.SMEM)

    def kernel(*refs):
        kernel_body(norm_scale, refs)

    got, gx, dw, dg = pl.pallas_call(
        kernel,
        out_shape=(
            jax.ShapeDtypeStruct((SEQ, GROUP, D), BF16),
            jax.ShapeDtypeStruct((256, D), BF16),
            jax.ShapeDtypeStruct((2, 2, 16, HALF), F32),
            jax.ShapeDtypeStruct((1, D), F32),
        ),
        in_specs=[vmem, vmem, smem, vmem, hbm, vmem, vmem],
        out_specs=(vmem,) * 4,
        scratch_shapes=[
            pltpu.VMEM((D, 3 * D), BF16),
            pltpu.VMEM((2, 32, D), BF16),
            pltpu.VMEM((2, 2, 4, NY, 48, HALF), BF16),
            pltpu.VMEM((SEQ, GROUP, D), BF16),
            pltpu.VMEM((SEQ, GROUP, D), BF16),
            pltpu.VMEM((SEQ, GROUP, D), BF16),
            pltpu.VMEM((256, D), BF16),
            pltpu.VMEM((256, D), BF16),
            pltpu.VMEM((256, 2 * D), BF16),
            pltpu.VMEM((3 * D, 256), BF16),
            pltpu.VMEM((256, 256), BF16),
            pltpu.VMEM((HEADS, 256, 256), F32),
            pltpu.VMEM((D, 512), BF16),
            pltpu.VMEM((1536, 256), BF16),
            pltpu.VMEM((256, 1536), BF16),
            pltpu.VMEM((256, D), BF16),
            pltpu.VMEM((D, 256), BF16),
            pltpu.VMEM((D, 256), BF16),
            pltpu.VMEM((3 * D, 256), BF16),
            pltpu.VMEM((D, 256), F32),
            pltpu.VMEM((D, 256), F32),
            pltpu.VMEM((512, HALF), BF16),
            pltpu.VMEM((NX, NY, 80, HALF), F32),
            pltpu.VMEM((NX, NY, 80, HALF), BF16),
            pltpu.VMEM((3, NY, 80, 384), BF16),
            pltpu.VMEM((3, NX, 80, 256), BF16),
            pltpu.VMEM((NY, 80, 384), F32),
            pltpu.VMEM((NX, 80, 256), F32),
            pltpu.VMEM((NY, 80, 384), BF16),
            pltpu.VMEM((NX, 80, 256), BF16),
            pltpu.VMEM((3, 80, 384), BF16),
            pltpu.VMEM((3, 80, 256), BF16),
            pltpu.VMEM((128, HALF), BF16),
            pltpu.VMEM((7, 16, HALF), BF16),
            pltpu.VMEM((16, HALF), F32),
            pltpu.VMEM((3, 1, D), F32),
            pltpu.VMEM((15, 1, D), F32),
            pltpu.VMEM((15, 1, D), F32),
            pltpu.VMEM((D, 256), F32),
            pltpu.SemaphoreType.DMA((3,)),
            pltpu.SemaphoreType.DMA((80,)),
            pltpu.SemaphoreType.DMA,
            pltpu.SemaphoreType.DMA,
            pltpu.SemaphoreType.DMA,
            pltpu.SemaphoreType.DMA,
            pltpu.SemaphoreType.DMA((72,)),
            pltpu.SemaphoreType.DMA((60,)),
        ],
        compiler_params=pltpu.CompilerParams(
            collective_id=0, has_side_effects=True, vmem_limit_bytes=LIMIT
        ),
    )(
        patches[0], token_dest, lengths[0], gain, w_qkv, w_out, cotangent[0],
    )
    merged, gx, own_weight, own_gain = pl.pallas_call(
        finish_kernel,
        out_shape=(
            jax.ShapeDtypeStruct((SEQ, GROUP * D), BF16),
            jax.ShapeDtypeStruct((256, D), BF16),
            jax.ShapeDtypeStruct((20, D), F32),
            jax.ShapeDtypeStruct((20,), F32),
        ),
        in_specs=[vmem] * 4,
        out_specs=(vmem,) * 4,
        compiler_params=pltpu.CompilerParams(vmem_limit_bytes=LIMIT),
    )(got, gx, dw, dg)
    return (merged[None], gx[None], own_weight, own_gain)


def solution(mesh):
    placed = (
        P("dp", "seq", None),
        P("dp", "seq", None),
        P("dp", "seq"),
        P(),
        P(),
        P("seq", None),
        P("dp", "seq", None),
    )
    return jax.shard_map(
        per_device,
        mesh=mesh,
        in_specs=placed,
        out_specs=(P("dp", "seq", None), P("dp", "seq", None), P("seq", None), P("seq")),
        check_vma=False,
    )
```

```python
import math

import jax
import jax.numpy as jnp
from jax import lax
from jax.experimental import pallas as pl
from jax.experimental.pallas import tpu as pltpu
from jax.sharding import PartitionSpec as P

HEADS = 16
GROUP = 4
D = 1280
HALF = 640
PLAIN = 128
X_FIRST = 384
NZ, NY, NX = 8, 4, 4
SEQ = 64
LIMIT = 56 * 2**20

eps = 1e-06
F32 = jnp.float32
BF16 = jnp.bfloat16


def place():
    seq = lax.axis_index("seq")
    x = lax.axis_index("dp")
    return seq, x, lax.div(seq, 8), lax.rem(lax.div(seq, 2), 4), lax.rem(seq, 2)


def seq_of(z, y, core):
    return z * 8 + y * 2 + core


def dev(seq, x):
    return {"seq": seq, "dp": x}


def remote(src, dst, send, recv, seq, x):
    return pltpu.make_async_remote_copy(
        src_ref=src,
        dst_ref=dst,
        send_sem=send,
        recv_sem=recv,
        device_id=dev(seq, x),
        device_id_type=pl.DeviceIdType.MESH,
    )


class Presence:
    def __init__(self, news):
        self.news = news

    def signal(self, sem, seq, x):
        pl.semaphore_signal(sem, inc=1, device_id=dev(seq, x), device_id_type=pl.DeviceIdType.MESH)

    def greet(self):
        seq, x, z, y, core = place()
        barrier = pltpu.get_barrier_semaphore()
        for k in range(1, NZ):
            self.signal(barrier, seq_of(lax.rem(z + k, NZ), y, core), x)
        for k in range(1, NY):
            self.signal(barrier, seq_of(z, lax.rem(y + k, NY), core), x)
        for k in range(1, NX):
            self.signal(barrier, seq, lax.rem(x + k, NX))
        self.signal(barrier, seq_of(z, y, 1 - core), x)

    def lines(self):
        seq, x, z, y, core = place()
        pl.semaphore_wait(pltpu.get_barrier_semaphore(), 14)
        for k in range(1, NY):
            self.signal(self.news.at[0], seq_of(z, lax.rem(y + k, NY), core), x)

    def half_plane(self):
        seq, x, z, y, core = place()
        pl.semaphore_wait(self.news.at[0], NY - 1)
        self.signal(self.news.at[1], seq_of(z, y, 1 - core), x)

    def plane(self):
        seq, x, z, y, core = place()
        pl.semaphore_wait(self.news.at[1], 1)
        for k in range(1, NX):
            self.signal(self.news.at[2], seq, lax.rem(x + k, NX))

    def everybody(self):
        pl.semaphore_wait(self.news.at[2], NX - 1)


def owner_of(x, y, z):
    return 16 * x + 4 * y + lax.div(z, 2)


def exchange_start(src, dst, send, recv):
    seq, x, z, y, core = place()

    @pl.loop(1, SEQ)
    def _(k):
        to = lax.rem(seq + k, SEQ)
        remote(src.at[to], dst.at[seq], send, recv, to, x).start()

    pltpu.make_async_copy(src.at[seq], dst.at[seq], recv).start()


def exchange_wait(src, dst, send, recv):
    pltpu.make_async_copy(dst, dst, recv).wait()
    part = src.at[pl.ds(0, SEQ - 1)]
    pltpu.make_async_copy(part, part, send).wait()


def matmul(a, b):
    return jnp.dot(a, b, preferred_element_type=F32)


def matmul_t(a, b):
    return lax.dot_general(a, b, (((1,), (1,)), ((), ())), preferred_element_type=F32)


class Pool:
    def __init__(self, sems):
        self.sems, self.used = sems, 0

    def take(self):
        self.used += 1
        return self.sems.at[self.used - 1]


def one_hot(rows, columns, want):
    r = lax.broadcasted_iota(jnp.int32, (rows, columns), 0)
    c = lax.broadcasted_iota(jnp.int32, (rows, columns), 1)
    return jnp.where(want(r, c), 1.0, 0.0).astype(BF16)


WINDOWS = []
for _h in range(8):
    _first = 80 * _h // 128 * 128
    _off = 80 * _h - _first
    WINDOWS.append((_first, 128 if _off + 80 <= 128 else 256, _off))


def lanes_of(width, offset):
    lane = lax.broadcasted_iota(jnp.int32, (1, width), 1)
    return jnp.where((lane >= offset) & (lane < offset + 80), 1.0, 0.0).astype(BF16)


class Gather:
    def __init__(self, w_ref, slots, wg, sems):
        self.w_ref, self.slots, self.wg = w_ref, slots, wg
        self.pool = Pool(sems)
        self.p, self.q = pl.ds(0, PLAIN), pl.ds(PLAIN, HALF - PLAIN)

    def send(self, part, to, x):
        one = remote(part, part, self.pool.take(), self.pool.take(), to, x)
        one.start()
        return one

    def pair(self):
        seq, x, z, y, core = place()
        slots = self.slots
        own = jnp.concatenate([self.w_ref[...].astype(F32), jnp.zeros((12, D), F32)], axis=0)
        slots[core] = own.astype(BF16)
        self.first = self.send(slots.at[core], seq_of(z, y, 1 - core), x)

    def along_z(self):
        seq, x, z, y, core = place()
        slots, wg = self.slots, self.wg
        zh, zl = lax.div(z, 4), lax.rem(z, 4)
        self.first.wait()

        def want(r, c):
            return (c == jnp.where(r < 20, r, r + 12)) & (r < 40)

        first = pl.multiple_of(core * HALF, 128)
        rows = jnp.concatenate([slots[0, :, pl.ds(first, HALF)], slots[1, :, pl.ds(first, HALF)]], axis=0)
        own = matmul(one_hot(48, 64, want), rows).astype(BF16)
        wg[core, zh, zl, y, :, self.p] = own[:, 0:PLAIN]
        self.zsend = [self.pool.take() for _ in range(1, NZ)]
        both = self.pool.used
        self.zrecv = [self.pool.take() for _ in range(2)]

        @pl.when(zl == x)
        def _():
            wg[core, zh, zl, y, :, self.q] = own[:, PLAIN:HALF]
            part = wg.at[core, zh, zl, y, :, self.q]
            for k in range(1, NZ):
                to = seq_of(lax.rem(z + k, NZ), y, core)
                remote(part, part, self.zsend[k - 1], self.pool.sems.at[both + zh], to, x).start()

        part = wg.at[core, zh, zl, y, :, self.p]
        self.pz = [self.send(part, seq_of(lax.rem(z + k, NZ), y, core), x) for k in range(1, NZ)]

    def q_forward(self, k):
        seq, x, z, y, core = place()
        part = self.wg.at[core, :, x, lax.rem(y + NY - k, NY), :, self.q]
        self.qx.append([self.send(part, seq, lax.rem(x + j, NX)) for j in range(1, NX)])

    def q_along_y(self):
        seq, x, z, y, core = place()
        wg = self.wg
        for j in range(2):

            @pl.when(z != x + 4 * j)
            def _():
                part = wg.at[core, j, x, y, :, self.q]
                pltpu.make_async_copy(part, part, self.zrecv[j]).wait()

        part = wg.at[core, :, x, y, :, self.q]
        self.qy = [self.send(part, seq_of(z, lax.rem(y + k, NY), core), x) for k in range(1, NY)]
        self.qx = []
        self.q_forward(0)

    def p_to_pair(self, k):
        seq, x, z, y, core = place()
        part = self.wg.at[core, :, :, lax.rem(y + NY - k, NY), :, self.p]
        self.last.append(self.send(part, seq_of(z, y, 1 - core), x))

    def p_along_y(self):
        seq, x, z, y, core = place()
        for one in self.pz:
            one.wait()
        part = self.wg.at[core, :, :, y, :, self.p]
        self.py = [self.send(part, seq_of(z, lax.rem(y + k, NY), core), x) for k in range(1, NY)]
        self.last = []
        self.p_to_pair(0)

    def q_along_x(self):
        for k in range(1, NY):
            self.qy[k - 1].wait()
            self.q_forward(k)

    def p_pair(self):
        for k in range(1, NY):
            self.py[k - 1].wait()
            self.p_to_pair(k)

    def q_pair(self):
        seq, x, z, y, core = place()
        for k in range(NY):
            for one in self.qx[k]:
                one.wait()
            part = self.wg.at[core, :, :, lax.rem(y + NY - k, NY), :, self.q]
            self.last.append(self.send(part, seq_of(z, y, 1 - core), x))

    def finish(self):
        seq, x, z, y, core = place()
        for one in self.last:
            one.wait()

        @pl.when(lax.rem(z, 4) == x)
        def _():
            part = self.wg.at[core, 0, 0, 0, :, self.q]
            for k in range(1, NZ):
                pltpu.make_async_copy(part, part, self.zsend[k - 1]).wait()


class Scatter:
    def __init__(self, at_ref, bg_ref, out, bufs, sems, norm_scale):
        self.at_ref, self.bg_ref, self.out, self.bufs, self.sems = at_ref, bg_ref, out, bufs, sems
        self.pool = Pool(sems)
        self.norm_scale = norm_scale
        self.a, self.b = pl.ds(0, X_FIRST), pl.ds(X_FIRST, HALF - X_FIRST)

    def wait(self):
        for one in self.now:
            one.wait()

    def send(self, src, dst, to, x):
        one = remote(src, dst, self.pool.take(), self.pool.take(), to, x)
        one.start()
        return one

    def send_attended(self):
        seq, x, z, y, core = place()
        at = self.at_ref
        self.now = [self.send(at.at[:, pl.ds(0, 256)], at.at[:, pl.ds(256, 256)], seq_of(z, y, 1 - core), x)]

    def send_grad(self):
        seq, x, z, y, core = place()
        pair = self.bufs[0]
        theirs = pl.multiple_of((1 - core) * HALF, 128)
        src = self.bg_ref.at[:, pl.ds(theirs, HALF)]
        self.now.append(self.send(src, pair.at[pl.ds(256, 256)], seq_of(z, y, 1 - core), x))
        pair[pl.ds(0, 256), :] = self.bg_ref[:, pl.ds(pl.multiple_of(core * HALF, 128), HALF)]

    def product(self):
        pair, wsum, wb, xa, yb, sa, sb, wa2, wb2, ya, xb, zs, zr, s3 = self.bufs
        seq, x, z, y, core = place()
        self.wait()
        self.now = []
        for k in (1, 2, 3, 0):
            i = lax.rem(x + k, NX)
            rows = pl.ds(pl.multiple_of(i * 320, 64), 320)
            part = matmul(self.at_ref[rows, :], pair[...]).reshape(NY, 80, HALF)
            wsum[i] = part
            wb[i] = part.astype(BF16)
            if k > 0:
                self.now.append(self.send(wb.at[i, :, :, self.a], xa.at[k - 1], seq, i))
            for j in range(1, NY):
                to = lax.rem(y + j, NY)
                self.now.append(self.send(wb.at[i, to, :, self.b], yb.at[j - 1, i], seq_of(z, to, core), x))

    def after_one(self):
        pair, wsum, wb, xa, yb, sa, sb, wa2, wb2, ya, xb, zs, zr, s3 = self.bufs
        seq, x, z, y, core = place()
        self.wait()

        @pl.loop(0, 4)
        def _(j):
            total = wsum[x, j, :, self.a]
            for k in range(3):
                total += xa[k, j].astype(F32)
            sa[j] = total
            wa2[j] = total.astype(BF16)
            total = wsum[j, y, :, self.b]
            for k in range(3):
                total += yb[k, j].astype(F32)
            sb[j] = total
            wb2[j] = total.astype(BF16)

        self.now = []
        for k in range(1, NY):
            to = lax.rem(y + k, NY)
            self.now.append(self.send(wa2.at[to], ya.at[k - 1], seq_of(z, to, core), x))
            to = lax.rem(x + k, NX)
            self.now.append(self.send(wb2.at[to], xb.at[k - 1], seq, to))

    def after_two(self):
        pair, wsum, wb, xa, yb, sa, sb, wa2, wb2, ya, xb, zs, zr, s3 = self.bufs
        seq, x, z, y, core = place()
        self.wait()
        total = sa[y]
        for k in range(3):
            total += ya[k].astype(F32)
        second = sb[x]
        for k in range(3):
            second += xb[k].astype(F32)

        def want(r, c):
            low = lax.rem(r, 16)
            return (c == lax.div(r, 16) * 10 + low) & (low < 10)

        chosen = one_hot(128, 80, want)
        zs[:, self.a] = matmul(chosen, total.astype(BF16)).astype(BF16)
        zs[:, self.b] = matmul(chosen, second.astype(BF16)).astype(BF16)
        self.now = []
        for k in range(1, NZ):
            to = lax.rem(z + k, NZ)
            src = zs.at[pl.ds(pl.multiple_of(to * 16, 16), 16)]
            self.now.append(self.send(src, zr.at[k - 1], seq_of(to, y, core), x))

    def after_z(self):
        zs, zr, s3 = self.bufs[-3:]
        seq, x, z, y, core = place()
        out = self.out
        self.wait()
        total = zs[pl.ds(pl.multiple_of(z * 16, 16), 16), :].astype(F32)
        for k in range(7):
            total += zr[k].astype(F32)
        s3[...] = total * self.norm_scale
        owner = owner_of(x, y, z)
        slot = out.at[lax.rem(z, 2), core]
        self.sent, self.got = self.pool.take(), self.pool.take()
        self.now = [
            remote(s3, slot, self.pool.take(), self.got, owner, lax.rem(x + k, NX)) for k in range(1, NX)
        ]
        for one in self.now:
            one.start()

        @pl.when(owner != seq)
        def _():
            remote(s3, slot, self.sent, self.got, owner, x).start()

        @pl.when(owner == seq)
        def _():
            pltpu.make_async_copy(s3, slot, self.got).start()

    def finish(self):
        seq, x, z, y, core = place()
        out, s3 = self.out, self.bufs[-1]
        for one in self.now:
            one.wait_send()

        @pl.when(owner_of(x, y, z) != seq)
        def _():
            pltpu.make_async_copy(s3, s3, self.sent).wait()

        pltpu.make_async_copy(out, out, self.got).wait()


class GainSum:
    def __init__(self, ghold, g1, g2, sems):
        self.ghold, self.g1, self.g2, self.sems = ghold, g1, g2, sems

    def first(self, total):
        seq, x, z, y, core = place()
        self.ghold[0] = total
        self.now = []
        for k in range(1, 16):
            kx, ky = k // 4, k % 4
            to = seq_of(z, lax.rem(y + ky, NY), core)
            self.now.append(
                remote(
                    self.ghold.at[0], self.g1.at[k - 1], self.sems.at[2 * k - 2], self.sems.at[2 * k - 1],
                    to, lax.rem(x + kx, NX),
                )
            )
        for one in self.now:
            one.start()

    def second(self):
        seq, x, z, y, core = place()
        for one in self.now:
            one.wait()
        total = self.ghold[0]
        for k in range(15):
            total += self.g1[k]
        self.ghold[1] = total
        self.now = []
        for k in range(1, 16):
            kz, kc = k // 2, k % 2
            to = seq_of(lax.rem(z + kz, NZ), y, lax.rem(core + kc, 2))
            self.now.append(
                remote(
                    self.ghold.at[1], self.g2.at[k - 1], self.sems.at[28 + 2 * k], self.sems.at[29 + 2 * k], to, x
                )
            )
        for one in self.now:
            one.start()

    def finish(self):
        for one in self.now:
            one.wait()
        total = self.ghold[1]
        for k in range(15):
            total += self.g2[k]
        return total


def kernel_body(norm_scale, refs):
    (x_ref, dest_ref, len_ref, gain_ref, wqkv_hbm, wout_ref, cot_ref,
     got, gx_ref, dw_ref, dg_ref,
     wqkv, slots, wg, cslab, crecv, tok, xp, normed, kv, projt, permt, probs, at, atp, apad, bg, bgt, dat, gt, gn, std, pair,
     wsum, wb, xa, yb, sa, sb, wa2, wb2, ya, xb, zs, zr, s3, ghold, g1, g2, gaincol,
     wsem, news, asem, csend, crecvs, tsend, trecvs, ssem, gsem) = refs
    score_scale = 1.0 / math.sqrt(80)

    loads = []
    for j in range(3):
        cols = pl.ds(j * D, D)
        loads.append(pltpu.make_async_copy(wqkv_hbm.at[:, cols], wqkv.at[:, cols], wsem.at[j]))
    for one in loads:
        one.start()

    presence = Presence(news)
    presence.greet()

    def shuffle(r, c):
        return c == lax.rem(r, 4) * 64 + lax.div(r, 4)

    stacked = jnp.concatenate([cot_ref[:, pl.ds(c * D, D)] for c in range(4)], axis=0)
    cslab[...] = matmul(one_hot(256, 256, shuffle), stacked).astype(BF16).reshape(SEQ, GROUP, D)
    slot = jnp.broadcast_to(lax.shift_right_logical(dest_ref[...], 6), (8, 64)).astype(F32).astype(BF16)
    to_row = matmul(slot, one_hot(64, 256, lambda r, c: r == lax.div(c, 4)))[0:1]
    to_col = matmul_t(one_hot(256, 64, lambda r, c: c == lax.div(r, 4)), slot)[:, 0:1]
    row_number = lax.broadcasted_iota(jnp.int32, (1, 256), 1)
    col_number = lax.broadcasted_iota(jnp.int32, (256, 1), 0)
    key_row = to_row.astype(jnp.int32) * GROUP + lax.rem(row_number, GROUP)
    key_col = to_col.astype(jnp.int32) * GROUP + lax.rem(col_number, GROUP)
    id_row, id_col = jnp.zeros((1, 256), F32), jnp.zeros((256, 1), F32)
    end = 0
    for j in range(3):
        end = end + len_ref[0, j] * GROUP
        id_row += jnp.where(row_number >= end, 1.0, 0.0)
        id_col += jnp.where(col_number >= end, 1.0, 0.0)
    ir = lax.broadcasted_iota(jnp.int32, (256, 256), 0)
    ic = lax.broadcasted_iota(jnp.int32, (256, 256), 1)
    perm = jnp.where(ir == key_row, 1.0, 0.0).astype(BF16)
    permt[...] = jnp.where(ic == key_col, 1.0, 0.0).astype(BF16)
    ids_k = jnp.sum(jnp.where(ir == key_row, id_row, 0.0), axis=1, keepdims=True)
    ids_q = jnp.sum(jnp.where(ic == key_col, id_col, 0.0), axis=0, keepdims=True)

    wide = matmul(perm, x_ref[...])
    xp[...] = wide.astype(BF16)
    centred = wide - jnp.mean(wide, axis=-1, keepdims=True)
    spread = lax.rsqrt(jnp.mean(centred * centred, axis=-1, keepdims=True) + eps)
    normed[...] = (centred * spread * gain_ref[...].reshape(1, D)).astype(BF16)

    presence.lines()
    gather = Gather(wout_ref, slots, wg, asem)
    gather.pair()

    def project(j):
        loads[j].wait()
        cols = pl.ds(j * D, D)
        part = matmul(normed[...], wqkv[:, cols]).astype(BF16)
        if j > 0:
            kv[:, pl.ds((j - 1) * D, D)] = part
        projt[cols, :] = part.T

    project(0)
    gather.along_z()
    presence.half_plane()
    project(1)
    project(2)
    presence.plane()
    gather.q_along_y()
    gather.p_along_y()
    exchange_start(cslab, crecv, csend, crecvs)
    same = ids_k == ids_q

    def attend(g):
        for h in range(8):
            first, width, off = WINDOWS[h]
            lanes = pl.ds(pl.multiple_of(g * HALF + first, 128), width)
            rows = pl.multiple_of(g * HALF + h * 80, 16)
            keys = kv[:, lanes] * lanes_of(width, off)
            scores = matmul(keys, projt[lanes, :]) * score_scale
            scores = jnp.where(same, scores, -jnp.inf)
            scores = jnp.exp(scores - jnp.max(scores, axis=0, keepdims=True))
            share = scores * (1.0 / jnp.sum(scores, axis=0, keepdims=True))
            probs[g * 8 + h] = share
            part = matmul(projt[pl.ds(2 * D + rows, 80), :], share.astype(BF16))
            at[pl.ds(rows, 80), pl.ds(0, 256)] = part.astype(BF16)
            gap = jnp.zeros((8, 256), F32)
            padded = jnp.concatenate([part[0:40], gap, part[40:80], gap], axis=0).astype(BF16)
            atp[pl.ds(pl.multiple_of(g * 768 + h * 96, 16), 96), :] = padded

    attend(0)
    gather.q_along_x()
    attend(1)
    scatter = Scatter(
        at, bg, dw_ref, (pair, wsum, wb, xa, yb, sa, sb, wa2, wb2, ya, xb, zs, zr, s3), ssem, norm_scale
    )
    scatter.send_attended()

    across = xp[...].T.astype(F32)
    across = across - jnp.mean(across, axis=0, keepdims=True)
    inv = lax.rsqrt(jnp.mean(across * across, axis=0, keepdims=True) + eps)
    std[...] = across * inv
    column = jnp.broadcast_to(gain_ref[...].reshape(1, D), (128, D)).T
    gaincol[:, 0:128] = column
    gaincol[:, 128:256] = column
    apad[...] = atp[...].T
    gather.p_pair()
    exchange_wait(cslab, crecv, csend, crecvs)
    bg[...] = crecv[...].reshape(256, D)
    scatter.send_grad()
    bgt[...] = bg[...].T
    scatter.product()
    gather.q_pair()
    gather.finish()
    for half in range(2):
        cols = pl.ds(half * HALF, HALF)
        branch = matmul(apad[...], wg[half].reshape(1536, HALF))
        block = (xp[:, cols].astype(F32) + branch).astype(BF16)
        tok[:, :, cols] = block.reshape(SEQ, GROUP, HALF)
    exchange_start(tok, got, tsend, trecvs)

    for i in range(4):
        part = matmul_t(wg[0, i // 2, pl.ds(2 * (i % 2), 2)].reshape(384, HALF), bg[:, pl.ds(0, HALF)])
        part += matmul_t(wg[1, i // 2, pl.ds(2 * (i % 2), 2)].reshape(384, HALF), bg[:, pl.ds(HALF, HALF)])
        for h in range(4):
            own = part[96 * h : 96 * h + 96]
            own = jnp.concatenate([own[0:40], own[48:88]], axis=0).astype(BF16)
            dat[pl.ds(i * 320 + 80 * h, 80), :] = own

    def back(g):
        for h in range(8):
            first, width, off = WINDOWS[h]
            lanes = pl.ds(pl.multiple_of(g * HALF + first, 128), width)
            rows = pl.multiple_of(g * HALF + h * 80, 16)
            values = kv[:, pl.ds(pl.multiple_of(D + g * HALF + first, 128), width)] * lanes_of(width, off)
            share = probs[g * 8 + h]
            gp = matmul(values, dat[lanes, :])
            delta = jnp.sum(gp * share, axis=0, keepdims=True)
            gs = (share * (gp - delta) * score_scale).astype(BF16)
            low = share.astype(BF16)
            gt[pl.ds(rows, 80), :] = matmul(projt[pl.ds(D + rows, 80), :], gs).astype(BF16)
            gt[pl.ds(D + rows, 80), :] = matmul_t(projt[pl.ds(rows, 80), :], gs).astype(BF16)
            gt[pl.ds(2 * D + rows, 80), :] = matmul_t(dat[pl.ds(rows, 80), :], low).astype(BF16)

    back(0)
    scatter.after_one()
    back(1)

    def grads(i):
        rows = pl.ds(i * HALF, HALF)
        part = matmul(wqkv[rows, :], gt[...])
        both = part * std[rows, :]
        both = both[:, 0:128] + both[:, 128:256]
        ghold[2, :, rows] = jnp.sum(both.T, axis=0, keepdims=True)
        scaled = part * gaincol[rows, :]
        gn[rows, :] = scaled
        return jnp.sum(scaled, axis=0, keepdims=True), jnp.sum(scaled * std[rows, :], axis=0, keepdims=True)

    low = grads(0)
    scatter.after_two()
    high = grads(1)
    presence.everybody()
    gains = GainSum(ghold, g1, g2, gsem)
    gains.first(ghold[2])
    mean_g = (low[0] + high[0]) * (1.0 / D)
    mean_gs = (low[1] + high[1]) * (1.0 / D)
    branch = inv * (gn[...] - mean_g - std[...] * mean_gs)
    total = (bgt[...].astype(F32) + branch).astype(BF16)
    gx_ref[...] = matmul_t(permt[...], total).astype(BF16)
    scatter.after_z()
    gains.second()
    exchange_wait(tok, got, tsend, trecvs)
    dg_ref[...] = gains.finish() * norm_scale
    scatter.finish()


def finish_kernel(got_ref, gx_in, dw_ref, dg_ref, merged_ref, gx_ref, own_ref, gain_out):
    ordered = matmul(
        one_hot(256, 256, lambda r, c: r == lax.rem(c, 4) * 64 + lax.div(c, 4)), got_ref[...].reshape(256, D)
    ).astype(BF16)
    for c in range(4):
        merged_ref[:, pl.ds(c * D, D)] = ordered[64 * c : 64 * c + 64]
    gx_ref[...] = gx_in[...]
    for part in range(2):
        for core in range(2):
            own_ref[pl.ds(10 * part, 10), pl.ds(core * HALF, HALF)] = dw_ref[part, core, 0:10, :]
    first = lax.axis_index("seq") * 20
    turned = pltpu.roll(jnp.broadcast_to(dg_ref[...], (8, D)), lax.rem(D - first, D), 1)
    gain_out[...] = turned[0, 0:20]


def per_device(patches, lengths, token_dest, gain, w_qkv, w_out, cotangent):
    norm_scale = 1.0 / math.sqrt(256 * SEQ * NX)
    vmem = pl.BlockSpec(memory_space=pltpu.VMEM)
    hbm = pl.BlockSpec(memory_space=pl.ANY)
    smem = pl.BlockSpec(memory_space=pltpu.SMEM)

    def kernel(*refs):
        kernel_body(norm_scale, refs)

    got, gx, dw, dg = pl.pallas_call(
        kernel,
        out_shape=(
            jax.ShapeDtypeStruct((SEQ, GROUP, D), BF16),
            jax.ShapeDtypeStruct((256, D), BF16),
            jax.ShapeDtypeStruct((2, 2, 16, HALF), F32),
            jax.ShapeDtypeStruct((1, D), F32),
        ),
        in_specs=[vmem, vmem, smem, vmem, hbm, vmem, vmem],
        out_specs=(vmem,) * 4,
        scratch_shapes=[
            pltpu.VMEM((D, 3 * D), BF16),
            pltpu.VMEM((2, 32, D), BF16),
            pltpu.VMEM((2, 2, 4, NY, 48, HALF), BF16),
            pltpu.VMEM((SEQ, GROUP, D), BF16),
            pltpu.VMEM((SEQ, GROUP, D), BF16),
            pltpu.VMEM((SEQ, GROUP, D), BF16),
            pltpu.VMEM((256, D), BF16),
            pltpu.VMEM((256, D), BF16),
            pltpu.VMEM((256, 2 * D), BF16),
            pltpu.VMEM((3 * D, 256), BF16),
            pltpu.VMEM((256, 256), BF16),
            pltpu.VMEM((HEADS, 256, 256), F32),
            pltpu.VMEM((D, 512), BF16),
            pltpu.VMEM((1536, 256), BF16),
            pltpu.VMEM((256, 1536), BF16),
            pltpu.VMEM((256, D), BF16),
            pltpu.VMEM((D, 256), BF16),
            pltpu.VMEM((D, 256), BF16),
            pltpu.VMEM((3 * D, 256), BF16),
            pltpu.VMEM((D, 256), F32),
            pltpu.VMEM((D, 256), F32),
            pltpu.VMEM((512, HALF), BF16),
            pltpu.VMEM((NX, NY, 80, HALF), F32),
            pltpu.VMEM((NX, NY, 80, HALF), BF16),
            pltpu.VMEM((3, NY, 80, X_FIRST), BF16),
            pltpu.VMEM((3, NX, 80, HALF - X_FIRST), BF16),
            pltpu.VMEM((NY, 80, X_FIRST), F32),
            pltpu.VMEM((NX, 80, HALF - X_FIRST), F32),
            pltpu.VMEM((NY, 80, X_FIRST), BF16),
            pltpu.VMEM((NX, 80, HALF - X_FIRST), BF16),
            pltpu.VMEM((3, 80, X_FIRST), BF16),
            pltpu.VMEM((3, 80, HALF - X_FIRST), BF16),
            pltpu.VMEM((128, HALF), BF16),
            pltpu.VMEM((7, 16, HALF), BF16),
            pltpu.VMEM((16, HALF), F32),
            pltpu.VMEM((3, 1, D), F32),
            pltpu.VMEM((15, 1, D), F32),
            pltpu.VMEM((15, 1, D), F32),
            pltpu.VMEM((D, 256), F32),
            pltpu.SemaphoreType.DMA((3,)),
            pltpu.SemaphoreType.REGULAR((3,)),
            pltpu.SemaphoreType.DMA((80,)),
            pltpu.SemaphoreType.DMA,
            pltpu.SemaphoreType.DMA,
            pltpu.SemaphoreType.DMA,
            pltpu.SemaphoreType.DMA,
            pltpu.SemaphoreType.DMA((72,)),
            pltpu.SemaphoreType.DMA((60,)),
        ],
        compiler_params=pltpu.CompilerParams(
            collective_id=0, has_side_effects=True, vmem_limit_bytes=LIMIT
        ),
    )(
        patches[0], token_dest, lengths[0], gain, w_qkv, w_out, cotangent[0],
    )
    merged, gx, own_weight, own_gain = pl.pallas_call(
        finish_kernel,
        out_shape=(
            jax.ShapeDtypeStruct((SEQ, GROUP * D), BF16),
            jax.ShapeDtypeStruct((256, D), BF16),
            jax.ShapeDtypeStruct((20, D), F32),
            jax.ShapeDtypeStruct((20,), F32),
        ),
        in_specs=[vmem] * 4,
        out_specs=(vmem,) * 4,
        compiler_params=pltpu.CompilerParams(vmem_limit_bytes=LIMIT),
    )(got, gx, dw, dg)
    return (merged[None], gx[None], own_weight, own_gain)


def solution(mesh):
    placed = (
        P("dp", "seq", None),
        P("dp", "seq", None),
        P("dp", "seq"),
        P(),
        P(),
        P("seq", None),
        P("dp", "seq", None),
    )
    return jax.shard_map(
        per_device,
        mesh=mesh,
        in_specs=placed,
        out_specs=(P("dp", "seq", None), P("dp", "seq", None), P("seq", None), P("seq")),
        check_vma=False,
    )
```

```python
import math

import jax
import jax.numpy as jnp
from jax import lax
from jax.experimental import pallas as pl
from jax.experimental.pallas import tpu as pltpu
from jax.sharding import PartitionSpec as P

HEADS = 16
GROUP = 4
D = 1280
HALF = 640
PLAIN = 128
X_FIRST = 384
NZ, NY, NX = 8, 4, 4
SEQ = 64
LIMIT = 56 * 2**20

eps = 1e-06
F32 = jnp.float32
BF16 = jnp.bfloat16


def place():
    seq = lax.axis_index("seq")
    x = lax.axis_index("dp")
    return seq, x, lax.div(seq, 8), lax.rem(lax.div(seq, 2), 4), lax.rem(seq, 2)


def seq_of(z, y, core):
    return z * 8 + y * 2 + core


def dev(seq, x):
    return {"seq": seq, "dp": x}


def remote(src, dst, send, recv, seq, x):
    return pltpu.make_async_remote_copy(
        src_ref=src,
        dst_ref=dst,
        send_sem=send,
        recv_sem=recv,
        device_id=dev(seq, x),
        device_id_type=pl.DeviceIdType.MESH,
    )


class Presence:
    def __init__(self, news):
        self.news = news

    def signal(self, sem, seq, x):
        pl.semaphore_signal(sem, inc=1, device_id=dev(seq, x), device_id_type=pl.DeviceIdType.MESH)

    def greet(self):
        seq, x, z, y, core = place()
        barrier = pltpu.get_barrier_semaphore()
        for k in range(1, NZ):
            self.signal(barrier, seq_of(lax.rem(z + k, NZ), y, core), x)
        for k in range(1, NY):
            self.signal(barrier, seq_of(z, lax.rem(y + k, NY), core), x)
        for k in range(1, NX):
            self.signal(barrier, seq, lax.rem(x + k, NX))
        self.signal(barrier, seq_of(z, y, 1 - core), x)

    def lines(self):
        seq, x, z, y, core = place()
        pl.semaphore_wait(pltpu.get_barrier_semaphore(), 14)
        for k in range(1, NY):
            self.signal(self.news.at[0], seq_of(z, lax.rem(y + k, NY), core), x)

    def half_plane(self):
        seq, x, z, y, core = place()
        pl.semaphore_wait(self.news.at[0], NY - 1)
        self.signal(self.news.at[1], seq_of(z, y, 1 - core), x)

    def plane(self):
        seq, x, z, y, core = place()
        pl.semaphore_wait(self.news.at[1], 1)
        for k in range(1, NX):
            self.signal(self.news.at[2], seq, lax.rem(x + k, NX))

    def everybody(self):
        pl.semaphore_wait(self.news.at[2], NX - 1)


def piece_of(x, z):
    return lax.rem(z - 2 * x + 3 + NZ, NZ)


def owner_of(x, y, z):
    piece = piece_of(x, z)
    return seq_of(2 * x + lax.div(piece, 4), y, lax.rem(lax.div(piece, 2), 2))


def exchange_start(src, dst, send, recv):
    seq, x, z, y, core = place()

    @pl.loop(1, SEQ)
    def _(k):
        to = lax.rem(seq + k, SEQ)
        remote(src.at[to], dst.at[seq], send, recv, to, x).start()

    pltpu.make_async_copy(src.at[seq], dst.at[seq], recv).start()


def exchange_wait(src, dst, send, recv):
    pltpu.make_async_copy(dst, dst, recv).wait()
    part = src.at[pl.ds(0, SEQ - 1)]
    pltpu.make_async_copy(part, part, send).wait()


def matmul(a, b):
    return jnp.dot(a, b, preferred_element_type=F32)


def matmul_t(a, b):
    return lax.dot_general(a, b, (((1,), (1,)), ((), ())), preferred_element_type=F32)


class Pool:
    def __init__(self, sems):
        self.sems, self.used = sems, 0

    def take(self):
        self.used += 1
        return self.sems.at[self.used - 1]


def one_hot(rows, columns, want):
    r = lax.broadcasted_iota(jnp.int32, (rows, columns), 0)
    c = lax.broadcasted_iota(jnp.int32, (rows, columns), 1)
    return jnp.where(want(r, c), 1.0, 0.0).astype(BF16)


WINDOWS = []
for _h in range(8):
    _first = 80 * _h // 128 * 128
    _off = 80 * _h - _first
    WINDOWS.append((_first, 128 if _off + 80 <= 128 else 256, _off))


def lanes_of(width, offset):
    lane = lax.broadcasted_iota(jnp.int32, (1, width), 1)
    return jnp.where((lane >= offset) & (lane < offset + 80), 1.0, 0.0).astype(BF16)


class Gather:
    def __init__(self, w_ref, slots, wg, sems):
        self.w_ref, self.slots, self.wg = w_ref, slots, wg
        self.pool = Pool(sems)
        self.p, self.q = pl.ds(0, PLAIN), pl.ds(PLAIN, HALF - PLAIN)

    def send(self, part, to, x):
        one = remote(part, part, self.pool.take(), self.pool.take(), to, x)
        one.start()
        return one

    def pair(self):
        seq, x, z, y, core = place()
        slots = self.slots
        own = jnp.concatenate([self.w_ref[...].astype(F32), jnp.zeros((12, D), F32)], axis=0)
        slots[core] = own.astype(BF16)
        self.first = self.send(slots.at[core], seq_of(z, y, 1 - core), x)

    def along_z(self):
        seq, x, z, y, core = place()
        slots, wg = self.slots, self.wg
        zh, zl = lax.div(z, 4), lax.rem(z, 4)
        self.first.wait()

        def want(r, c):
            return (c == jnp.where(r < 20, r, r + 12)) & (r < 40)

        first = pl.multiple_of(core * HALF, 128)
        rows = jnp.concatenate([slots[0, :, pl.ds(first, HALF)], slots[1, :, pl.ds(first, HALF)]], axis=0)
        own = matmul(one_hot(48, 64, want), rows).astype(BF16)
        wg[core, zh, zl, y, :, self.p] = own[:, 0:PLAIN]
        self.zsend = [self.pool.take() for _ in range(1, NZ)]
        both = self.pool.used
        self.zrecv = [self.pool.take() for _ in range(2)]

        @pl.when(zl == x)
        def _():
            wg[core, zh, zl, y, :, self.q] = own[:, PLAIN:HALF]
            part = wg.at[core, zh, zl, y, :, self.q]
            for k in range(1, NZ):
                to = seq_of(lax.rem(z + k, NZ), y, core)
                remote(part, part, self.zsend[k - 1], self.pool.sems.at[both + zh], to, x).start()

        part = wg.at[core, zh, zl, y, :, self.p]
        self.pz = [self.send(part, seq_of(lax.rem(z + k, NZ), y, core), x) for k in range(1, NZ)]

    def q_forward(self, k):
        seq, x, z, y, core = place()
        part = self.wg.at[core, :, x, lax.rem(y + NY - k, NY), :, self.q]
        self.qx.append([self.send(part, seq, lax.rem(x + j, NX)) for j in range(1, NX)])

    def q_along_y(self):
        seq, x, z, y, core = place()
        wg = self.wg
        for j in range(2):

            @pl.when(z != x + 4 * j)
            def _():
                part = wg.at[core, j, x, y, :, self.q]
                pltpu.make_async_copy(part, part, self.zrecv[j]).wait()

        part = wg.at[core, :, x, y, :, self.q]
        self.qy = [self.send(part, seq_of(z, lax.rem(y + k, NY), core), x) for k in range(1, NY)]
        self.qx = []
        self.q_forward(0)

    def p_to_pair(self, k):
        seq, x, z, y, core = place()
        part = self.wg.at[core, :, :, lax.rem(y + NY - k, NY), :, self.p]
        self.last.append(self.send(part, seq_of(z, y, 1 - core), x))

    def p_along_y(self):
        seq, x, z, y, core = place()
        for one in self.pz:
            one.wait()
        part = self.wg.at[core, :, :, y, :, self.p]
        self.py = [self.send(part, seq_of(z, lax.rem(y + k, NY), core), x) for k in range(1, NY)]
        self.last = []
        self.p_to_pair(0)

    def q_along_x(self):
        for k in range(1, NY):
            self.qy[k - 1].wait()
            self.q_forward(k)

    def p_pair(self):
        for k in range(1, NY):
            self.py[k - 1].wait()
            self.p_to_pair(k)

    def q_pair(self):
        seq, x, z, y, core = place()
        for k in range(NY):
            for one in self.qx[k]:
                one.wait()
            part = self.wg.at[core, :, :, lax.rem(y + NY - k, NY), :, self.q]
            self.last.append(self.send(part, seq_of(z, y, 1 - core), x))

    def finish(self):
        seq, x, z, y, core = place()
        for one in self.last:
            one.wait()

        @pl.when(lax.rem(z, 4) == x)
        def _():
            part = self.wg.at[core, 0, 0, 0, :, self.q]
            for k in range(1, NZ):
                pltpu.make_async_copy(part, part, self.zsend[k - 1]).wait()


class Scatter:
    def __init__(self, at_ref, bg_ref, out, bufs, sems, norm_scale):
        self.at_ref, self.bg_ref, self.out, self.bufs, self.sems = at_ref, bg_ref, out, bufs, sems
        self.pool = Pool(sems)
        self.norm_scale = norm_scale
        self.a, self.b = pl.ds(0, X_FIRST), pl.ds(X_FIRST, HALF - X_FIRST)

    def wait(self):
        for one in self.now:
            one.wait()

    def send(self, src, dst, to, x):
        one = remote(src, dst, self.pool.take(), self.pool.take(), to, x)
        one.start()
        return one

    def send_attended(self):
        seq, x, z, y, core = place()
        at = self.at_ref
        self.now = [self.send(at.at[:, pl.ds(0, 256)], at.at[:, pl.ds(256, 256)], seq_of(z, y, 1 - core), x)]

    def send_grad(self):
        seq, x, z, y, core = place()
        pair = self.bufs[0]
        theirs = pl.multiple_of((1 - core) * HALF, 128)
        src = self.bg_ref.at[:, pl.ds(theirs, HALF)]
        self.now.append(self.send(src, pair.at[pl.ds(256, 256)], seq_of(z, y, 1 - core), x))
        pair[pl.ds(0, 256), :] = self.bg_ref[:, pl.ds(pl.multiple_of(core * HALF, 128), HALF)]

    def product(self):
        pair, wsum, wb, xa, yb, sa, sb, wa2, wb2, ya, xb, zs, zr, s3 = self.bufs
        seq, x, z, y, core = place()
        self.wait()
        self.now = []
        for k in (1, 2, 3, 0):
            i = lax.rem(x + k, NX)
            rows = pl.ds(pl.multiple_of(i * 320, 64), 320)
            part = matmul(self.at_ref[rows, :], pair[...]).reshape(2, NY, 40, HALF)
            for j in range(NY):
                own = jnp.concatenate([part[0, j], part[1, j]], axis=0)
                wsum[i, j] = own
                wb[i, j] = own.astype(BF16)
            if k > 0:
                self.now.append(self.send(wb.at[i, :, :, self.a], xa.at[k - 1], seq, i))
            for j in range(1, NY):
                to = lax.rem(y + j, NY)
                self.now.append(self.send(wb.at[i, to, :, self.b], yb.at[j - 1, i], seq_of(z, to, core), x))

    def after_one(self):
        pair, wsum, wb, xa, yb, sa, sb, wa2, wb2, ya, xb, zs, zr, s3 = self.bufs
        seq, x, z, y, core = place()
        self.wait()

        @pl.loop(0, 4)
        def _(j):
            total = wsum[x, j, :, self.a]
            for k in range(3):
                total += xa[k, j].astype(F32)
            sa[j] = total
            wa2[j] = total.astype(BF16)
            total = wsum[j, y, :, self.b]
            for k in range(3):
                total += yb[k, j].astype(F32)
            sb[j] = total
            wb2[j] = total.astype(BF16)

        self.now = []
        for k in range(1, NY):
            to = lax.rem(y + k, NY)
            self.now.append(self.send(wa2.at[to], ya.at[k - 1], seq_of(z, to, core), x))
            to = lax.rem(x + k, NX)
            self.now.append(self.send(wb2.at[to], xb.at[k - 1], seq, to))

    def after_two(self):
        pair, wsum, wb, xa, yb, sa, sb, wa2, wb2, ya, xb, zs, zr, s3 = self.bufs
        seq, x, z, y, core = place()
        self.wait()
        total = sa[y]
        for k in range(3):
            total += ya[k].astype(F32)
        second = sb[x]
        for k in range(3):
            second += xb[k].astype(F32)

        def want(r, c):
            low = lax.rem(r, 16)
            return (c == lax.div(r, 16) * 10 + low) & (low < 10)

        chosen = one_hot(128, 80, want)
        zs[:, self.a] = matmul(chosen, total.astype(BF16)).astype(BF16)
        zs[:, self.b] = matmul(chosen, second.astype(BF16)).astype(BF16)
        self.now = []
        for k in range(1, NZ):
            to = lax.rem(z + k, NZ)
            src = zs.at[pl.ds(pl.multiple_of(piece_of(x, to) * 16, 16), 16)]
            self.now.append(self.send(src, zr.at[k - 1], seq_of(to, y, core), x))

    def after_z(self):
        zs, zr, s3 = self.bufs[-3:]
        seq, x, z, y, core = place()
        out = self.out
        self.wait()
        total = zs[pl.ds(pl.multiple_of(piece_of(x, z) * 16, 16), 16), :].astype(F32)
        for k in range(7):
            total += zr[k].astype(F32)
        s3[...] = (total * self.norm_scale).astype(BF16)
        owner = owner_of(x, y, z)
        slot = out.at[lax.rem(piece_of(x, z), 2), core]
        self.sent, self.got = self.pool.take(), self.pool.take()
        self.now = [
            remote(s3, slot, self.pool.take(), self.got, owner, lax.rem(x + k, NX)) for k in range(1, NX)
        ]
        for one in self.now:
            one.start()

        @pl.when(owner != seq)
        def _():
            remote(s3, slot, self.sent, self.got, owner, x).start()

        @pl.when(owner == seq)
        def _():
            pltpu.make_async_copy(s3, slot, self.got).start()

    def finish(self):
        seq, x, z, y, core = place()
        out, s3 = self.out, self.bufs[-1]
        for one in self.now:
            one.wait_send()

        @pl.when(owner_of(x, y, z) != seq)
        def _():
            pltpu.make_async_copy(s3, s3, self.sent).wait()

        pltpu.make_async_copy(out, out, self.got).wait()


class GainSum:
    def __init__(self, ghold, g1, g2, sems):
        self.ghold, self.g1, self.g2, self.sems = ghold, g1, g2, sems

    def first(self, total):
        seq, x, z, y, core = place()
        self.ghold[0] = total
        self.now = []
        for k in range(1, 16):
            kx, ky = k // 4, k % 4
            to = seq_of(z, lax.rem(y + ky, NY), core)
            self.now.append(
                remote(
                    self.ghold.at[0], self.g1.at[k - 1], self.sems.at[2 * k - 2], self.sems.at[2 * k - 1],
                    to, lax.rem(x + kx, NX),
                )
            )
        for one in self.now:
            one.start()

    def second(self):
        seq, x, z, y, core = place()
        for one in self.now:
            one.wait()
        total = self.ghold[0]
        for k in range(15):
            total += self.g1[k]
        self.ghold[1] = total
        self.now = []
        for k in range(1, 16):
            kz, kc = k // 2, k % 2
            to = seq_of(lax.rem(z + kz, NZ), y, lax.rem(core + kc, 2))
            self.now.append(
                remote(
                    self.ghold.at[1], self.g2.at[k - 1], self.sems.at[28 + 2 * k], self.sems.at[29 + 2 * k], to, x
                )
            )
        for one in self.now:
            one.start()

    def finish(self):
        for one in self.now:
            one.wait()
        total = self.ghold[1]
        for k in range(15):
            total += self.g2[k]
        return total


def kernel_body(norm_scale, refs):
    (x_hbm, dest_ref, len_ref, gain_ref, wqkv_hbm, wout_hbm, cot_hbm,
     got, gx_ref, dw_ref, dg_ref,
     x_ref, wout_ref, cot_ref, wqkv, slots, wg, cslab, crecv, tok, xp, normed, kv, projt, permt, probs, at, atp, apad, bg, bgt, dat, gt, gn, std, pair,
     wsum, wb, xa, yb, sa, sb, wa2, wb2, ya, xb, zs, zr, s3, ghold, g1, g2, gaincol,
     wsem, news, asem, csend, crecvs, tsend, trecvs, ssem, gsem) = refs
    score_scale = 1.0 / math.sqrt(80)

    cot_load = pltpu.make_async_copy(cot_hbm, cot_ref, wsem.at[3])
    x_load = pltpu.make_async_copy(x_hbm, x_ref, wsem.at[4])
    out_load = pltpu.make_async_copy(wout_hbm, wout_ref, wsem.at[5])
    for one in (cot_load, out_load, x_load):
        one.start()
    presence = Presence(news)
    presence.greet()
    loads = []
    for j in range(3):
        cols = pl.ds(j * D, D)
        loads.append(pltpu.make_async_copy(wqkv_hbm.at[:, cols], wqkv.at[:, cols], wsem.at[j]))
    for one in loads:
        one.start()

    def shuffle(r, c):
        return c == lax.rem(r, 4) * 64 + lax.div(r, 4)

    cot_load.wait()
    stacked = jnp.concatenate([cot_ref[:, pl.ds(c * D, D)] for c in range(4)], axis=0)
    cslab[...] = matmul(one_hot(256, 256, shuffle), stacked).astype(BF16).reshape(SEQ, GROUP, D)
    slot = jnp.broadcast_to(lax.shift_right_logical(dest_ref[...], 6), (8, 64)).astype(F32).astype(BF16)
    to_row = matmul(slot, one_hot(64, 256, lambda r, c: r == lax.div(c, 4)))[0:1]
    to_col = matmul_t(one_hot(256, 64, lambda r, c: c == lax.div(r, 4)), slot)[:, 0:1]
    row_number = lax.broadcasted_iota(jnp.int32, (1, 256), 1)
    col_number = lax.broadcasted_iota(jnp.int32, (256, 1), 0)
    key_row = to_row.astype(jnp.int32) * GROUP + lax.rem(row_number, GROUP)
    key_col = to_col.astype(jnp.int32) * GROUP + lax.rem(col_number, GROUP)
    id_row, id_col = jnp.zeros((1, 256), F32), jnp.zeros((256, 1), F32)
    end = 0
    for j in range(3):
        end = end + len_ref[0, j] * GROUP
        id_row += jnp.where(row_number >= end, 1.0, 0.0)
        id_col += jnp.where(col_number >= end, 1.0, 0.0)
    ir = lax.broadcasted_iota(jnp.int32, (256, 256), 0)
    ic = lax.broadcasted_iota(jnp.int32, (256, 256), 1)
    perm = jnp.where(ir == key_row, 1.0, 0.0).astype(BF16)
    permt[...] = jnp.where(ic == key_col, 1.0, 0.0).astype(BF16)
    ids_k = jnp.sum(jnp.where(ir == key_row, id_row, 0.0), axis=1, keepdims=True)
    ids_q = jnp.sum(jnp.where(ic == key_col, id_col, 0.0), axis=0, keepdims=True)

    x_load.wait()
    out_load.wait()
    wide = matmul(perm, x_ref[...])
    xp[...] = wide.astype(BF16)
    centred = wide - jnp.mean(wide, axis=-1, keepdims=True)
    spread = lax.rsqrt(jnp.mean(centred * centred, axis=-1, keepdims=True) + eps)
    normed[...] = (centred * spread * gain_ref[...].reshape(1, D)).astype(BF16)

    presence.lines()
    gather = Gather(wout_ref, slots, wg, asem)
    gather.pair()

    def project(j):
        loads[j].wait()
        cols = pl.ds(j * D, D)
        part = matmul(normed[...], wqkv[:, cols]).astype(BF16)
        if j > 0:
            kv[:, pl.ds((j - 1) * D, D)] = part
        projt[cols, :] = part.T

    project(0)
    gather.along_z()
    presence.half_plane()
    project(1)
    project(2)
    presence.plane()
    gather.q_along_y()
    gather.p_along_y()
    exchange_start(cslab, crecv, csend, crecvs)
    same = ids_k == ids_q

    def attend(g):
        for h in range(8):
            first, width, off = WINDOWS[h]
            lanes = pl.ds(pl.multiple_of(g * HALF + first, 128), width)
            rows = pl.multiple_of(g * HALF + h * 80, 16)
            keys = kv[:, lanes] * lanes_of(width, off)
            scores = matmul(keys, projt[lanes, :]) * score_scale
            scores = jnp.where(same, scores, -jnp.inf)
            scores = jnp.exp(scores - jnp.max(scores, axis=0, keepdims=True))
            share = scores * (1.0 / jnp.sum(scores, axis=0, keepdims=True))
            probs[g * 8 + h] = share
            part = matmul(projt[pl.ds(2 * D + rows, 80), :], share.astype(BF16))
            at[pl.ds(rows, 80), pl.ds(0, 256)] = part.astype(BF16)
            gap = jnp.zeros((8, 256), F32)
            padded = jnp.concatenate([part[0:40], gap, part[40:80], gap], axis=0).astype(BF16)
            atp[pl.ds(pl.multiple_of(g * 768 + h * 96, 16), 96), :] = padded

    attend(0)
    gather.q_along_x()
    attend(1)
    scatter = Scatter(
        at, bg, dw_ref, (pair, wsum, wb, xa, yb, sa, sb, wa2, wb2, ya, xb, zs, zr, s3), ssem, norm_scale
    )
    scatter.send_attended()

    across = xp[...].T.astype(F32)
    across = across - jnp.mean(across, axis=0, keepdims=True)
    inv = lax.rsqrt(jnp.mean(across * across, axis=0, keepdims=True) + eps)
    std[...] = across * inv
    column = jnp.broadcast_to(gain_ref[...].reshape(1, D), (128, D)).T
    gaincol[:, 0:128] = column
    gaincol[:, 128:256] = column
    apad[...] = atp[...].T
    gather.p_pair()
    exchange_wait(cslab, crecv, csend, crecvs)
    bg[...] = crecv[...].reshape(256, D)
    scatter.send_grad()
    bgt[...] = bg[...].T
    scatter.product()
    gather.q_pair()
    gather.finish()
    for half in range(2):
        cols = pl.ds(half * HALF, HALF)
        branch = matmul(apad[...], wg[half].reshape(1536, HALF))
        block = (xp[:, cols].astype(F32) + branch).astype(BF16)
        tok[:, :, cols] = block.reshape(SEQ, GROUP, HALF)
    exchange_start(tok, got, tsend, trecvs)

    for i in range(4):
        part = matmul_t(wg[0, i // 2, pl.ds(2 * (i % 2), 2)].reshape(384, HALF), bg[:, pl.ds(0, HALF)])
        part += matmul_t(wg[1, i // 2, pl.ds(2 * (i % 2), 2)].reshape(384, HALF), bg[:, pl.ds(HALF, HALF)])
        for h in range(4):
            own = part[96 * h : 96 * h + 96]
            own = jnp.concatenate([own[0:40], own[48:88]], axis=0).astype(BF16)
            dat[pl.ds(i * 320 + 80 * h, 80), :] = own

    def back(g):
        for h in range(8):
            first, width, off = WINDOWS[h]
            lanes = pl.ds(pl.multiple_of(g * HALF + first, 128), width)
            rows = pl.multiple_of(g * HALF + h * 80, 16)
            values = kv[:, pl.ds(pl.multiple_of(D + g * HALF + first, 128), width)] * lanes_of(width, off)
            share = probs[g * 8 + h]
            gp = matmul(values, dat[lanes, :])
            delta = jnp.sum(gp * share, axis=0, keepdims=True)
            gs = (share * (gp - delta) * score_scale).astype(BF16)
            low = share.astype(BF16)
            gt[pl.ds(rows, 80), :] = matmul(projt[pl.ds(D + rows, 80), :], gs).astype(BF16)
            gt[pl.ds(D + rows, 80), :] = matmul_t(projt[pl.ds(rows, 80), :], gs).astype(BF16)
            gt[pl.ds(2 * D + rows, 80), :] = matmul_t(dat[pl.ds(rows, 80), :], low).astype(BF16)

    back(0)
    scatter.after_one()
    back(1)

    def grads(i):
        rows = pl.ds(i * HALF, HALF)
        part = matmul(wqkv[rows, :], gt[...])
        both = part * std[rows, :]
        both = both[:, 0:128] + both[:, 128:256]
        ghold[2, :, rows] = jnp.sum(both.T, axis=0, keepdims=True)
        scaled = part * gaincol[rows, :]
        gn[rows, :] = scaled
        return jnp.sum(scaled, axis=0, keepdims=True), jnp.sum(scaled * std[rows, :], axis=0, keepdims=True)

    low = grads(0)
    scatter.after_two()
    high = grads(1)
    presence.everybody()
    gains = GainSum(ghold, g1, g2, gsem)
    gains.first(ghold[2])
    mean_g = (low[0] + high[0]) * (1.0 / D)
    mean_gs = (low[1] + high[1]) * (1.0 / D)
    branch = inv * (gn[...] - mean_g - std[...] * mean_gs)
    total = (bgt[...].astype(F32) + branch).astype(BF16)
    gx_ref[...] = matmul_t(permt[...], total).astype(BF16)
    scatter.after_z()
    gains.second()
    exchange_wait(tok, got, tsend, trecvs)
    dg_ref[...] = gains.finish() * norm_scale
    scatter.finish()


def finish_kernel(got_ref, gx_in, dw_ref, dg_ref, merged_ref, gx_ref, own_ref, gain_out):
    ordered = matmul(
        one_hot(256, 256, lambda r, c: r == lax.rem(c, 4) * 64 + lax.div(c, 4)), got_ref[...].reshape(256, D)
    ).astype(BF16)
    for c in range(4):
        merged_ref[:, pl.ds(c * D, D)] = ordered[64 * c : 64 * c + 64]
    gx_ref[...] = gx_in[...]
    for part in range(2):
        for core in range(2):
            own = dw_ref[part, core].astype(F32)
            own_ref[pl.ds(10 * part, 10), pl.ds(core * HALF, HALF)] = own[0:10]
    first = lax.axis_index("seq") * 20
    turned = pltpu.roll(jnp.broadcast_to(dg_ref[...], (8, D)), lax.rem(D - first, D), 1)
    gain_out[...] = turned[0, 0:20]


def per_device(patches, lengths, token_dest, gain, w_qkv, w_out, cotangent):
    norm_scale = 1.0 / math.sqrt(256 * SEQ * NX)
    vmem = pl.BlockSpec(memory_space=pltpu.VMEM)
    hbm = pl.BlockSpec(memory_space=pl.ANY)
    smem = pl.BlockSpec(memory_space=pltpu.SMEM)

    def kernel(*refs):
        kernel_body(norm_scale, refs)

    got, gx, dw, dg = pl.pallas_call(
        kernel,
        out_shape=(
            jax.ShapeDtypeStruct((SEQ, GROUP, D), BF16),
            jax.ShapeDtypeStruct((256, D), BF16),
            jax.ShapeDtypeStruct((2, 2, 16, HALF), BF16),
            jax.ShapeDtypeStruct((1, D), F32),
        ),
        in_specs=[hbm, vmem, smem, vmem, hbm, hbm, hbm],
        out_specs=(hbm, vmem, vmem, vmem),
        scratch_shapes=[
            pltpu.VMEM((256, D), BF16),
            pltpu.VMEM((20, D), BF16),
            pltpu.VMEM((SEQ, GROUP * D), BF16),
            pltpu.VMEM((D, 3 * D), BF16),
            pltpu.VMEM((2, 32, D), BF16),
            pltpu.VMEM((2, 2, 4, NY, 48, HALF), BF16),
            pltpu.VMEM((SEQ, GROUP, D), BF16),
            pltpu.VMEM((SEQ, GROUP, D), BF16),
            pltpu.VMEM((SEQ, GROUP, D), BF16),
            pltpu.VMEM((256, D), BF16),
            pltpu.VMEM((256, D), BF16),
            pltpu.VMEM((256, 2 * D), BF16),
            pltpu.VMEM((3 * D, 256), BF16),
            pltpu.VMEM((256, 256), BF16),
            pltpu.VMEM((HEADS, 256, 256), F32),
            pltpu.VMEM((D, 512), BF16),
            pltpu.VMEM((1536, 256), BF16),
            pltpu.VMEM((256, 1536), BF16),
            pltpu.VMEM((256, D), BF16),
            pltpu.VMEM((D, 256), BF16),
            pltpu.VMEM((D, 256), BF16),
            pltpu.VMEM((3 * D, 256), BF16),
            pltpu.VMEM((D, 256), F32),
            pltpu.VMEM((D, 256), F32),
            pltpu.VMEM((512, HALF), BF16),
            pltpu.VMEM((NX, NY, 80, HALF), F32),
            pltpu.VMEM((NX, NY, 80, HALF), BF16),
            pltpu.VMEM((3, NY, 80, X_FIRST), BF16),
            pltpu.VMEM((3, NX, 80, HALF - X_FIRST), BF16),
            pltpu.VMEM((NY, 80, X_FIRST), F32),
            pltpu.VMEM((NX, 80, HALF - X_FIRST), F32),
            pltpu.VMEM((NY, 80, X_FIRST), BF16),
            pltpu.VMEM((NX, 80, HALF - X_FIRST), BF16),
            pltpu.VMEM((3, 80, X_FIRST), BF16),
            pltpu.VMEM((3, 80, HALF - X_FIRST), BF16),
            pltpu.VMEM((128, HALF), BF16),
            pltpu.VMEM((7, 16, HALF), BF16),
            pltpu.VMEM((16, HALF), BF16),
            pltpu.VMEM((3, 1, D), F32),
            pltpu.VMEM((15, 1, D), F32),
            pltpu.VMEM((15, 1, D), F32),
            pltpu.VMEM((D, 256), F32),
            pltpu.SemaphoreType.DMA((6,)),
            pltpu.SemaphoreType.REGULAR((3,)),
            pltpu.SemaphoreType.DMA((80,)),
            pltpu.SemaphoreType.DMA,
            pltpu.SemaphoreType.DMA,
            pltpu.SemaphoreType.DMA,
            pltpu.SemaphoreType.DMA,
            pltpu.SemaphoreType.DMA((72,)),
            pltpu.SemaphoreType.DMA((60,)),
        ],
        compiler_params=pltpu.CompilerParams(
            collective_id=0, has_side_effects=True, vmem_limit_bytes=LIMIT
        ),
    )(
        patches[0], token_dest, lengths[0], gain, w_qkv, w_out, cotangent[0],
    )
    merged, gx, own_weight, own_gain = pl.pallas_call(
        finish_kernel,
        out_shape=(
            jax.ShapeDtypeStruct((SEQ, GROUP * D), BF16),
            jax.ShapeDtypeStruct((256, D), BF16),
            jax.ShapeDtypeStruct((20, D), F32),
            jax.ShapeDtypeStruct((20,), F32),
        ),
        in_specs=[vmem] * 4,
        out_specs=(vmem,) * 4,
        compiler_params=pltpu.CompilerParams(vmem_limit_bytes=LIMIT),
    )(got, gx, dw, dg)
    return (merged[None], gx[None], own_weight, own_gain)


def solution(mesh):
    placed = (
        P("dp", "seq", None),
        P("dp", "seq", None),
        P("dp", "seq"),
        P(),
        P(),
        P("seq", None),
        P("dp", "seq", None),
    )
    return jax.shard_map(
        per_device,
        mesh=mesh,
        in_specs=placed,
        out_specs=(P("dp", "seq", None), P("dp", "seq", None), P("seq", None), P("seq")),
        check_vma=False,
    )
```

```python
import math

import jax
import jax.numpy as jnp
from jax import lax
from jax.experimental import pallas as pl
from jax.experimental.pallas import tpu as pltpu
from jax.sharding import PartitionSpec as P

HEADS = 16
GROUP = 4
D = 1280
HALF = 640
PLAIN = 128
X_FIRST = 384
NZ, NY, NX = 8, 4, 4
SEQ = 64
LIMIT = 56 * 2**20

eps = 1e-06
F32 = jnp.float32
BF16 = jnp.bfloat16


def place():
    seq = lax.axis_index("seq")
    x = lax.axis_index("dp")
    return seq, x, lax.div(seq, 8), lax.rem(lax.div(seq, 2), 4), lax.rem(seq, 2)


def seq_of(z, y, core):
    return z * 8 + y * 2 + core


def dev(seq, x):
    return {"seq": seq, "dp": x}


def remote(src, dst, send, recv, seq, x):
    return pltpu.make_async_remote_copy(
        src_ref=src,
        dst_ref=dst,
        send_sem=send,
        recv_sem=recv,
        device_id=dev(seq, x),
        device_id_type=pl.DeviceIdType.MESH,
    )


class Presence:
    def __init__(self, news):
        self.news = news

    def signal(self, sem, seq, x):
        pl.semaphore_signal(sem, inc=1, device_id=dev(seq, x), device_id_type=pl.DeviceIdType.MESH)

    def greet(self):
        seq, x, z, y, core = place()
        barrier = pltpu.get_barrier_semaphore()
        for k in range(1, NZ):
            self.signal(barrier, seq_of(lax.rem(z + k, NZ), y, core), x)
        for k in range(1, NY):
            self.signal(barrier, seq_of(z, lax.rem(y + k, NY), core), x)
        for k in range(1, NX):
            self.signal(barrier, seq, lax.rem(x + k, NX))
        self.signal(barrier, seq_of(z, y, 1 - core), x)

    def lines(self):
        seq, x, z, y, core = place()
        pl.semaphore_wait(pltpu.get_barrier_semaphore(), 14)
        for k in range(1, NY):
            self.signal(self.news.at[0], seq_of(z, lax.rem(y + k, NY), core), x)

    def half_plane(self):
        seq, x, z, y, core = place()
        pl.semaphore_wait(self.news.at[0], NY - 1)
        self.signal(self.news.at[1], seq_of(z, y, 1 - core), x)

    def plane(self):
        seq, x, z, y, core = place()
        pl.semaphore_wait(self.news.at[1], 1)
        for k in range(1, NX):
            self.signal(self.news.at[2], seq, lax.rem(x + k, NX))

    def everybody(self):
        pl.semaphore_wait(self.news.at[2], NX - 1)


def piece_of(x, z):
    return lax.rem(z - 2 * x + 3 + NZ, NZ)


def owner_of(x, y, z):
    piece = piece_of(x, z)
    return seq_of(2 * x + lax.div(piece, 4), y, lax.rem(lax.div(piece, 2), 2))


def exchange_start(src, dst, send, recv):
    seq, x, z, y, core = place()

    @pl.loop(1, SEQ)
    def _(k):
        to = lax.rem(seq + k, SEQ)
        remote(src.at[to], dst.at[seq], send, recv, to, x).start()

    pltpu.make_async_copy(src.at[seq], dst.at[seq], recv).start()


def exchange_wait(src, dst, send, recv):
    pltpu.make_async_copy(dst, dst, recv).wait()
    part = src.at[pl.ds(0, SEQ - 1)]
    pltpu.make_async_copy(part, part, send).wait()


def matmul(a, b):
    return jnp.dot(a, b, preferred_element_type=F32)


def matmul_t(a, b):
    return lax.dot_general(a, b, (((1,), (1,)), ((), ())), preferred_element_type=F32)


class Pool:
    def __init__(self, sems):
        self.sems, self.used = sems, 0

    def take(self):
        self.used += 1
        return self.sems.at[self.used - 1]


def one_hot(rows, columns, want):
    r = lax.broadcasted_iota(jnp.int32, (rows, columns), 0)
    c = lax.broadcasted_iota(jnp.int32, (rows, columns), 1)
    return jnp.where(want(r, c), 1.0, 0.0).astype(BF16)


WINDOWS = []
for _h in range(8):
    _first = 80 * _h // 128 * 128
    _off = 80 * _h - _first
    WINDOWS.append((_first, 128 if _off + 80 <= 128 else 256, _off))


def lanes_of(width, offset):
    lane = lax.broadcasted_iota(jnp.int32, (1, width), 1)
    return jnp.where((lane >= offset) & (lane < offset + 80), 1.0, 0.0).astype(BF16)


class Gather:
    def __init__(self, w_ref, slots, wg, sems):
        self.w_ref, self.slots, self.wg = w_ref, slots, wg
        self.pool = Pool(sems)
        self.p, self.q = pl.ds(0, PLAIN), pl.ds(PLAIN, HALF - PLAIN)

    def send(self, part, to, x):
        one = remote(part, part, self.pool.take(), self.pool.take(), to, x)
        one.start()
        return one

    def pair(self):
        seq, x, z, y, core = place()
        slots = self.slots
        own = jnp.concatenate([self.w_ref[...].astype(F32), jnp.zeros((12, D), F32)], axis=0)
        slots[core] = own.astype(BF16)
        self.first = self.send(slots.at[core], seq_of(z, y, 1 - core), x)

    def along_z(self):
        seq, x, z, y, core = place()
        slots, wg = self.slots, self.wg
        zh, zl = lax.div(z, 4), lax.rem(z, 4)
        self.first.wait()

        def want(r, c):
            return (c == jnp.where(r < 20, r, r + 12)) & (r < 40)

        first = pl.multiple_of(core * HALF, 128)
        rows = jnp.concatenate([slots[0, :, pl.ds(first, HALF)], slots[1, :, pl.ds(first, HALF)]], axis=0)
        own = matmul(one_hot(48, 64, want), rows).astype(BF16)
        wg[core, zh, zl, y, :, self.p] = own[:, 0:PLAIN]
        self.zsend = [self.pool.take() for _ in range(1, NZ)]
        both = self.pool.used
        self.zrecv = [self.pool.take() for _ in range(2)]

        @pl.when(zl == x)
        def _():
            wg[core, zh, zl, y, :, self.q] = own[:, PLAIN:HALF]
            part = wg.at[core, zh, zl, y, :, self.q]
            for k in range(1, NZ):
                to = seq_of(lax.rem(z + k, NZ), y, core)
                remote(part, part, self.zsend[k - 1], self.pool.sems.at[both + zh], to, x).start()

        part = wg.at[core, zh, zl, y, :, self.p]
        self.pz = [self.send(part, seq_of(lax.rem(z + k, NZ), y, core), x) for k in range(1, NZ)]

    def q_forward(self, k):
        seq, x, z, y, core = place()
        part = self.wg.at[core, :, x, lax.rem(y + NY - k, NY), :, self.q]
        self.qx.append([self.send(part, seq, lax.rem(x + j, NX)) for j in range(1, NX)])

    def q_along_y(self):
        seq, x, z, y, core = place()
        wg = self.wg
        for j in range(2):

            @pl.when(z != x + 4 * j)
            def _():
                part = wg.at[core, j, x, y, :, self.q]
                pltpu.make_async_copy(part, part, self.zrecv[j]).wait()

        part = wg.at[core, :, x, y, :, self.q]
        self.qy = [self.send(part, seq_of(z, lax.rem(y + k, NY), core), x) for k in range(1, NY)]
        self.qx = []
        self.q_forward(0)

    def p_to_pair(self, k):
        seq, x, z, y, core = place()
        part = self.wg.at[core, :, :, lax.rem(y + NY - k, NY), :, self.p]
        self.last.append(self.send(part, seq_of(z, y, 1 - core), x))

    def p_along_y(self):
        seq, x, z, y, core = place()
        for one in self.pz:
            one.wait()
        part = self.wg.at[core, :, :, y, :, self.p]
        self.py = [self.send(part, seq_of(z, lax.rem(y + k, NY), core), x) for k in range(1, NY)]
        self.last = []
        self.p_to_pair(0)

    def q_along_x(self):
        for k in range(1, NY):
            self.qy[k - 1].wait()
            self.q_forward(k)

    def p_pair(self):
        for k in range(1, NY):
            self.py[k - 1].wait()
            self.p_to_pair(k)

    def q_pair(self):
        seq, x, z, y, core = place()
        for k in range(NY):
            for one in self.qx[k]:
                one.wait()
            part = self.wg.at[core, :, :, lax.rem(y + NY - k, NY), :, self.q]
            self.last.append(self.send(part, seq_of(z, y, 1 - core), x))

    def finish(self):
        seq, x, z, y, core = place()
        for one in self.last:
            one.wait()

        @pl.when(lax.rem(z, 4) == x)
        def _():
            part = self.wg.at[core, 0, 0, 0, :, self.q]
            for k in range(1, NZ):
                pltpu.make_async_copy(part, part, self.zsend[k - 1]).wait()


class Scatter:
    def __init__(self, at_ref, bg_ref, out, bufs, sems, norm_scale):
        self.at_ref, self.bg_ref, self.out, self.bufs, self.sems = at_ref, bg_ref, out, bufs, sems
        self.pool = Pool(sems)
        self.norm_scale = norm_scale
        self.a, self.b = pl.ds(0, X_FIRST), pl.ds(X_FIRST, HALF - X_FIRST)

    def wait(self):
        for one in self.now:
            one.wait()

    def send(self, src, dst, to, x):
        one = remote(src, dst, self.pool.take(), self.pool.take(), to, x)
        one.start()
        return one

    def send_attended(self):
        seq, x, z, y, core = place()
        at = self.at_ref
        self.now = [self.send(at.at[:, pl.ds(0, 256)], at.at[:, pl.ds(256, 256)], seq_of(z, y, 1 - core), x)]

    def send_grad(self):
        seq, x, z, y, core = place()
        pair = self.bufs[0]
        theirs = pl.multiple_of((1 - core) * HALF, 128)
        src = self.bg_ref.at[:, pl.ds(theirs, HALF)]
        self.now.append(self.send(src, pair.at[pl.ds(256, 256)], seq_of(z, y, 1 - core), x))
        pair[pl.ds(0, 256), :] = self.bg_ref[:, pl.ds(pl.multiple_of(core * HALF, 128), HALF)]

    def product(self):
        pair, wsum, wb, xa, yb, sa, sb, wa2, wb2, ya, xb, zs, zr, s3 = self.bufs
        seq, x, z, y, core = place()
        self.wait()
        self.now = []
        for k in (1, 2, 3, 0):
            i = lax.rem(x + k, NX)
            rows = pl.ds(pl.multiple_of(i * 320, 64), 320)
            part = matmul(self.at_ref[rows, :], pair[...]).reshape(2, NY, 40, HALF)
            for j in range(NY):
                own = jnp.concatenate([part[0, j], part[1, j]], axis=0)
                wsum[i, j] = own
                wb[i, j] = own.astype(BF16)
            if k > 0:
                self.now.append(self.send(wb.at[i, :, :, self.a], xa.at[k - 1], seq, i))
            for j in range(1, NY):
                to = lax.rem(y + j, NY)
                self.now.append(self.send(wb.at[i, to, :, self.b], yb.at[j - 1, i], seq_of(z, to, core), x))

    def after_one(self):
        pair, wsum, wb, xa, yb, sa, sb, wa2, wb2, ya, xb, zs, zr, s3 = self.bufs
        seq, x, z, y, core = place()
        self.wait()

        @pl.loop(0, 4)
        def _(j):
            total = wsum[x, j, :, self.a]
            for k in range(3):
                total += xa[k, j].astype(F32)
            sa[j] = total
            wa2[j] = total.astype(BF16)
            total = wsum[j, y, :, self.b]
            for k in range(3):
                total += yb[k, j].astype(F32)
            sb[j] = total
            wb2[j] = total.astype(BF16)

        self.now = []
        for k in range(1, NY):
            to = lax.rem(y + k, NY)
            self.now.append(self.send(wa2.at[to], ya.at[k - 1], seq_of(z, to, core), x))
            to = lax.rem(x + k, NX)
            self.now.append(self.send(wb2.at[to], xb.at[k - 1], seq, to))

    def after_two(self):
        pair, wsum, wb, xa, yb, sa, sb, wa2, wb2, ya, xb, zs, zr, s3 = self.bufs
        seq, x, z, y, core = place()
        self.wait()
        total = sa[y]
        for k in range(3):
            total += ya[k].astype(F32)
        second = sb[x]
        for k in range(3):
            second += xb[k].astype(F32)

        def want(r, c):
            low = lax.rem(r, 16)
            return (c == lax.div(r, 16) * 10 + low) & (low < 10)

        chosen = one_hot(128, 80, want)
        zs[:, self.a] = matmul(chosen, total.astype(BF16)).astype(BF16)
        zs[:, self.b] = matmul(chosen, second.astype(BF16)).astype(BF16)
        self.now = []
        for k in range(1, NZ):
            to = lax.rem(z + k, NZ)
            src = zs.at[pl.ds(pl.multiple_of(piece_of(x, to) * 16, 16), 16)]
            self.now.append(self.send(src, zr.at[k - 1], seq_of(to, y, core), x))

    def after_z(self):
        zs, zr, s3 = self.bufs[-3:]
        seq, x, z, y, core = place()
        out = self.out
        self.wait()
        total = zs[pl.ds(pl.multiple_of(piece_of(x, z) * 16, 16), 16), :].astype(F32)
        for k in range(7):
            total += zr[k].astype(F32)
        s3[...] = (total * self.norm_scale).astype(BF16)
        owner = owner_of(x, y, z)
        slot = out.at[lax.rem(piece_of(x, z), 2), core]
        self.sent, self.got = self.pool.take(), self.pool.take()
        self.now = [
            remote(s3, slot, self.pool.take(), self.got, owner, lax.rem(x + k, NX)) for k in range(1, NX)
        ]
        for one in self.now:
            one.start()

        @pl.when(owner != seq)
        def _():
            remote(s3, slot, self.sent, self.got, owner, x).start()

        @pl.when(owner == seq)
        def _():
            pltpu.make_async_copy(s3, slot, self.got).start()

    def finish(self):
        seq, x, z, y, core = place()
        out, s3 = self.out, self.bufs[-1]
        for one in self.now:
            one.wait_send()

        @pl.when(owner_of(x, y, z) != seq)
        def _():
            pltpu.make_async_copy(s3, s3, self.sent).wait()

        pltpu.make_async_copy(out, out, self.got).wait()


class GainSum:
    def __init__(self, ghold, g1, g2, sems):
        self.ghold, self.g1, self.g2, self.sems = ghold, g1, g2, sems

    def first(self, total):
        seq, x, z, y, core = place()
        self.ghold[0] = total
        self.now = []
        for k in range(1, 16):
            kx, ky = k // 4, k % 4
            to = seq_of(z, lax.rem(y + ky, NY), core)
            self.now.append(
                remote(
                    self.ghold.at[0], self.g1.at[k - 1], self.sems.at[2 * k - 2], self.sems.at[2 * k - 1],
                    to, lax.rem(x + kx, NX),
                )
            )
        for one in self.now:
            one.start()

    def second(self):
        seq, x, z, y, core = place()
        for one in self.now:
            one.wait()
        total = self.ghold[0]
        for k in range(15):
            total += self.g1[k]
        self.ghold[1] = total
        self.now = []
        for k in range(1, 16):
            kz, kc = k // 2, k % 2
            to = seq_of(lax.rem(z + kz, NZ), y, lax.rem(core + kc, 2))
            self.now.append(
                remote(
                    self.ghold.at[1], self.g2.at[k - 1], self.sems.at[28 + 2 * k], self.sems.at[29 + 2 * k], to, x
                )
            )
        for one in self.now:
            one.start()

    def finish(self):
        for one in self.now:
            one.wait()
        total = self.ghold[1]
        for k in range(15):
            total += self.g2[k]
        return total


def kernel_body(norm_scale, refs):
    (x_hbm, dest_ref, len_ref, gain_ref, wqkv_hbm, wout_hbm, cot_hbm,
     got, gx_ref, dw_ref, dg_ref,
     x_ref, wout_ref, cot_ref, wqkv, slots, wg, cslab, crecv, tok, xp, normed, kv, projt, permt, probs, at, atp, apad, bg, bgt, dat, gt, gn, std, pair,
     wsum, wb, xa, yb, sa, sb, wa2, wb2, ya, xb, zs, zr, s3, ghold, g1, g2, gaincol,
     wsem, news, asem, csend, crecvs, tsend, trecvs, ssem, gsem) = refs
    score_scale = 1.0 / math.sqrt(80)

    cot_load = pltpu.make_async_copy(cot_hbm, cot_ref, wsem.at[3])
    x_load = pltpu.make_async_copy(x_hbm, x_ref, wsem.at[4])
    out_load = pltpu.make_async_copy(wout_hbm, wout_ref, wsem.at[5])
    for one in (cot_load, out_load, x_load):
        one.start()
    presence = Presence(news)
    presence.greet()
    loads = []
    for j in range(3):
        cols = pl.ds(j * D, D)
        loads.append(pltpu.make_async_copy(wqkv_hbm.at[:, cols], wqkv.at[:, cols], wsem.at[j]))
    for one in loads:
        one.start()

    def shuffle(r, c):
        return c == lax.rem(r, 4) * 64 + lax.div(r, 4)

    cot_load.wait()
    stacked = jnp.concatenate([cot_ref[:, pl.ds(c * D, D)] for c in range(4)], axis=0)
    cslab[...] = matmul(one_hot(256, 256, shuffle), stacked).astype(BF16).reshape(SEQ, GROUP, D)
    slot = jnp.broadcast_to(lax.shift_right_logical(dest_ref[...], 6), (8, 64)).astype(F32).astype(BF16)
    to_row = matmul(slot, one_hot(64, 256, lambda r, c: r == lax.div(c, 4)))[0:1]
    to_col = matmul_t(one_hot(256, 64, lambda r, c: c == lax.div(r, 4)), slot)[:, 0:1]
    row_number = lax.broadcasted_iota(jnp.int32, (1, 256), 1)
    col_number = lax.broadcasted_iota(jnp.int32, (256, 1), 0)
    key_row = to_row.astype(jnp.int32) * GROUP + lax.rem(row_number, GROUP)
    key_col = to_col.astype(jnp.int32) * GROUP + lax.rem(col_number, GROUP)
    id_row, id_col = jnp.zeros((1, 256), F32), jnp.zeros((256, 1), F32)
    end = 0
    for j in range(3):
        end = end + len_ref[0, j] * GROUP
        id_row += jnp.where(row_number >= end, 1.0, 0.0)
        id_col += jnp.where(col_number >= end, 1.0, 0.0)
    ir = lax.broadcasted_iota(jnp.int32, (256, 256), 0)
    ic = lax.broadcasted_iota(jnp.int32, (256, 256), 1)
    perm = jnp.where(ir == key_row, 1.0, 0.0).astype(BF16)
    permt[...] = jnp.where(ic == key_col, 1.0, 0.0).astype(BF16)
    ids_k = jnp.sum(jnp.where(ir == key_row, id_row, 0.0), axis=1, keepdims=True)
    ids_q = jnp.sum(jnp.where(ic == key_col, id_col, 0.0), axis=0, keepdims=True)

    x_load.wait()
    out_load.wait()
    wide = matmul(perm, x_ref[...])
    xp[...] = wide.astype(BF16)
    centred = wide - jnp.mean(wide, axis=-1, keepdims=True)
    spread = lax.rsqrt(jnp.mean(centred * centred, axis=-1, keepdims=True) + eps)
    normed[...] = (centred * spread * gain_ref[...].reshape(1, D)).astype(BF16)

    presence.lines()
    gather = Gather(wout_ref, slots, wg, asem)
    gather.pair()

    def project(j):
        loads[j].wait()
        cols = pl.ds(j * D, D)
        part = matmul(normed[...], wqkv[:, cols]).astype(BF16)
        if j > 0:
            kv[:, pl.ds((j - 1) * D, D)] = part
        projt[cols, :] = part.T

    project(0)
    gather.along_z()
    presence.half_plane()
    project(1)
    project(2)
    presence.plane()
    gather.q_along_y()
    gather.p_along_y()
    exchange_start(cslab, crecv, csend, crecvs)
    same = ids_k == ids_q

    def attend(g):
        for h in range(8):
            first, width, off = WINDOWS[h]
            lanes = pl.ds(pl.multiple_of(g * HALF + first, 128), width)
            rows = pl.multiple_of(g * HALF + h * 80, 16)
            keys = kv[:, lanes] * lanes_of(width, off)
            scores = matmul(keys, projt[lanes, :]) * score_scale
            scores = jnp.where(same, scores, -jnp.inf)
            scores = jnp.exp(scores - jnp.max(scores, axis=0, keepdims=True))
            share = scores * (1.0 / jnp.sum(scores, axis=0, keepdims=True))
            probs[g * 8 + h] = share
            part = matmul(projt[pl.ds(2 * D + rows, 80), :], share.astype(BF16))
            at[pl.ds(rows, 80), pl.ds(0, 256)] = part.astype(BF16)
            gap = jnp.zeros((8, 256), F32)
            padded = jnp.concatenate([part[0:40], gap, part[40:80], gap], axis=0).astype(BF16)
            atp[pl.ds(pl.multiple_of(g * 768 + h * 96, 16), 96), :] = padded

    attend(0)
    gather.q_along_x()
    attend(1)
    scatter = Scatter(
        at, bg, dw_ref, (pair, wsum, wb, xa, yb, sa, sb, wa2, wb2, ya, xb, zs, zr, s3), ssem, norm_scale
    )
    scatter.send_attended()

    across = xp[...].T.astype(F32)
    across = across - jnp.mean(across, axis=0, keepdims=True)
    inv = lax.rsqrt(jnp.mean(across * across, axis=0, keepdims=True) + eps)
    std[...] = across * inv
    column = jnp.broadcast_to(gain_ref[...].reshape(1, D), (128, D)).T
    gaincol[:, 0:128] = column
    gaincol[:, 128:256] = column
    apad[...] = atp[...].T
    gather.p_pair()
    exchange_wait(cslab, crecv, csend, crecvs)
    bg[...] = crecv[...].reshape(256, D)
    scatter.send_grad()
    bgt[...] = bg[...].T
    scatter.product()
    gather.q_pair()
    gather.finish()
    for half in range(2):
        cols = pl.ds(half * HALF, HALF)
        branch = matmul(apad[...], wg[half].reshape(1536, HALF))
        block = (xp[:, cols].astype(F32) + branch).astype(BF16)
        tok[:, :, cols] = block.reshape(SEQ, GROUP, HALF)
    exchange_start(tok, got, tsend, trecvs)

    for i in range(4):
        part = matmul_t(wg[0, i // 2, pl.ds(2 * (i % 2), 2)].reshape(384, HALF), bg[:, pl.ds(0, HALF)])
        part += matmul_t(wg[1, i // 2, pl.ds(2 * (i % 2), 2)].reshape(384, HALF), bg[:, pl.ds(HALF, HALF)])
        for h in range(4):
            own = part[96 * h : 96 * h + 96]
            own = jnp.concatenate([own[0:40], own[48:88]], axis=0).astype(BF16)
            dat[pl.ds(i * 320 + 80 * h, 80), :] = own

    def back(g):
        for h in range(8):
            first, width, off = WINDOWS[h]
            lanes = pl.ds(pl.multiple_of(g * HALF + first, 128), width)
            rows = pl.multiple_of(g * HALF + h * 80, 16)
            values = kv[:, pl.ds(pl.multiple_of(D + g * HALF + first, 128), width)] * lanes_of(width, off)
            share = probs[g * 8 + h]
            gp = matmul(values, dat[lanes, :])
            delta = jnp.sum(gp * share, axis=0, keepdims=True)
            gs = (share * (gp - delta) * score_scale).astype(BF16)
            low = share.astype(BF16)
            gt[pl.ds(rows, 80), :] = matmul(projt[pl.ds(D + rows, 80), :], gs).astype(BF16)
            gt[pl.ds(D + rows, 80), :] = matmul_t(projt[pl.ds(rows, 80), :], gs).astype(BF16)
            gt[pl.ds(2 * D + rows, 80), :] = matmul_t(dat[pl.ds(rows, 80), :], low).astype(BF16)

    back(0)
    back(1)
    scatter.after_one()

    def grads(i):
        rows = pl.ds(i * HALF, HALF)
        part = matmul(wqkv[rows, :], gt[...])
        both = part * std[rows, :]
        both = both[:, 0:128] + both[:, 128:256]
        ghold[2, :, rows] = jnp.sum(both.T, axis=0, keepdims=True)
        scaled = part * gaincol[rows, :]
        gn[rows, :] = scaled
        return jnp.sum(scaled, axis=0, keepdims=True), jnp.sum(scaled * std[rows, :], axis=0, keepdims=True)

    low = grads(0)
    high = grads(1)
    presence.everybody()
    gains = GainSum(ghold, g1, g2, gsem)
    gains.first(ghold[2])
    scatter.after_two()
    mean_g = (low[0] + high[0]) * (1.0 / D)
    mean_gs = (low[1] + high[1]) * (1.0 / D)
    branch = inv * (gn[...] - mean_g - std[...] * mean_gs)
    total = (bgt[...].astype(F32) + branch).astype(BF16)
    gx_ref[...] = matmul_t(permt[...], total).astype(BF16)
    gains.second()
    scatter.after_z()
    exchange_wait(tok, got, tsend, trecvs)
    dg_ref[...] = gains.finish() * norm_scale
    scatter.finish()


def finish_kernel(got_ref, gx_in, dw_ref, dg_ref, merged_ref, gx_ref, own_ref, gain_out):
    ordered = matmul(
        one_hot(256, 256, lambda r, c: r == lax.rem(c, 4) * 64 + lax.div(c, 4)), got_ref[...].reshape(256, D)
    ).astype(BF16)
    for c in range(4):
        merged_ref[:, pl.ds(c * D, D)] = ordered[64 * c : 64 * c + 64]
    gx_ref[...] = gx_in[...]
    for part in range(2):
        for core in range(2):
            own = dw_ref[part, core].astype(F32)
            own_ref[pl.ds(10 * part, 10), pl.ds(core * HALF, HALF)] = own[0:10]
    first = lax.axis_index("seq") * 20
    turned = pltpu.roll(jnp.broadcast_to(dg_ref[...], (8, D)), lax.rem(D - first, D), 1)
    gain_out[...] = turned[0, 0:20]


def per_device(patches, lengths, token_dest, gain, w_qkv, w_out, cotangent):
    norm_scale = 1.0 / math.sqrt(256 * SEQ * NX)
    vmem = pl.BlockSpec(memory_space=pltpu.VMEM)
    hbm = pl.BlockSpec(memory_space=pl.ANY)
    smem = pl.BlockSpec(memory_space=pltpu.SMEM)

    def kernel(*refs):
        kernel_body(norm_scale, refs)

    got, gx, dw, dg = pl.pallas_call(
        kernel,
        out_shape=(
            jax.ShapeDtypeStruct((SEQ, GROUP, D), BF16),
            jax.ShapeDtypeStruct((256, D), BF16),
            jax.ShapeDtypeStruct((2, 2, 16, HALF), BF16),
            jax.ShapeDtypeStruct((1, D), F32),
        ),
        in_specs=[hbm, vmem, smem, vmem, hbm, hbm, hbm],
        out_specs=(hbm, vmem, vmem, vmem),
        scratch_shapes=[
            pltpu.VMEM((256, D), BF16),
            pltpu.VMEM((20, D), BF16),
            pltpu.VMEM((SEQ, GROUP * D), BF16),
            pltpu.VMEM((D, 3 * D), BF16),
            pltpu.VMEM((2, 32, D), BF16),
            pltpu.VMEM((2, 2, 4, NY, 48, HALF), BF16),
            pltpu.VMEM((SEQ, GROUP, D), BF16),
            pltpu.VMEM((SEQ, GROUP, D), BF16),
            pltpu.VMEM((SEQ, GROUP, D), BF16),
            pltpu.VMEM((256, D), BF16),
            pltpu.VMEM((256, D), BF16),
            pltpu.VMEM((256, 2 * D), BF16),
            pltpu.VMEM((3 * D, 256), BF16),
            pltpu.VMEM((256, 256), BF16),
            pltpu.VMEM((HEADS, 256, 256), F32),
            pltpu.VMEM((D, 512), BF16),
            pltpu.VMEM((1536, 256), BF16),
            pltpu.VMEM((256, 1536), BF16),
            pltpu.VMEM((256, D), BF16),
            pltpu.VMEM((D, 256), BF16),
            pltpu.VMEM((D, 256), BF16),
            pltpu.VMEM((3 * D, 256), BF16),
            pltpu.VMEM((D, 256), F32),
            pltpu.VMEM((D, 256), F32),
            pltpu.VMEM((512, HALF), BF16),
            pltpu.VMEM((NX, NY, 80, HALF), F32),
            pltpu.VMEM((NX, NY, 80, HALF), BF16),
            pltpu.VMEM((3, NY, 80, X_FIRST), BF16),
            pltpu.VMEM((3, NX, 80, HALF - X_FIRST), BF16),
            pltpu.VMEM((NY, 80, X_FIRST), F32),
            pltpu.VMEM((NX, 80, HALF - X_FIRST), F32),
            pltpu.VMEM((NY, 80, X_FIRST), BF16),
            pltpu.VMEM((NX, 80, HALF - X_FIRST), BF16),
            pltpu.VMEM((3, 80, X_FIRST), BF16),
            pltpu.VMEM((3, 80, HALF - X_FIRST), BF16),
            pltpu.VMEM((128, HALF), BF16),
            pltpu.VMEM((7, 16, HALF), BF16),
            pltpu.VMEM((16, HALF), BF16),
            pltpu.VMEM((3, 1, D), F32),
            pltpu.VMEM((15, 1, D), F32),
            pltpu.VMEM((15, 1, D), F32),
            pltpu.VMEM((D, 256), F32),
            pltpu.SemaphoreType.DMA((6,)),
            pltpu.SemaphoreType.REGULAR((3,)),
            pltpu.SemaphoreType.DMA((80,)),
            pltpu.SemaphoreType.DMA,
            pltpu.SemaphoreType.DMA,
            pltpu.SemaphoreType.DMA,
            pltpu.SemaphoreType.DMA,
            pltpu.SemaphoreType.DMA((72,)),
            pltpu.SemaphoreType.DMA((60,)),
        ],
        compiler_params=pltpu.CompilerParams(
            collective_id=0, has_side_effects=True, vmem_limit_bytes=LIMIT
        ),
    )(
        patches[0], token_dest, lengths[0], gain, w_qkv, w_out, cotangent[0],
    )
    merged, gx, own_weight, own_gain = pl.pallas_call(
        finish_kernel,
        out_shape=(
            jax.ShapeDtypeStruct((SEQ, GROUP * D), BF16),
            jax.ShapeDtypeStruct((256, D), BF16),
            jax.ShapeDtypeStruct((20, D), F32),
            jax.ShapeDtypeStruct((20,), F32),
        ),
        in_specs=[vmem] * 4,
        out_specs=(vmem,) * 4,
        compiler_params=pltpu.CompilerParams(vmem_limit_bytes=LIMIT),
    )(got, gx, dw, dg)
    return (merged[None], gx[None], own_weight, own_gain)


def solution(mesh):
    placed = (
        P("dp", "seq", None),
        P("dp", "seq", None),
        P("dp", "seq"),
        P(),
        P(),
        P("seq", None),
        P("dp", "seq", None),
    )
    return jax.shard_map(
        per_device,
        mesh=mesh,
        in_specs=placed,
        out_specs=(P("dp", "seq", None), P("dp", "seq", None), P("seq", None), P("seq")),
        check_vma=False,
    )
```

```python
import math

import jax
import jax.numpy as jnp
from jax import lax
from jax.experimental import pallas as pl
from jax.experimental.pallas import tpu as pltpu
from jax.sharding import PartitionSpec as P

HEADS = 16
GROUP = 4
D = 1280
HALF = 640
PLAIN = 128
X_FIRST = 384
NZ, NY, NX = 8, 4, 4
SEQ = 64
LIMIT = 56 * 2**20

eps = 1e-06
F32 = jnp.float32
BF16 = jnp.bfloat16


def place():
    seq = lax.axis_index("seq")
    x = lax.axis_index("dp")
    return seq, x, lax.div(seq, 8), lax.rem(lax.div(seq, 2), 4), lax.rem(seq, 2)


def seq_of(z, y, core):
    return z * 8 + y * 2 + core


def dev(seq, x):
    return {"seq": seq, "dp": x}


def remote(src, dst, send, recv, seq, x):
    return pltpu.make_async_remote_copy(
        src_ref=src,
        dst_ref=dst,
        send_sem=send,
        recv_sem=recv,
        device_id=dev(seq, x),
        device_id_type=pl.DeviceIdType.MESH,
    )


class Presence:
    def __init__(self, news):
        self.news = news

    def signal(self, sem, seq, x):
        pl.semaphore_signal(sem, inc=1, device_id=dev(seq, x), device_id_type=pl.DeviceIdType.MESH)

    def greet(self):
        seq, x, z, y, core = place()
        barrier = pltpu.get_barrier_semaphore()
        for k in range(1, NZ):
            self.signal(barrier, seq_of(lax.rem(z + k, NZ), y, core), x)
        for k in range(1, NY):
            self.signal(barrier, seq_of(z, lax.rem(y + k, NY), core), x)
        for k in range(1, NX):
            self.signal(barrier, seq, lax.rem(x + k, NX))
        self.signal(barrier, seq_of(z, y, 1 - core), x)

    def lines(self):
        seq, x, z, y, core = place()
        pl.semaphore_wait(pltpu.get_barrier_semaphore(), 14)
        for k in range(1, NY):
            self.signal(self.news.at[0], seq_of(z, lax.rem(y + k, NY), core), x)

    def half_plane(self):
        seq, x, z, y, core = place()
        pl.semaphore_wait(self.news.at[0], NY - 1)
        self.signal(self.news.at[1], seq_of(z, y, 1 - core), x)

    def plane(self):
        seq, x, z, y, core = place()
        pl.semaphore_wait(self.news.at[1], 1)
        for k in range(1, NX):
            self.signal(self.news.at[2], seq, lax.rem(x + k, NX))

    def everybody(self):
        pl.semaphore_wait(self.news.at[2], NX - 1)


def piece_of(x, z):
    return lax.rem(z - 2 * x + 3 + NZ, NZ)


def owner_of(x, y, z):
    piece = piece_of(x, z)
    return seq_of(2 * x + lax.div(piece, 4), y, lax.rem(lax.div(piece, 2), 2))


def exchange_start(src, dst, send, recv):
    seq, x, z, y, core = place()
    ways = [(kz, ky, kc) for kz in range(NZ) for ky in range(NY) for kc in range(2)][1:]
    ways.sort(key=lambda way: -min(way[0], NZ - way[0]) - min(way[1], NY - way[1]))
    for kz, ky, kc in ways:
        to = seq_of(lax.rem(z + kz, NZ), lax.rem(y + ky, NY), lax.rem(core + kc, 2))
        remote(src.at[to], dst.at[seq], send, recv, to, x).start()
    pltpu.make_async_copy(src.at[seq], dst.at[seq], recv).start()


def exchange_wait(src, dst, send, recv):
    pltpu.make_async_copy(dst, dst, recv).wait()
    part = src.at[pl.ds(0, SEQ - 1)]
    pltpu.make_async_copy(part, part, send).wait()


def matmul(a, b):
    return jnp.dot(a, b, preferred_element_type=F32)


def matmul_t(a, b):
    return lax.dot_general(a, b, (((1,), (1,)), ((), ())), preferred_element_type=F32)


class Pool:
    def __init__(self, sems):
        self.sems, self.used = sems, 0

    def take(self):
        self.used += 1
        return self.sems.at[self.used - 1]


def one_hot(rows, columns, want):
    r = lax.broadcasted_iota(jnp.int32, (rows, columns), 0)
    c = lax.broadcasted_iota(jnp.int32, (rows, columns), 1)
    return jnp.where(want(r, c), 1.0, 0.0).astype(BF16)


WINDOWS = []
for _h in range(8):
    _first = 80 * _h // 128 * 128
    _off = 80 * _h - _first
    WINDOWS.append((_first, 128 if _off + 80 <= 128 else 256, _off))


def lanes_of(width, offset):
    lane = lax.broadcasted_iota(jnp.int32, (1, width), 1)
    return jnp.where((lane >= offset) & (lane < offset + 80), 1.0, 0.0).astype(BF16)


class Gather:
    def __init__(self, w_ref, slots, wg, sems):
        self.w_ref, self.slots, self.wg = w_ref, slots, wg
        self.pool = Pool(sems)
        self.p, self.q = pl.ds(0, PLAIN), pl.ds(PLAIN, HALF - PLAIN)

    def send(self, part, to, x):
        one = remote(part, part, self.pool.take(), self.pool.take(), to, x)
        one.start()
        return one

    def pair(self):
        seq, x, z, y, core = place()
        slots = self.slots
        own = jnp.concatenate([self.w_ref[...].astype(F32), jnp.zeros((12, D), F32)], axis=0)
        slots[core] = own.astype(BF16)
        self.first = self.send(slots.at[core], seq_of(z, y, 1 - core), x)

    def along_z(self):
        seq, x, z, y, core = place()
        slots, wg = self.slots, self.wg
        zh, zl = lax.div(z, 4), lax.rem(z, 4)
        self.first.wait()

        def want(r, c):
            return (c == jnp.where(r < 20, r, r + 12)) & (r < 40)

        first = pl.multiple_of(core * HALF, 128)
        rows = jnp.concatenate([slots[0, :, pl.ds(first, HALF)], slots[1, :, pl.ds(first, HALF)]], axis=0)
        own = matmul(one_hot(48, 64, want), rows).astype(BF16)
        wg[core, zh, zl, y, :, self.p] = own[:, 0:PLAIN]
        self.zsend = [self.pool.take() for _ in range(1, NZ)]
        both = self.pool.used
        self.zrecv = [self.pool.take() for _ in range(2)]

        @pl.when(zl == x)
        def _():
            wg[core, zh, zl, y, :, self.q] = own[:, PLAIN:HALF]
            part = wg.at[core, zh, zl, y, :, self.q]
            for k in range(1, NZ):
                to = seq_of(lax.rem(z + k, NZ), y, core)
                remote(part, part, self.zsend[k - 1], self.pool.sems.at[both + zh], to, x).start()

        part = wg.at[core, zh, zl, y, :, self.p]
        self.pz = [self.send(part, seq_of(lax.rem(z + k, NZ), y, core), x) for k in range(1, NZ)]

    def q_forward(self, k):
        seq, x, z, y, core = place()
        part = self.wg.at[core, :, x, lax.rem(y + NY - k, NY), :, self.q]
        self.qx.append([self.send(part, seq, lax.rem(x + j, NX)) for j in range(1, NX)])

    def q_along_y(self):
        seq, x, z, y, core = place()
        wg = self.wg
        for j in range(2):

            @pl.when(z != x + 4 * j)
            def _():
                part = wg.at[core, j, x, y, :, self.q]
                pltpu.make_async_copy(part, part, self.zrecv[j]).wait()

        part = wg.at[core, :, x, y, :, self.q]
        self.qy = [self.send(part, seq_of(z, lax.rem(y + k, NY), core), x) for k in range(1, NY)]
        self.qx = []
        self.q_forward(0)

    def p_to_pair(self, k):
        seq, x, z, y, core = place()
        part = self.wg.at[core, :, :, lax.rem(y + NY - k, NY), :, self.p]
        self.last.append(self.send(part, seq_of(z, y, 1 - core), x))

    def p_along_y(self):
        seq, x, z, y, core = place()
        for one in self.pz:
            one.wait()
        part = self.wg.at[core, :, :, y, :, self.p]
        self.py = [self.send(part, seq_of(z, lax.rem(y + k, NY), core), x) for k in range(1, NY)]
        self.last = []
        self.p_to_pair(0)

    def q_along_x(self):
        for k in range(1, NY):
            self.qy[k - 1].wait()
            self.q_forward(k)

    def p_pair(self):
        for k in range(1, NY):
            self.py[k - 1].wait()
            self.p_to_pair(k)

    def q_pair(self):
        seq, x, z, y, core = place()
        for k in range(NY):
            for one in self.qx[k]:
                one.wait()
            part = self.wg.at[core, :, :, lax.rem(y + NY - k, NY), :, self.q]
            self.last.append(self.send(part, seq_of(z, y, 1 - core), x))

    def finish(self):
        seq, x, z, y, core = place()
        for one in self.last:
            one.wait()

        @pl.when(lax.rem(z, 4) == x)
        def _():
            part = self.wg.at[core, 0, 0, 0, :, self.q]
            for k in range(1, NZ):
                pltpu.make_async_copy(part, part, self.zsend[k - 1]).wait()


class Scatter:
    def __init__(self, at_ref, bg_ref, out, bufs, sems, norm_scale):
        self.at_ref, self.bg_ref, self.out, self.bufs, self.sems = at_ref, bg_ref, out, bufs, sems
        self.pool = Pool(sems)
        self.norm_scale = norm_scale
        self.a, self.b = pl.ds(0, X_FIRST), pl.ds(X_FIRST, HALF - X_FIRST)

    def wait(self):
        for one in self.now:
            one.wait()

    def send(self, src, dst, to, x):
        one = remote(src, dst, self.pool.take(), self.pool.take(), to, x)
        one.start()
        return one

    def send_attended(self):
        seq, x, z, y, core = place()
        at = self.at_ref
        self.now = [self.send(at.at[:, pl.ds(0, 256)], at.at[:, pl.ds(256, 256)], seq_of(z, y, 1 - core), x)]

    def send_grad(self):
        seq, x, z, y, core = place()
        pair = self.bufs[0]
        theirs = pl.multiple_of((1 - core) * HALF, 128)
        src = self.bg_ref.at[:, pl.ds(theirs, HALF)]
        self.now.append(self.send(src, pair.at[pl.ds(256, 256)], seq_of(z, y, 1 - core), x))
        pair[pl.ds(0, 256), :] = self.bg_ref[:, pl.ds(pl.multiple_of(core * HALF, 128), HALF)]

    def product(self):
        pair, wsum, wb, xa, yb, sa, sb, wa2, wb2, ya, xb, zs, zr, s3 = self.bufs
        seq, x, z, y, core = place()
        self.wait()
        self.now = []
        for k in (1, 2, 3, 0):
            i = lax.rem(x + k, NX)
            rows = pl.ds(pl.multiple_of(i * 320, 64), 320)
            part = matmul(self.at_ref[rows, :], pair[...]).reshape(2, NY, 40, HALF)
            for j in range(NY):
                own = jnp.concatenate([part[0, j], part[1, j]], axis=0)
                wsum[i, j] = own
                wb[i, j] = own.astype(BF16)
            if k > 0:
                self.now.append(self.send(wb.at[i, :, :, self.a], xa.at[k - 1], seq, i))
            for j in range(1, NY):
                to = lax.rem(y + j, NY)
                self.now.append(self.send(wb.at[i, to, :, self.b], yb.at[j - 1, i], seq_of(z, to, core), x))

    def after_one(self):
        pair, wsum, wb, xa, yb, sa, sb, wa2, wb2, ya, xb, zs, zr, s3 = self.bufs
        seq, x, z, y, core = place()
        self.wait()

        @pl.loop(0, 4)
        def _(j):
            total = wsum[x, j, :, self.a]
            for k in range(3):
                total += xa[k, j].astype(F32)
            sa[j] = total
            wa2[j] = total.astype(BF16)
            total = wsum[j, y, :, self.b]
            for k in range(3):
                total += yb[k, j].astype(F32)
            sb[j] = total
            wb2[j] = total.astype(BF16)

        self.now = []
        for k in range(1, NY):
            to = lax.rem(y + k, NY)
            self.now.append(self.send(wa2.at[to], ya.at[k - 1], seq_of(z, to, core), x))
            to = lax.rem(x + k, NX)
            self.now.append(self.send(wb2.at[to], xb.at[k - 1], seq, to))

    def after_two(self):
        pair, wsum, wb, xa, yb, sa, sb, wa2, wb2, ya, xb, zs, zr, s3 = self.bufs
        seq, x, z, y, core = place()
        self.wait()
        total = sa[y]
        for k in range(3):
            total += ya[k].astype(F32)
        second = sb[x]
        for k in range(3):
            second += xb[k].astype(F32)

        def want(r, c):
            low = lax.rem(r, 16)
            return (c == lax.div(r, 16) * 10 + low) & (low < 10)

        chosen = one_hot(128, 80, want)
        zs[:, self.a] = matmul(chosen, total.astype(BF16)).astype(BF16)
        zs[:, self.b] = matmul(chosen, second.astype(BF16)).astype(BF16)
        self.now = []
        for k in range(1, NZ):
            to = lax.rem(z + k, NZ)
            src = zs.at[pl.ds(pl.multiple_of(piece_of(x, to) * 16, 16), 16)]
            self.now.append(self.send(src, zr.at[k - 1], seq_of(to, y, core), x))

    def after_z(self):
        zs, zr, s3 = self.bufs[-3:]
        seq, x, z, y, core = place()
        out = self.out
        self.wait()
        total = zs[pl.ds(pl.multiple_of(piece_of(x, z) * 16, 16), 16), :].astype(F32)
        for k in range(7):
            total += zr[k].astype(F32)
        s3[...] = (total * self.norm_scale).astype(BF16)
        owner = owner_of(x, y, z)
        slot = out.at[lax.rem(piece_of(x, z), 2), core]
        self.sent, self.got = self.pool.take(), self.pool.take()
        self.now = [
            remote(s3, slot, self.pool.take(), self.got, owner, lax.rem(x + k, NX)) for k in range(1, NX)
        ]
        for one in self.now:
            one.start()

        @pl.when(owner != seq)
        def _():
            remote(s3, slot, self.sent, self.got, owner, x).start()

        @pl.when(owner == seq)
        def _():
            pltpu.make_async_copy(s3, slot, self.got).start()

    def finish(self):
        seq, x, z, y, core = place()
        out, s3 = self.out, self.bufs[-1]
        for one in self.now:
            one.wait_send()

        @pl.when(owner_of(x, y, z) != seq)
        def _():
            pltpu.make_async_copy(s3, s3, self.sent).wait()

        pltpu.make_async_copy(out, out, self.got).wait()


class GainSum:
    def __init__(self, ghold, g1, g2, sems):
        self.ghold, self.g1, self.g2, self.sems = ghold, g1, g2, sems

    def first(self, total):
        seq, x, z, y, core = place()
        self.ghold[0] = total
        self.now = []
        for k in range(1, 16):
            kx, ky = k // 4, k % 4
            to = seq_of(z, lax.rem(y + ky, NY), core)
            self.now.append(
                remote(
                    self.ghold.at[0], self.g1.at[k - 1], self.sems.at[2 * k - 2], self.sems.at[2 * k - 1],
                    to, lax.rem(x + kx, NX),
                )
            )
        for one in self.now:
            one.start()

    def second(self):
        seq, x, z, y, core = place()
        for one in self.now:
            one.wait()
        total = self.ghold[0]
        for k in range(15):
            total += self.g1[k]
        self.ghold[1] = total
        self.now = []
        for k in range(1, 16):
            kz, kc = k // 2, k % 2
            to = seq_of(lax.rem(z + kz, NZ), y, lax.rem(core + kc, 2))
            self.now.append(
                remote(
                    self.ghold.at[1], self.g2.at[k - 1], self.sems.at[28 + 2 * k], self.sems.at[29 + 2 * k], to, x
                )
            )
        for one in self.now:
            one.start()

    def finish(self):
        for one in self.now:
            one.wait()
        total = self.ghold[1]
        for k in range(15):
            total += self.g2[k]
        return total


def kernel_body(norm_scale, refs):
    (x_hbm, dest_ref, len_ref, gain_ref, wqkv_hbm, wout_hbm, cot_hbm,
     got, gx_ref, dw_ref, dg_ref,
     x_ref, wout_ref, cot_ref, wqkv, slots, wg, cslab, crecv, tok, xp, normed, kv, projt, permt, probs, at, atp, apad, bg, bgt, dat, gt, gn, std, pair,
     wsum, wb, xa, yb, sa, sb, wa2, wb2, ya, xb, zs, zr, s3, ghold, g1, g2, gaincol,
     wsem, news, asem, csend, crecvs, tsend, trecvs, ssem, gsem) = refs
    score_scale = 1.0 / math.sqrt(80)

    cot_load = pltpu.make_async_copy(cot_hbm, cot_ref, wsem.at[3])
    x_load = pltpu.make_async_copy(x_hbm, x_ref, wsem.at[4])
    out_load = pltpu.make_async_copy(wout_hbm, wout_ref, wsem.at[5])
    for one in (cot_load, out_load, x_load):
        one.start()
    presence = Presence(news)
    presence.greet()
    loads = []
    for j in range(3):
        cols = pl.ds(j * D, D)
        loads.append(pltpu.make_async_copy(wqkv_hbm.at[:, cols], wqkv.at[:, cols], wsem.at[j]))
    for one in loads:
        one.start()

    def shuffle(r, c):
        return c == lax.rem(r, 4) * 64 + lax.div(r, 4)

    cot_load.wait()
    stacked = jnp.concatenate([cot_ref[:, pl.ds(c * D, D)] for c in range(4)], axis=0)
    cslab[...] = matmul(one_hot(256, 256, shuffle), stacked).astype(BF16).reshape(SEQ, GROUP, D)
    slot = jnp.broadcast_to(lax.shift_right_logical(dest_ref[...], 6), (8, 64)).astype(F32).astype(BF16)
    to_row = matmul(slot, one_hot(64, 256, lambda r, c: r == lax.div(c, 4)))[0:1]
    to_col = matmul_t(one_hot(256, 64, lambda r, c: c == lax.div(r, 4)), slot)[:, 0:1]
    row_number = lax.broadcasted_iota(jnp.int32, (1, 256), 1)
    col_number = lax.broadcasted_iota(jnp.int32, (256, 1), 0)
    key_row = to_row.astype(jnp.int32) * GROUP + lax.rem(row_number, GROUP)
    key_col = to_col.astype(jnp.int32) * GROUP + lax.rem(col_number, GROUP)
    id_row, id_col = jnp.zeros((1, 256), F32), jnp.zeros((256, 1), F32)
    end = 0
    for j in range(3):
        end = end + len_ref[0, j] * GROUP
        id_row += jnp.where(row_number >= end, 1.0, 0.0)
        id_col += jnp.where(col_number >= end, 1.0, 0.0)
    ir = lax.broadcasted_iota(jnp.int32, (256, 256), 0)
    ic = lax.broadcasted_iota(jnp.int32, (256, 256), 1)
    perm = jnp.where(ir == key_row, 1.0, 0.0).astype(BF16)
    permt[...] = jnp.where(ic == key_col, 1.0, 0.0).astype(BF16)
    ids_k = jnp.sum(jnp.where(ir == key_row, id_row, 0.0), axis=1, keepdims=True)
    ids_q = jnp.sum(jnp.where(ic == key_col, id_col, 0.0), axis=0, keepdims=True)

    x_load.wait()
    out_load.wait()
    wide = matmul(perm, x_ref[...])
    xp[...] = wide.astype(BF16)
    centred = wide - jnp.mean(wide, axis=-1, keepdims=True)
    spread = lax.rsqrt(jnp.mean(centred * centred, axis=-1, keepdims=True) + eps)
    normed[...] = (centred * spread * gain_ref[...].reshape(1, D)).astype(BF16)

    presence.lines()
    gather = Gather(wout_ref, slots, wg, asem)
    gather.pair()

    def project(j):
        loads[j].wait()
        cols = pl.ds(j * D, D)
        part = matmul(normed[...], wqkv[:, cols]).astype(BF16)
        if j > 0:
            kv[:, pl.ds((j - 1) * D, D)] = part
        projt[cols, :] = part.T

    project(0)
    gather.along_z()
    presence.half_plane()
    project(1)
    project(2)
    presence.plane()
    gather.q_along_y()
    gather.p_along_y()
    exchange_start(cslab, crecv, csend, crecvs)
    same = ids_k == ids_q

    def attend(g):
        for h in range(8):
            first, width, off = WINDOWS[h]
            lanes = pl.ds(pl.multiple_of(g * HALF + first, 128), width)
            rows = pl.multiple_of(g * HALF + h * 80, 16)
            keys = kv[:, lanes] * lanes_of(width, off)
            scores = matmul(keys, projt[lanes, :]) * score_scale
            scores = jnp.where(same, scores, -jnp.inf)
            scores = jnp.exp(scores - jnp.max(scores, axis=0, keepdims=True))
            share = scores * (1.0 / jnp.sum(scores, axis=0, keepdims=True))
            probs[g * 8 + h] = share
            part = matmul(projt[pl.ds(2 * D + rows, 80), :], share.astype(BF16))
            at[pl.ds(rows, 80), pl.ds(0, 256)] = part.astype(BF16)
            gap = jnp.zeros((8, 256), F32)
            padded = jnp.concatenate([part[0:40], gap, part[40:80], gap], axis=0).astype(BF16)
            atp[pl.ds(pl.multiple_of(g * 768 + h * 96, 16), 96), :] = padded

    attend(0)
    gather.q_along_x()
    attend(1)
    scatter = Scatter(
        at, bg, dw_ref, (pair, wsum, wb, xa, yb, sa, sb, wa2, wb2, ya, xb, zs, zr, s3), ssem, norm_scale
    )
    scatter.send_attended()

    across = xp[...].T.astype(F32)
    across = across - jnp.mean(across, axis=0, keepdims=True)
    inv = lax.rsqrt(jnp.mean(across * across, axis=0, keepdims=True) + eps)
    std[...] = across * inv
    column = jnp.broadcast_to(gain_ref[...].reshape(1, D), (128, D)).T
    gaincol[:, 0:128] = column
    gaincol[:, 128:256] = column
    apad[...] = atp[...].T
    gather.p_pair()
    exchange_wait(cslab, crecv, csend, crecvs)
    bg[...] = crecv[...].reshape(256, D)
    scatter.send_grad()
    bgt[...] = bg[...].T
    scatter.product()
    gather.q_pair()
    gather.finish()
    for half in range(2):
        cols = pl.ds(half * HALF, HALF)
        branch = matmul(apad[...], wg[half].reshape(1536, HALF))
        block = (xp[:, cols].astype(F32) + branch).astype(BF16)
        tok[:, :, cols] = block.reshape(SEQ, GROUP, HALF)
    exchange_start(tok, got, tsend, trecvs)

    for i in range(4):
        part = matmul_t(wg[0, i // 2, pl.ds(2 * (i % 2), 2)].reshape(384, HALF), bg[:, pl.ds(0, HALF)])
        part += matmul_t(wg[1, i // 2, pl.ds(2 * (i % 2), 2)].reshape(384, HALF), bg[:, pl.ds(HALF, HALF)])
        for h in range(4):
            own = part[96 * h : 96 * h + 96]
            own = jnp.concatenate([own[0:40], own[48:88]], axis=0).astype(BF16)
            dat[pl.ds(i * 320 + 80 * h, 80), :] = own

    def back(g):
        for h in range(8):
            first, width, off = WINDOWS[h]
            lanes = pl.ds(pl.multiple_of(g * HALF + first, 128), width)
            rows = pl.multiple_of(g * HALF + h * 80, 16)
            values = kv[:, pl.ds(pl.multiple_of(D + g * HALF + first, 128), width)] * lanes_of(width, off)
            share = probs[g * 8 + h]
            gp = matmul(values, dat[lanes, :])
            delta = jnp.sum(gp * share, axis=0, keepdims=True)
            gs = (share * (gp - delta) * score_scale).astype(BF16)
            low = share.astype(BF16)
            gt[pl.ds(rows, 80), :] = matmul(projt[pl.ds(D + rows, 80), :], gs).astype(BF16)
            gt[pl.ds(D + rows, 80), :] = matmul_t(projt[pl.ds(rows, 80), :], gs).astype(BF16)
            gt[pl.ds(2 * D + rows, 80), :] = matmul_t(dat[pl.ds(rows, 80), :], low).astype(BF16)

    back(0)
    back(1)
    scatter.after_one()

    def grads(i):
        rows = pl.ds(i * HALF, HALF)
        part = matmul(wqkv[rows, :], gt[...])
        both = part * std[rows, :]
        both = both[:, 0:128] + both[:, 128:256]
        ghold[2, :, rows] = jnp.sum(both.T, axis=0, keepdims=True)
        scaled = part * gaincol[rows, :]
        gn[rows, :] = scaled
        return jnp.sum(scaled, axis=0, keepdims=True), jnp.sum(scaled * std[rows, :], axis=0, keepdims=True)

    low = grads(0)
    high = grads(1)
    presence.everybody()
    gains = GainSum(ghold, g1, g2, gsem)
    gains.first(ghold[2])
    scatter.after_two()
    mean_g = (low[0] + high[0]) * (1.0 / D)
    mean_gs = (low[1] + high[1]) * (1.0 / D)
    branch = inv * (gn[...] - mean_g - std[...] * mean_gs)
    total = (bgt[...].astype(F32) + branch).astype(BF16)
    gx_ref[...] = matmul_t(permt[...], total).astype(BF16)
    gains.second()
    scatter.after_z()
    exchange_wait(tok, got, tsend, trecvs)
    dg_ref[...] = gains.finish() * norm_scale
    scatter.finish()


def finish_kernel(got_ref, gx_in, dw_ref, dg_ref, merged_ref, gx_ref, own_ref, gain_out):
    ordered = matmul(
        one_hot(256, 256, lambda r, c: r == lax.rem(c, 4) * 64 + lax.div(c, 4)), got_ref[...].reshape(256, D)
    ).astype(BF16)
    for c in range(4):
        merged_ref[:, pl.ds(c * D, D)] = ordered[64 * c : 64 * c + 64]
    gx_ref[...] = gx_in[...]
    for part in range(2):
        for core in range(2):
            own = dw_ref[part, core].astype(F32)
            own_ref[pl.ds(10 * part, 10), pl.ds(core * HALF, HALF)] = own[0:10]
    first = lax.axis_index("seq") * 20
    turned = pltpu.roll(jnp.broadcast_to(dg_ref[...], (8, D)), lax.rem(D - first, D), 1)
    gain_out[...] = turned[0, 0:20]


def per_device(patches, lengths, token_dest, gain, w_qkv, w_out, cotangent):
    norm_scale = 1.0 / math.sqrt(256 * SEQ * NX)
    vmem = pl.BlockSpec(memory_space=pltpu.VMEM)
    hbm = pl.BlockSpec(memory_space=pl.ANY)
    smem = pl.BlockSpec(memory_space=pltpu.SMEM)

    def kernel(*refs):
        kernel_body(norm_scale, refs)

    got, gx, dw, dg = pl.pallas_call(
        kernel,
        out_shape=(
            jax.ShapeDtypeStruct((SEQ, GROUP, D), BF16),
            jax.ShapeDtypeStruct((256, D), BF16),
            jax.ShapeDtypeStruct((2, 2, 16, HALF), BF16),
            jax.ShapeDtypeStruct((1, D), F32),
        ),
        in_specs=[hbm, vmem, smem, vmem, hbm, hbm, hbm],
        out_specs=(hbm, vmem, vmem, vmem),
        scratch_shapes=[
            pltpu.VMEM((256, D), BF16),
            pltpu.VMEM((20, D), BF16),
            pltpu.VMEM((SEQ, GROUP * D), BF16),
            pltpu.VMEM((D, 3 * D), BF16),
            pltpu.VMEM((2, 32, D), BF16),
            pltpu.VMEM((2, 2, 4, NY, 48, HALF), BF16),
            pltpu.VMEM((SEQ, GROUP, D), BF16),
            pltpu.VMEM((SEQ, GROUP, D), BF16),
            pltpu.VMEM((SEQ, GROUP, D), BF16),
            pltpu.VMEM((256, D), BF16),
            pltpu.VMEM((256, D), BF16),
            pltpu.VMEM((256, 2 * D), BF16),
            pltpu.VMEM((3 * D, 256), BF16),
            pltpu.VMEM((256, 256), BF16),
            pltpu.VMEM((HEADS, 256, 256), F32),
            pltpu.VMEM((D, 512), BF16),
            pltpu.VMEM((1536, 256), BF16),
            pltpu.VMEM((256, 1536), BF16),
            pltpu.VMEM((256, D), BF16),
            pltpu.VMEM((D, 256), BF16),
            pltpu.VMEM((D, 256), BF16),
            pltpu.VMEM((3 * D, 256), BF16),
            pltpu.VMEM((D, 256), F32),
            pltpu.VMEM((D, 256), F32),
            pltpu.VMEM((512, HALF), BF16),
            pltpu.VMEM((NX, NY, 80, HALF), F32),
            pltpu.VMEM((NX, NY, 80, HALF), BF16),
            pltpu.VMEM((3, NY, 80, X_FIRST), BF16),
            pltpu.VMEM((3, NX, 80, HALF - X_FIRST), BF16),
            pltpu.VMEM((NY, 80, X_FIRST), F32),
            pltpu.VMEM((NX, 80, HALF - X_FIRST), F32),
            pltpu.VMEM((NY, 80, X_FIRST), BF16),
            pltpu.VMEM((NX, 80, HALF - X_FIRST), BF16),
            pltpu.VMEM((3, 80, X_FIRST), BF16),
            pltpu.VMEM((3, 80, HALF - X_FIRST), BF16),
            pltpu.VMEM((128, HALF), BF16),
            pltpu.VMEM((7, 16, HALF), BF16),
            pltpu.VMEM((16, HALF), BF16),
            pltpu.VMEM((3, 1, D), F32),
            pltpu.VMEM((15, 1, D), F32),
            pltpu.VMEM((15, 1, D), F32),
            pltpu.VMEM((D, 256), F32),
            pltpu.SemaphoreType.DMA((6,)),
            pltpu.SemaphoreType.REGULAR((3,)),
            pltpu.SemaphoreType.DMA((80,)),
            pltpu.SemaphoreType.DMA,
            pltpu.SemaphoreType.DMA,
            pltpu.SemaphoreType.DMA,
            pltpu.SemaphoreType.DMA,
            pltpu.SemaphoreType.DMA((72,)),
            pltpu.SemaphoreType.DMA((60,)),
        ],
        compiler_params=pltpu.CompilerParams(
            collective_id=0, has_side_effects=True, vmem_limit_bytes=LIMIT
        ),
    )(
        patches[0], token_dest, lengths[0], gain, w_qkv, w_out, cotangent[0],
    )
    merged, gx, own_weight, own_gain = pl.pallas_call(
        finish_kernel,
        out_shape=(
            jax.ShapeDtypeStruct((SEQ, GROUP * D), BF16),
            jax.ShapeDtypeStruct((256, D), BF16),
            jax.ShapeDtypeStruct((20, D), F32),
            jax.ShapeDtypeStruct((20,), F32),
        ),
        in_specs=[vmem] * 4,
        out_specs=(vmem,) * 4,
        compiler_params=pltpu.CompilerParams(vmem_limit_bytes=LIMIT),
    )(got, gx, dw, dg)
    return (merged[None], gx[None], own_weight, own_gain)


def solution(mesh):
    placed = (
        P("dp", "seq", None),
        P("dp", "seq", None),
        P("dp", "seq"),
        P(),
        P(),
        P("seq", None),
        P("dp", "seq", None),
    )
    return jax.shard_map(
        per_device,
        mesh=mesh,
        in_specs=placed,
        out_specs=(P("dp", "seq", None), P("dp", "seq", None), P("seq", None), P("seq")),
        check_vma=False,
    )
```
